512 devices in a mesh: grp: 16 (over z_lo, x), feat: 32 (over y, z_hi, core).
Axes of the slice: x: 4, y: 4, z: 16 (z_hi: 4, z_lo: 4; z = z_hi * 4 + z_lo), core: 2. Of those that a mesh axis runs over, the one named last changes fastest.
Arguments:
- features: bfloat16 [16384, 768], P('grp', 'feat'), may hold values from -6 to 6
- adjacency: bfloat16 [128, 128, 256], P('grp'), may hold values from 0 to 0.119628906
- offsets: int32 [128], P('grp'), may hold values from 0 to 1024, as said below
- live: int32 [128], P('grp'), may hold values 0 or 1
- w_self: bfloat16 [768, 1024], P('feat'), may hold values from -0.21875 to 0.21875
- w_neigh: bfloat16 [768, 1024], P('feat'), may hold values from -0.21875 to 0.21875
- bias: float32 [1024], replicated, may hold values from -3 to 3
- targets: bfloat16 [1024, 16384], P('feat', 'grp'), may hold values from -6 to 6
Outputs:
- hidden: bfloat16 [1024, 16384], P('feat', 'grp')
- grad_self: float32 [768, 1024], P('feat')
- grad_neigh: float32 [768, 1024], P('feat')
- grad_bias: float32 [1024], replicated
The draws below stay inside these ranges and needn't reach their ends.
Inputs may be any that keep to these rules, and one draw needn't show every extreme that they name: `offsets`: tile k of a range (counted from 0) starts between k * 128 and k * 128 + 128; the first tile of range 0 starts at 0 and the last tile of the last range at 1024.
All inputs are finite; a program needn't handle non-finite values. No bound on the sum of `live` on one device may be relied on, other than what follows from the above.
Results may differ from the reference program's by a relative error of at most 0.0039.
Values may be sent and summed in bfloat16 or wider, within the bound.
A program may use at most 64 MiB of HBM per device.

```python
import math
import jax
import jax.numpy as jnp
from jax import lax

D = 768
HID = 1024
ROWS_GRP = 1024
TILE = 128
BAND = 256
HALO = 128
NODES = 16384
TILES = 128


def draw_offsets(key, part):
    key = jax.random.fold_in(key, 5)
    tiles_group = ROWS_GRP // TILE
    index = jnp.arange(TILES, dtype=jnp.int32)
    position = index % tiles_group
    jitter = jax.random.randint(key, (TILES,), 0, TILE + 1, dtype=jnp.int32)
    jitter = jnp.where(index == 0, 0, jnp.where(index == TILES - 1, TILE, jitter))
    return (position * TILE + jitter).astype(jnp.int32)


def set_ends(entries, stream_key, least, high):
    shape = entries.shape
    place = [jax.random.randint(jax.random.fold_in(stream_key, axis), (), 0, shape[axis]) for axis in range(len(shape))]
    entries = entries.at[tuple(place)].set(least)
    longest = shape.index(max(shape))
    place[longest] = (place[longest] + 1) % shape[longest]
    return entries.at[tuple(place)].set(high)


def levels(key, extent, shards, least, top_value):
    loudness = 1.0
    for dim, shards_of in shards:
        heights = jax.random.uniform(jax.random.fold_in(jax.random.fold_in(key, 6), dim), (shards_of,), jnp.float32, least / len(shards), top_value / len(shards))
        loudness = loudness * jnp.repeat(jnp.exp(heights), extent[dim] // shards_of).reshape((-1,) + (1,) * (len(extent) - 1 - dim))
    return loudness


def bell_draw(key, extent, spread, bound, cuts=(), held_as=jnp.bfloat16):
    values = jax.random.normal(key, extent, jnp.float32) * spread
    if len(cuts) > 0:
        values = levels(key, extent, cuts, -0.22, 0.18) * values
    return jnp.clip(values, min=-bound, max=bound).astype(held_as)


def setup_inputs(seed: int = 0) -> dict:
    key_of = jax.random.split(jax.random.key(seed), 9)
    return {
        "features": bell_draw(key_of[0], (NODES, D), 1.0, 6.0, ((0, 16), (1, 32))),
        "adjacency": jnp.clip(0.119628906 * jax.random.uniform(key_of[1], (TILES, TILE, BAND), jnp.float32) ** levels(key_of[1], (TILES, TILE, BAND), ((0, 16),), -0.2, 0.2), 0.0, 0.119628906).astype(jnp.bfloat16),
        "offsets": draw_offsets(jax.random.fold_in(key_of[8], 71), 0),
        "live": set_ends((jax.random.randint(key_of[3], (TILES,), 0, 8) < 7).astype(jnp.int32), jax.random.fold_in(key_of[3], 1), 0, 1),
        "w_self": bell_draw(key_of[4], (D, HID), D ** -0.5, 0.21875, ((0, 32),)),
        "w_neigh": bell_draw(key_of[5], (D, HID), D ** -0.5, 0.21875, ((0, 32),)),
        "bias": bell_draw(key_of[6], (HID,), 0.5, 3.0, (), jnp.float32),
        "targets": bell_draw(key_of[7], (HID, NODES), 1.0, 6.0, ((0, 32), (1, 16))),
    }


def slope(values):
    logistic = jax.nn.sigmoid(values)
    return logistic * (1.0 + values * (1.0 - logistic))

def reference(features, adjacency, offsets, live, w_self, w_neigh, bias, targets):
    padded = jnp.pad(features, ((HALO, HALO), (0, 0)))
    tiles_group = ROWS_GRP // TILE

    def one_tile(index):
        group = index // tiles_group
        start = (group * ROWS_GRP + offsets[index]).astype(jnp.int32)
        window = lax.dynamic_slice_in_dim(padded, start, BAND, 0)
        summed = jnp.dot(adjacency[index], window, preferred_element_type=jnp.float32)
        return (summed * live[index].astype(jnp.float32)).astype(jnp.bfloat16)
    neighbour = lax.map(one_tile, jnp.arange(TILES, dtype=jnp.int32)).reshape(NODES, D)
    pre = jnp.dot(features, w_self, preferred_element_type=jnp.float32)
    pre = pre + jnp.dot(neighbour, w_neigh, preferred_element_type=jnp.float32) + bias
    act = jax.nn.silu(pre)
    hidden = act.T.astype(jnp.bfloat16)
    delta = (act - targets.T.astype(jnp.float32)) * slope(pre) / math.sqrt(NODES)
    grad_self = jnp.dot(features.T.astype(jnp.float32), delta, precision=lax.Precision.HIGHEST)
    grad_neigh = jnp.dot(neighbour.T.astype(jnp.float32), delta, precision=lax.Precision.HIGHEST)
    grad_bias = lax.optimization_barrier(jnp.sum(delta, axis=0))
    return (hidden, grad_self, grad_neigh, grad_bias)
```

```python
import jax
import jax.numpy as jnp
from jax import lax
from jax.experimental import pallas as pl
from jax.experimental.pallas import tpu as pltpu
from jax.sharding import PartitionSpec as P

F32 = jnp.float32
BF16 = jnp.bfloat16
MESH = pl.DeviceIdType.MESH

COLS = 24
PAIR = 48
COLUMN = 4 * PAIR
HALF = 640
PART_A = 384
PART_B = HALF - PART_A
TILE = 128
SENDS = 96
RECVS = 64


def mod4(value):
    return lax.rem(value + 4, 4)


def kernel(
    feat_h, adj_h, off_h, live_h, ws_h, wn_h, bias_h, tgt_h,
    out,
    feat, adj, off, live, ws, wn, bias, tgt,
    wide, stage, xg, nb, band, wsend, wg, wt, pre_acc, rsend, ra, rbs, rb, fg, fin,
    in_sem, send_sem, recv_sem,
):
    loads = [
        pltpu.make_async_copy(src, dst, in_sem.at[i])
        for i, (src, dst) in enumerate(
            [(feat_h, feat), (ws_h, ws), (wn_h, wn), (adj_h, adj), (off_h, off), (live_h, live),
             (bias_h, bias), (tgt_h, tgt)]
        )
    ]
    for load in loads:
        load.start()

    g = lax.axis_index("grp")
    f = lax.axis_index("feat")
    c = lax.rem(f, 2)
    p = lax.div(f, 2)
    y = lax.div(p, 4)
    zh = lax.rem(p, 4)
    x = lax.rem(g, 4)
    zl = lax.div(g, 4)
    other = 1 - c
    sign = 1 - 2 * c

    def device(group, chip, core):
        return (group, chip * 2 + core)

    partner = device(g, p, other)
    y_fwd = device(g, mod4(y + sign) * 4 + zh, c)
    y_bwd = device(g, mod4(y - sign) * 4 + zh, c)
    y_far = device(g, mod4(y + 2) * 4 + zh, c)
    z_fwd = device(g, y * 4 + mod4(zh + sign), c)
    z_bwd = device(g, y * 4 + mod4(zh - sign), c)
    stays = jnp.logical_and(zh == zl, jnp.logical_and(x == 0, y == 0))

    barrier = pltpu.get_barrier_semaphore()

    def tell(target):
        pl.semaphore_signal(barrier, inc=1, device_id=target, device_id_type=MESH)

    @pl.when(jnp.logical_and(c == 0, g > 0))
    def _():
        tell(device(g - 1, p, 0))
        tell(device(g - 1, p, 1))

    @pl.when(jnp.logical_and(c == 1, g < 15))
    def _():
        tell(device(g + 1, p, 0))
        tell(device(g + 1, p, 1))

    for target in (z_fwd, z_bwd, y_fwd, y_bwd, y_far, partner):
        tell(target)

    w_src_y = mod4(y + x)
    w_dst_y = mod4(y - x)
    r_chip = mod4(x - y) * 4 + zl
    for step in range(1, 4):
        tell(device(g, w_src_y * 4 + mod4(zh + step), c))
        tell(device(mod4(zl + step) * 4 + y, r_chip, c))

    @pl.when(x != 0)
    def _():
        tell(device(g, w_src_y * 4 + zh, c))

    @pl.when(jnp.logical_not(stays))
    def _():
        tell(device(zl * 4 + y, r_chip, c))

    def tell_far(step, carry):
        tell(device(lax.rem(g + step, 16), p, c))
        return carry

    lax.fori_loop(1, 16, tell_far, 0)

    loads[0].wait()
    wide[...] = feat[...].astype(F32)

    @pl.when(c == 0)
    def _():
        stage[0:COLS, TILE:HALF] = wide[:, 0:512]

        @pl.when(g == 0)
        def _():
            stage[:, 0:TILE] = jnp.zeros((PAIR, TILE), F32)

    @pl.when(c == 1)
    def _():
        stage[COLS:PAIR, 0:512] = wide[:, 512:1024]

        @pl.when(g == 15)
        def _():
            stage[:, 512:HALF] = jnp.zeros((PAIR, TILE), F32)

    waits = (
        6 + 3 + 3 + 15
        + (x != 0).astype(jnp.int32)
        + jnp.logical_not(stays).astype(jnp.int32)
        + (g < 15).astype(jnp.int32)
        + (g > 0).astype(jnp.int32)
    )
    pl.semaphore_wait(barrier, waits)

    used = [0, 0]
    sent = []

    def slot(which, count=1):
        used[which] += count
        return used[which] - count

    def remote(src, dst, target, send, recv):
        return pltpu.make_async_remote_copy(
            src_ref=src, dst_ref=dst, send_sem=send_sem.at[send], recv_sem=recv_sem.at[recv],
            device_id=target, device_id_type=MESH,
        )

    def copy(src, dst, target, recv):
        made = remote(src, dst, target, slot(0), recv)
        made.start()
        sent.append(made)

    def await_bytes(ref, recv):
        pltpu.make_async_copy(ref, ref, recv_sem.at[recv]).wait()

    own_rows = pl.ds(pl.multiple_of(c * COLS, 8), COLS)
    other_rows = pl.ds(pl.multiple_of(other * COLS, 8), COLS)
    r_left, r_right, r_swap = slot(1, 2), slot(1, 2), slot(1)
    halo_up = remote(
        wide.at[:, 896:1024], stage.at[own_rows, 0:TILE], device(g + 1, p, 0), slot(0), r_left + c
    )
    halo_down = remote(
        wide.at[:, 0:TILE], stage.at[own_rows, 512:HALF], device(g - 1, p, 1), slot(0), r_right + c
    )

    @pl.when(g < 15)
    def _():
        halo_up.start()

    @pl.when(g > 0)
    def _():
        halo_down.start()

    copy(
        wide.at[:, pl.ds(pl.multiple_of(other * 512, 128), 512)],
        stage.at[own_rows, pl.ds(pl.multiple_of(c * TILE, 128), 512)],
        partner, r_swap,
    )

    loads[1].wait()
    loads[2].wait()
    lane = lax.broadcasted_iota(jnp.int32, (COLS, 128), 1)
    pad = jnp.zeros((32 - COLS, 128), F32)
    for pair in range(8):
        s_tile = ws[:, pair * 128:(pair + 1) * 128].astype(F32)
        n_tile = wn[:, pair * 128:(pair + 1) * 128].astype(F32)
        low = jnp.where(lane < 64, s_tile, pltpu.roll(n_tile, 64, 1))
        high = jnp.where(lane < 64, pltpu.roll(s_tile, 64, 1), n_tile)
        wsend[2 * pair] = jnp.concatenate([low, pad], 0).astype(BF16)
        wsend[2 * pair + 1] = jnp.concatenate([high, pad], 0).astype(BF16)

    r_w1 = slot(1, 4)
    for step in range(1, 4):
        chip = w_dst_y * 4 + mod4(zh + step)
        copy(wsend.at[chip], wg.at[c, p], device(g, chip, c), r_w1 + step)
    chip0 = w_dst_y * 4 + zh
    w_zero = remote(wsend.at[chip0], wg.at[c, p], device(g, chip0, c), slot(0), r_w1)

    @pl.when(x != 0)
    def _():
        w_zero.start()

    @pl.when(x == 0)
    def _():
        wg[c, p] = wsend[chip0]

    for load in loads[3:6]:
        load.wait()
    for tile in range(8):
        dense = adj[tile].astype(F32)
        padded = jnp.concatenate([dense, jnp.zeros((TILE, TILE), F32)], 1)
        moved = pltpu.roll(padded, off[tile] - tile * TILE, 1)
        band[tile] = (moved * live[tile].astype(F32)).astype(BF16)

    await_bytes(stage.at[other_rows, pl.ds(pl.multiple_of(other * TILE, 128), 512)], r_swap)

    @pl.when(jnp.logical_and(c == 0, g > 0))
    def _():
        await_bytes(stage.at[0:COLS, 0:TILE], r_left)
        await_bytes(stage.at[COLS:PAIR, 0:TILE], r_left + 1)

    @pl.when(jnp.logical_and(c == 1, g < 15))
    def _():
        await_bytes(stage.at[0:COLS, 512:HALF], r_right)
        await_bytes(stage.at[COLS:PAIR, 512:HALF], r_right + 1)

    def block(by, bz, part):
        rows = pl.ds(pl.multiple_of((mod4(bz) * 4 + mod4(by)) * PAIR, 16), PAIR)
        start = {"all": 0, "a": 0, "b": PART_A}[part]
        width = {"all": HALF, "a": PART_A, "b": PART_B}[part]
        return xg.at[rows, pl.ds(pl.multiple_of(c * HALF + start, 128), width)]

    block(y, zh, "all")[...] = stage[...].astype(BF16)

    r_pair = slot(1, 4)

    def forward(by, bz, part, target, recv):
        view = block(by, bz, part)
        copy(view, view, target, recv)

    def share(by, bz, part):
        forward(by, bz, part, partner, r_pair + mod4(bz))

    r_z1 = slot(1, 4)
    r_z2 = slot(1, 2)
    r_y1 = slot(1, 6)
    r_y2 = slot(1, 6)
    r_y3 = slot(1, 6)

    def column(number):
        return zh + sign * (0, -1, 1)[number]

    def send_y1(number):
        forward(y, column(number), "all", y_fwd, r_y1 + 2 * number)
        forward(y, column(number), "all", y_bwd, r_y1 + 2 * number + 1)

    def take_y1(number):
        bz = column(number)
        await_bytes(block(y - sign, bz, "all"), r_y1 + 2 * number)
        forward(y - sign, bz, "a", y_fwd, r_y2 + 2 * number)
        await_bytes(block(y + sign, bz, "all"), r_y1 + 2 * number + 1)
        forward(y + sign, bz, "b", y_bwd, r_y2 + 2 * number + 1)
        share(y - sign, bz, "all")
        share(y + sign, bz, "all")

    def take_y2(number):
        bz = column(number)
        await_bytes(block(y + 2, bz, "a"), r_y2 + 2 * number)
        share(y + 2, bz, "a")
        await_bytes(block(y + 2, bz, "b"), r_y2 + 2 * number + 1)
        share(y + 2, bz, "b")

    def send_y3(part):
        first = r_y3 + (0 if part == "a" else 3)
        forward(y, zh + 2, part, y_fwd, first)
        forward(y, zh + 2, part, y_bwd, first + 1)
        forward(y, zh + 2, part, y_far, first + 2)
        share(y, zh + 2, part)

    def take_y3(part):
        first = r_y3 + (0 if part == "a" else 3)
        for offset, by in enumerate((y - sign, y + sign, y + 2)):
            await_bytes(block(by, zh + 2, part), first + offset)
            share(by, zh + 2, part)

    forward(y, zh, "a", z_fwd, r_z1)
    forward(y, zh, "b", z_bwd, r_z1 + 1)
    forward(y, zh, "b", z_fwd, r_z1 + 2)
    forward(y, zh, "a", z_bwd, r_z1 + 3)
    send_y1(0)
    share(y, zh, "all")

    for step in range(1, 4):
        await_bytes(wg.at[c, w_src_y * 4 + mod4(zh + step)], r_w1 + 4 - step)

    @pl.when(x != 0)
    def _():
        await_bytes(wg.at[c, w_src_y * 4 + zh], r_w1)

    r_w2 = slot(1, 4)
    part_w = wg.at[c, pl.ds(w_src_y * 4, 4)]
    for step in range(1, 4):
        copy(part_w, part_w, device(g - x + mod4(x + step), p, c), r_w2 + step)

    take_y1(0)

    for step in range(1, 4):
        await_bytes(wg.at[c, pl.ds(mod4(y + x - step) * 4, 4)], r_w2 + step)
    r_w3 = slot(1)
    copy(wg.at[c], wg.at[c], partner, r_w3)
    take_y2(0)

    await_bytes(block(y, zh - sign, "a"), r_z1)
    forward(y, zh - sign, "a", z_fwd, r_z2)
    await_bytes(block(y, zh + sign, "b"), r_z1 + 1)
    forward(y, zh + sign, "b", z_bwd, r_z2 + 1)

    await_bytes(wg.at[other], r_w3)
    for col in range(4):
        rows = []
        for row in range(4):
            for core in range(2):
                rows.append(wg[core, row * 4 + col].astype(F32)[0:COLS])
        wt[col] = jnp.concatenate(rows, 0).T.astype(BF16)

    await_bytes(block(y, zh - sign, "b"), r_z1 + 2)
    send_y1(1)
    await_bytes(block(y, zh + sign, "a"), r_z1 + 3)
    send_y1(2)
    share(y, zh - sign, "all")
    share(y, zh + sign, "all")

    loads[6].wait()
    spot = lax.broadcasted_iota(jnp.int32, (32, 1024), 1)
    row = lax.broadcasted_iota(jnp.int32, (32, 1024), 0)
    bias_own = jnp.sum(
        jnp.where(spot == row + f * 32, jnp.broadcast_to(bias[...], (32, 1024)), 0.0),
        axis=1, keepdims=True,
    )
    pre_acc[...] = jnp.broadcast_to(bias_own, (32, 1024))

    def compute(bz):
        col = mod4(bz)
        rows = pl.ds(pl.multiple_of(col * COLUMN, 16), COLUMN)
        await_bytes(xg.at[rows, pl.ds(pl.multiple_of(other * HALF, 128), HALF)], r_pair + col)
        for tile in range(8):
            nb[rows, tile * TILE:(tile + 1) * TILE] = lax.dot_general(
                xg[rows, tile * TILE:tile * TILE + 3 * TILE], band[tile],
                (((1,), (1,)), ((), ())), preferred_element_type=F32,
            ).astype(BF16)
        ws_t = wt[col, pl.ds(pl.multiple_of(c * 32, 16), 32), :]
        wn_t = wt[col, pl.ds(pl.multiple_of(64 + c * 32, 16), 32), :]
        pre_acc[...] += (
            jnp.dot(ws_t, xg[rows, TILE:TILE + 1024], preferred_element_type=F32)
            + jnp.dot(wn_t, nb[rows, :], preferred_element_type=F32)
        )

    compute(zh)
    take_y1(1)
    take_y1(2)
    await_bytes(block(y, zh + 2, "a"), r_z2)
    send_y3("a")
    await_bytes(block(y, zh + 2, "b"), r_z2 + 1)
    send_y3("b")
    take_y2(1)
    take_y2(2)
    compute(zh - 1)
    take_y3("a")
    take_y3("b")
    compute(zh + 1)
    compute(zh + 2)

    loads[7].wait()
    pre = pre_acc[...]
    gate = jax.nn.sigmoid(pre)
    act = pre * gate
    out[0:32] = act
    delta = (act - tgt[...].astype(F32)) * (gate * (1.0 + pre * (1.0 - gate))) * (1.0 / 128.0)

    head = delta.astype(BF16)
    rest = (delta - head.astype(F32)).astype(BF16)
    both = jnp.concatenate([head] * 4 + [rest] * 4, 0)
    turn = (((1,), (1,)), ((), ()))
    gs = lax.dot_general(xg[:, TILE:TILE + 1024], both, turn, preferred_element_type=F32)
    gn = lax.dot_general(nb[...], both, turn, preferred_element_type=F32)
    gs = gs[:, 0:128] + gs[:, 128:256]
    gn = gn[:, 0:128] + gn[:, 128:256]
    lanes = lax.broadcasted_iota(jnp.int32, (32, 128), 1)
    bias_term = jnp.sum(delta, axis=1, keepdims=True)
    quarter = lax.div(lax.broadcasted_iota(jnp.int32, (PAIR, 128), 1), 32)
    blank = jnp.zeros((32, 128), F32)

    def packed(grad, row):
        parts = [grad[(col * 4 + row) * PAIR:(col * 4 + row + 1) * PAIR] for col in range(4)]
        low = jnp.where(quarter == 0, parts[0], parts[1])
        high = jnp.where(quarter == 2, parts[2], parts[3])
        return jnp.where(quarter < 2, low, high)

    for row in range(4):
        turned = jnp.concatenate([packed(gs, row), packed(gn, row), blank], 0).T
        for col in range(4):
            rsend[row, col] = jnp.where(lanes == 96, bias_term, turned[col * 32:(col + 1) * 32])

    r_ra = slot(1, 4)
    for step in range(1, 4):
        to_x = mod4(x + step)
        copy(rsend.at[to_x], ra.at[step], device(g - x + to_x, p, c), r_ra + step)

    def with_bias(tile, total):
        first = total.astype(BF16).astype(F32)
        tile = jnp.where(lanes == 96, first, tile)
        return jnp.where(lanes == 97, total - first, tile).astype(BF16)

    for step in range(1, 4):
        await_bytes(ra.at[step], r_ra + step)
    for col in range(4):
        summed = (rsend[x, col] + ra[1, col]) + (ra[2, col] + ra[3, col])
        rbs[col] = with_bias(summed, summed[:, 96:97])

    r_rb = slot(1)
    to_group = zh * 4 + mod4(y + x)
    for step in range(1, 4):
        col = mod4(zh + step)
        copy(rbs.at[col], rb.at[zl], device(to_group, x * 4 + col, c), r_rb)
    r_zero = remote(rbs.at[zh], rb.at[zl], device(to_group, x * 4 + zh, c), slot(0), r_rb)

    @pl.when(jnp.logical_not(stays))
    def _():
        r_zero.start()

    @pl.when(stays)
    def _():
        pltpu.make_async_copy(rbs.at[zh], rb.at[zl], recv_sem.at[r_rb]).start()

    await_bytes(rb, r_rb)
    total = (rb[0].astype(F32) + rb[1].astype(F32)) + (rb[2].astype(F32) + rb[3].astype(F32))
    fg[r_chip, c] = with_bias(total, total[:, 96:97] + total[:, 97:98])

    r_r2 = slot(1)
    mine = fg.at[r_chip, c]
    for step in range(1, 16):
        copy(mine, mine, device(lax.rem(g + step, 16), p, c), r_r2)
    await_bytes(fg.at[pl.ds(0, 15), c], r_r2)
    r_r3 = slot(1)
    copy(fg.at[:, c], fg.at[:, c], partner, r_r3)
    await_bytes(fg.at[:, other], r_r3)
    for part in range(8):
        rows = [fg[2 * part + j, core].astype(F32) for j in range(2) for core in range(2)]
        fin[:, part * 128:(part + 1) * 128] = jnp.concatenate(rows, 0).T
    out[32:56] = fin[pl.ds(pl.multiple_of(c * COLS, 8), COLS), :]
    out[56:80] = fin[pl.ds(pl.multiple_of(PAIR + c * COLS, 8), COLS), :]
    out[80:81] = fin[96:97, :] + fin[97:98, :]

    for made in sent:
        made.wait_send()

    @pl.when(g < 15)
    def _():
        halo_up.wait_send()

    @pl.when(g > 0)
    def _():
        halo_down.wait_send()

    @pl.when(x != 0)
    def _():
        w_zero.wait_send()

    @pl.when(jnp.logical_not(stays))
    def _():
        r_zero.wait_send()

    assert used[0] <= SENDS and used[1] <= RECVS, used


def shards(features, adjacency, offsets, live, w_self, w_neigh, bias, targets):
    vmem = pl.BlockSpec(memory_space=pltpu.VMEM)
    hbm = pl.BlockSpec(memory_space=pltpu.HBM)
    joined = pl.pallas_call(
        kernel,
        out_shape=jax.ShapeDtypeStruct((88, 1024), F32),
        in_specs=[hbm] * 8,
        out_specs=vmem,
        scratch_shapes=[
            pltpu.VMEM((COLS, 1024), BF16),
            pltpu.VMEM((8, TILE, 256), BF16),
            pltpu.SMEM((8,), jnp.int32),
            pltpu.SMEM((8,), jnp.int32),
            pltpu.VMEM((COLS, 1024), BF16),
            pltpu.VMEM((COLS, 1024), BF16),
            pltpu.VMEM((1, 1024), F32),
            pltpu.VMEM((32, 1024), BF16),
            pltpu.VMEM((COLS, 1024), F32),
            pltpu.VMEM((PAIR, HALF), F32),
            pltpu.VMEM((768, 1280), BF16),
            pltpu.VMEM((768, 1024), BF16),
            pltpu.VMEM((8, TILE, 384), BF16),
            pltpu.VMEM((16, 32, 128), BF16),
            pltpu.VMEM((2, 16, 32, 128), BF16),
            pltpu.VMEM((4, 128, COLUMN), BF16),
            pltpu.VMEM((32, 1024), F32),
            pltpu.VMEM((4, 4, 32, 128), F32),
            pltpu.VMEM((4, 4, 32, 128), F32),
            pltpu.VMEM((4, 32, 128), BF16),
            pltpu.VMEM((4, 32, 128), BF16),
            pltpu.VMEM((16, 2, 32, 128), BF16),
            pltpu.VMEM((128, 1024), F32),
            pltpu.SemaphoreType.DMA((8,)),
            pltpu.SemaphoreType.DMA((SENDS,)),
            pltpu.SemaphoreType.DMA((RECVS,)),
        ],
        compiler_params=pltpu.CompilerParams(
            collective_id=0, has_side_effects=True, vmem_limit_bytes=63 * 1024 * 1024
        ),
        cost_estimate=pl.CostEstimate(flops=10**9, bytes_accessed=10**7, transcendentals=32768),
    )(
        features.T, adjacency, offsets, live, w_self, w_neigh, bias.reshape(1, 1024), targets
    )
    return joined[0:32].astype(BF16), joined[32:56], joined[56:80], joined[80]


def solution(mesh):
    in_specs = (
        P("grp", "feat"),
        P("grp", None, None),
        P("grp"),
        P("grp"),
        P("feat", None),
        P("feat", None),
        P(),
        P("feat", "grp"),
    )
    out_specs = (P("feat", "grp"), P("feat", None), P("feat", None), P())
    return jax.shard_map(shards, mesh=mesh, in_specs=in_specs, out_specs=out_specs, check_vma=False)
```

```python
import jax
import jax.numpy as jnp
from jax import lax
from jax.experimental import pallas as pl
from jax.experimental.pallas import tpu as pltpu
from jax.sharding import PartitionSpec as P

F32 = jnp.float32
BF16 = jnp.bfloat16
MESH = pl.DeviceIdType.MESH

COLS = 24
PAIR = 48
COLUMN = 4 * PAIR
HALF = 640
PART_A = 384
PART_B = HALF - PART_A
TILE = 128
SENDS = 96
RECVS = 64


def mod4(value):
    return lax.rem(value + 4, 4)


def kernel(
    feat_h, adj_h, off_h, live_h, ws_h, wn_h, bias_h, tgt_h,
    hid, gs_o, gn_o, gb_o,
    feat, adj, off, live, ws, wn, bias, tgt,
    wide, stage, xg, nb, band, wsend, wg, wt, pre_acc, rsend, ra, rbs, rb, fg,
    in_sem, send_sem, recv_sem,
):
    loads = [
        pltpu.make_async_copy(src, dst, in_sem.at[i])
        for i, (src, dst) in enumerate(
            [(feat_h, feat), (ws_h, ws), (wn_h, wn), (adj_h, adj), (off_h, off), (live_h, live),
             (bias_h, bias), (tgt_h, tgt)]
        )
    ]
    for load in loads:
        load.start()

    g = lax.axis_index("grp")
    f = lax.axis_index("feat")
    c = lax.rem(f, 2)
    p = lax.div(f, 2)
    y = lax.div(p, 4)
    zh = lax.rem(p, 4)
    x = lax.rem(g, 4)
    zl = lax.div(g, 4)
    other = 1 - c
    sign = 1 - 2 * c

    def device(group, chip, core):
        return (group, chip * 2 + core)

    partner = device(g, p, other)
    y_fwd = device(g, mod4(y + sign) * 4 + zh, c)
    y_bwd = device(g, mod4(y - sign) * 4 + zh, c)
    y_far = device(g, mod4(y + 2) * 4 + zh, c)
    z_fwd = device(g, y * 4 + mod4(zh + sign), c)
    z_bwd = device(g, y * 4 + mod4(zh - sign), c)
    stays = jnp.logical_and(zh == zl, jnp.logical_and(x == 0, y == 0))

    barrier = pltpu.get_barrier_semaphore()

    def tell(target):
        pl.semaphore_signal(barrier, inc=1, device_id=target, device_id_type=MESH)

    @pl.when(jnp.logical_and(c == 0, g > 0))
    def _():
        tell(device(g - 1, p, 0))
        tell(device(g - 1, p, 1))

    @pl.when(jnp.logical_and(c == 1, g < 15))
    def _():
        tell(device(g + 1, p, 0))
        tell(device(g + 1, p, 1))

    for target in (z_fwd, z_bwd, y_fwd, y_bwd, y_far, partner):
        tell(target)

    w_src_y = mod4(y + x)
    w_dst_y = mod4(y - x)
    r_chip = mod4(x - y) * 4 + zl
    for step in range(1, 4):
        tell(device(g, w_src_y * 4 + mod4(zh + step), c))
        tell(device(mod4(zl + step) * 4 + y, r_chip, 0))
        tell(device(mod4(zl + step) * 4 + y, r_chip, 1))

    @pl.when(x != 0)
    def _():
        tell(device(g, w_src_y * 4 + zh, c))

    tell(device(zl * 4 + y, r_chip, other))

    @pl.when(jnp.logical_not(stays))
    def _():
        tell(device(zl * 4 + y, r_chip, c))

    def tell_far(step, carry):
        tell(device(lax.rem(g + step, 16), p, c))
        return carry

    lax.fori_loop(1, 16, tell_far, 0)

    loads[0].wait()
    wide[...] = feat[...].astype(F32)

    @pl.when(c == 0)
    def _():
        stage[0:COLS, TILE:HALF] = wide[:, 0:512]

        @pl.when(g == 0)
        def _():
            stage[:, 0:TILE] = jnp.zeros((PAIR, TILE), F32)

    @pl.when(c == 1)
    def _():
        stage[COLS:PAIR, 0:512] = wide[:, 512:1024]

        @pl.when(g == 15)
        def _():
            stage[:, 512:HALF] = jnp.zeros((PAIR, TILE), F32)

    waits = (
        6 + 3 + 7 + 15
        + (x != 0).astype(jnp.int32)
        + jnp.logical_not(stays).astype(jnp.int32)
        + (g < 15).astype(jnp.int32)
        + (g > 0).astype(jnp.int32)
    )
    pl.semaphore_wait(barrier, waits)

    used = [0, 0]
    sent = []

    def slot(which, count=1):
        used[which] += count
        return used[which] - count

    def remote(src, dst, target, send, recv):
        return pltpu.make_async_remote_copy(
            src_ref=src, dst_ref=dst, send_sem=send_sem.at[send], recv_sem=recv_sem.at[recv],
            device_id=target, device_id_type=MESH,
        )

    def copy(src, dst, target, recv):
        made = remote(src, dst, target, slot(0), recv)
        made.start()
        sent.append(made)

    def start_unless(skip, made):
        @pl.when(jnp.logical_not(skip))
        def _():
            made.start()

    def await_bytes(ref, recv):
        pltpu.make_async_copy(ref, ref, recv_sem.at[recv]).wait()

    own_rows = pl.ds(pl.multiple_of(c * COLS, 8), COLS)
    other_rows = pl.ds(pl.multiple_of(other * COLS, 8), COLS)
    r_left, r_right, r_swap = slot(1, 2), slot(1, 2), slot(1)
    halo_up = remote(
        wide.at[:, 896:1024], stage.at[own_rows, 0:TILE], device(g + 1, p, 0), slot(0), r_left + c
    )
    halo_down = remote(
        wide.at[:, 0:TILE], stage.at[own_rows, 512:HALF], device(g - 1, p, 1), slot(0), r_right + c
    )

    @pl.when(g < 15)
    def _():
        halo_up.start()

    @pl.when(g > 0)
    def _():
        halo_down.start()

    copy(
        wide.at[:, pl.ds(pl.multiple_of(other * 512, 128), 512)],
        stage.at[own_rows, pl.ds(pl.multiple_of(c * TILE, 128), 512)],
        partner, r_swap,
    )

    loads[1].wait()
    loads[2].wait()
    lane = lax.broadcasted_iota(jnp.int32, (COLS, 128), 1)
    pad = jnp.zeros((32 - COLS, 128), F32)
    for pair in range(8):
        s_tile = ws[:, pair * 128:(pair + 1) * 128].astype(F32)
        n_tile = wn[:, pair * 128:(pair + 1) * 128].astype(F32)
        low = jnp.where(lane < 64, s_tile, pltpu.roll(n_tile, 64, 1))
        high = jnp.where(lane < 64, pltpu.roll(s_tile, 64, 1), n_tile)
        wsend[2 * pair] = jnp.concatenate([low, pad], 0).astype(BF16)
        wsend[2 * pair + 1] = jnp.concatenate([high, pad], 0).astype(BF16)

    r_w1 = slot(1, 4)
    for step in range(1, 4):
        chip = w_dst_y * 4 + mod4(zh + step)
        copy(wsend.at[chip], wg.at[c, p], device(g, chip, c), r_w1 + step)
    chip0 = w_dst_y * 4 + zh
    w_zero = remote(wsend.at[chip0], wg.at[c, p], device(g, chip0, c), slot(0), r_w1)

    @pl.when(x != 0)
    def _():
        w_zero.start()

    @pl.when(x == 0)
    def _():
        wg[c, p] = wsend[chip0]

    def block(by, bz, part):
        rows = pl.ds(pl.multiple_of((mod4(bz) * 4 + mod4(by)) * PAIR, 16), PAIR)
        start = {"all": 0, "a": other * PART_B, "b": c * PART_A}[part]
        width = {"all": HALF, "a": PART_A, "b": PART_B}[part]
        return xg.at[rows, pl.ds(pl.multiple_of(c * HALF + start, 128), width)]

    r_pair = slot(1, 4)

    def forward(by, bz, part, target, recv):
        view = block(by, bz, part)
        copy(view, view, target, recv)

    def share(by, bz, part):
        forward(by, bz, part, partner, r_pair + mod4(bz))

    r_z1 = slot(1, 4)
    r_z2 = slot(1, 2)
    r_y1 = slot(1, 6)
    r_y2 = slot(1, 6)
    r_y3 = slot(1, 6)

    await_bytes(stage.at[other_rows, pl.ds(pl.multiple_of(other * TILE, 128), 512)], r_swap)
    block(y, zh, "a")[...] = stage[:, pl.ds(pl.multiple_of(other * PART_B, 128), PART_A)].astype(BF16)
    forward(y, zh, "a", z_fwd, r_z1)
    forward(y, zh, "a", z_bwd, r_z1 + 3)

    @pl.when(jnp.logical_and(c == 0, g > 0))
    def _():
        await_bytes(stage.at[0:COLS, 0:TILE], r_left)
        await_bytes(stage.at[COLS:PAIR, 0:TILE], r_left + 1)

    @pl.when(jnp.logical_and(c == 1, g < 15))
    def _():
        await_bytes(stage.at[0:COLS, 512:HALF], r_right)
        await_bytes(stage.at[COLS:PAIR, 512:HALF], r_right + 1)

    block(y, zh, "b")[...] = stage[:, pl.ds(pl.multiple_of(c * PART_A, 128), PART_B)].astype(BF16)
    forward(y, zh, "b", z_bwd, r_z1 + 1)
    forward(y, zh, "b", z_fwd, r_z1 + 2)

    def column(number):
        return zh + sign * (0, -1, 1)[number]

    def send_y1(number):
        forward(y, column(number), "all", y_fwd, r_y1 + 2 * number)
        forward(y, column(number), "all", y_bwd, r_y1 + 2 * number + 1)

    def take_y1(number):
        bz = column(number)
        await_bytes(block(y - sign, bz, "all"), r_y1 + 2 * number)
        forward(y - sign, bz, "a", y_fwd, r_y2 + 2 * number)
        await_bytes(block(y + sign, bz, "all"), r_y1 + 2 * number + 1)
        forward(y + sign, bz, "b", y_bwd, r_y2 + 2 * number + 1)
        share(y - sign, bz, "all")
        share(y + sign, bz, "all")

    def take_y2(number):
        bz = column(number)
        await_bytes(block(y + 2, bz, "a"), r_y2 + 2 * number)
        share(y + 2, bz, "a")
        await_bytes(block(y + 2, bz, "b"), r_y2 + 2 * number + 1)
        share(y + 2, bz, "b")

    def send_y3(part):
        first = r_y3 + (0 if part == "a" else 3)
        forward(y, zh + 2, part, y_fwd, first)
        forward(y, zh + 2, part, y_bwd, first + 1)
        forward(y, zh + 2, part, y_far, first + 2)
        share(y, zh + 2, part)

    def take_y3(part):
        first = r_y3 + (0 if part == "a" else 3)
        for offset, by in enumerate((y - sign, y + sign, y + 2)):
            await_bytes(block(by, zh + 2, part), first + offset)
            share(by, zh + 2, part)

    send_y1(0)
    share(y, zh, "all")

    for load in loads[3:6]:
        load.wait()
    for tile in range(8):
        dense = adj[tile].astype(F32)
        padded = jnp.concatenate([dense, jnp.zeros((TILE, TILE), F32)], 1)
        moved = pltpu.roll(padded, off[tile] - tile * TILE, 1)
        band[tile] = (moved * live[tile].astype(F32)).astype(BF16)

    for step in range(1, 4):
        await_bytes(wg.at[c, w_src_y * 4 + mod4(zh + step)], r_w1 + 4 - step)

    @pl.when(x != 0)
    def _():
        await_bytes(wg.at[c, w_src_y * 4 + zh], r_w1)

    r_w2 = slot(1, 4)
    part_w = wg.at[c, pl.ds(w_src_y * 4, 4)]
    for step in range(1, 4):
        copy(part_w, part_w, device(g - x + mod4(x + step), p, c), r_w2 + step)

    take_y1(0)

    for step in range(1, 4):
        await_bytes(wg.at[c, pl.ds(mod4(y + x - step) * 4, 4)], r_w2 + step)
    r_w3 = slot(1)
    copy(wg.at[c], wg.at[c], partner, r_w3)
    take_y2(0)

    await_bytes(block(y, zh - sign, "a"), r_z1)
    forward(y, zh - sign, "a", z_fwd, r_z2)
    await_bytes(block(y, zh + sign, "b"), r_z1 + 1)
    forward(y, zh + sign, "b", z_bwd, r_z2 + 1)
    await_bytes(block(y, zh + sign, "a"), r_z1 + 3)
    send_y1(2)
    await_bytes(block(y, zh - sign, "b"), r_z1 + 2)
    send_y1(1)
    share(y, zh - sign, "all")
    share(y, zh + sign, "all")

    await_bytes(wg.at[other], r_w3)
    for col in range(4):
        rows = []
        for row in range(4):
            for core in range(2):
                rows.append(wg[core, row * 4 + col].astype(F32)[0:COLS])
        wt[col] = jnp.concatenate(rows, 0).T.astype(BF16)

    loads[6].wait()
    spot = lax.broadcasted_iota(jnp.int32, (32, 1024), 1)
    row = lax.broadcasted_iota(jnp.int32, (32, 1024), 0)
    bias_own = jnp.sum(
        jnp.where(spot == row + f * 32, jnp.broadcast_to(bias[...], (32, 1024)), 0.0),
        axis=1, keepdims=True,
    )
    pre_acc[...] = jnp.broadcast_to(bias_own, (32, 1024))

    def compute(bz):
        col = mod4(bz)
        rows = pl.ds(pl.multiple_of(col * COLUMN, 16), COLUMN)
        await_bytes(xg.at[rows, pl.ds(pl.multiple_of(other * HALF, 128), HALF)], r_pair + col)
        for tile in range(8):
            nb[rows, tile * TILE:(tile + 1) * TILE] = lax.dot_general(
                xg[rows, tile * TILE:tile * TILE + 3 * TILE], band[tile],
                (((1,), (1,)), ((), ())), preferred_element_type=F32,
            ).astype(BF16)
        ws_t = wt[col, pl.ds(pl.multiple_of(c * 32, 16), 32), :]
        wn_t = wt[col, pl.ds(pl.multiple_of(64 + c * 32, 16), 32), :]
        pre_acc[...] += (
            jnp.dot(ws_t, xg[rows, TILE:TILE + 1024], preferred_element_type=F32)
            + jnp.dot(wn_t, nb[rows, :], preferred_element_type=F32)
        )

    compute(zh)
    take_y1(2)
    take_y1(1)
    await_bytes(block(y, zh + 2, "a"), r_z2)
    send_y3("a")
    await_bytes(block(y, zh + 2, "b"), r_z2 + 1)
    send_y3("b")
    take_y2(2)
    take_y2(1)
    compute(zh - 1)
    compute(zh + 1)
    take_y3("a")
    take_y3("b")
    compute(zh + 2)

    loads[7].wait()
    pre = pre_acc[...]
    gate = jax.nn.sigmoid(pre)
    act = pre * gate
    hid[...] = act.astype(BF16)
    delta = (act - tgt[...].astype(F32)) * (gate * (1.0 + pre * (1.0 - gate))) * (1.0 / 128.0)

    head = delta.astype(BF16)
    rest = (delta - head.astype(F32)).astype(BF16)
    both = jnp.concatenate([head] * 4 + [rest] * 4, 0)
    turn = (((1,), (1,)), ((), ()))
    lanes = lax.broadcasted_iota(jnp.int32, (32, 128), 1)
    spots = lax.rem(lanes, 64)
    bias_term = jnp.sum(delta, axis=1, keepdims=True)
    quarter = lax.div(lax.broadcasted_iota(jnp.int32, (PAIR, 128), 1), 32)
    blank = jnp.zeros((16, 128), F32)

    r_ra = slot(1, 4)
    terms = []
    for row in range(4):
        spans = [slice((col * 4 + row) * PAIR, (col * 4 + row + 1) * PAIR) for col in range(4)]
        left = jnp.concatenate(
            [xg[span, TILE:TILE + 1024] for span in spans] + [nb[span, :] for span in spans], 0
        )
        grad = lax.dot_general(left, both, turn, preferred_element_type=F32)
        grad = grad[:, 0:128] + grad[:, 128:256]

        def packed(first):
            parts = [grad[first + col * PAIR:first + (col + 1) * PAIR] for col in range(4)]
            low = jnp.where(quarter == 0, parts[0], parts[1])
            high = jnp.where(quarter == 2, parts[2], parts[3])
            return jnp.where(quarter < 2, low, high)

        own_term, nb_term = packed(0), packed(COLUMN)
        turned = jnp.concatenate(
            [own_term[0:COLS], nb_term[0:COLS], blank, own_term[COLS:PAIR], nb_term[COLS:PAIR], blank], 0
        ).T
        for col in range(4):
            rsend[row, col] = jnp.where(spots == 48, bias_term, turned[col * 32:(col + 1) * 32])
        terms.append(remote(rsend.at[row], ra.at[x], device(g - x + row, p, c), slot(0), r_ra + x))
        start_unless(x == row, terms[row])

    def with_bias(tile, low_total, high_total):
        lane_of = lax.broadcasted_iota(jnp.int32, tile.shape, 1)
        bias_sum = jnp.where(lane_of < 64, low_total, high_total)
        first = bias_sum.astype(BF16).astype(F32)
        tile = jnp.where(lax.rem(lane_of, 64) == 48, first, tile)
        return jnp.where(lax.rem(lane_of, 64) == 49, bias_sum - first, tile)

    for step in range(1, 4):
        from_x = mod4(x + step)
        await_bytes(ra.at[from_x], r_ra + from_x)
    xs = [mod4(x + step) for step in range(1, 4)]
    halves = lax.broadcasted_iota(jnp.int32, (16, 128), 1) < 64
    for col in range(4):
        summed = (rsend[x, col] + ra[xs[0], col]) + (ra[xs[1], col] + ra[xs[2], col])
        summed = with_bias(summed, summed[:, 48:49], summed[:, 48:49])
        top, bottom = summed[0:16], summed[16:32]
        rbs[col, 0] = jnp.where(halves, top, pltpu.roll(bottom, 64, 1)).astype(BF16)
        rbs[col, 1] = jnp.where(halves, pltpu.roll(top, 64, 1), bottom).astype(BF16)

    r_rb = slot(1)
    to_group = zh * 4 + mod4(y + x)
    for step in range(1, 4):
        col = mod4(zh + step)
        for core in range(2):
            copy(rbs.at[col, core], rb.at[zl, c], device(to_group, x * 4 + col, core), r_rb)
    copy(rbs.at[zh, other], rb.at[zl, c], device(to_group, x * 4 + zh, other), r_rb)
    r_zero = remote(rbs.at[zh, c], rb.at[zl, c], device(to_group, x * 4 + zh, c), slot(0), r_rb)
    start_unless(stays, r_zero)

    @pl.when(stays)
    def _():
        pltpu.make_async_copy(rbs.at[zh, c], rb.at[zl, c], recv_sem.at[r_rb]).start()

    await_bytes(rb, r_rb)
    for core in range(2):
        total = (rb[0, core].astype(F32) + rb[1, core].astype(F32)) + (
            rb[2, core].astype(F32) + rb[3, core].astype(F32)
        )
        fg[r_chip, core] = with_bias(
            total, total[:, 48:49] + total[:, 49:50], total[:, 112:113] + total[:, 113:114]
        ).astype(BF16)

    r_r2 = slot(1)
    for step in range(1, 16):
        copy(fg.at[r_chip], fg.at[r_chip], device(lax.rem(g + step, 16), p, c), r_r2)
    await_bytes(fg.at[0:15], r_r2)
    for part in range(8):
        rows = []
        for chip in (2 * part, 2 * part + 1):
            for core in range(2):
                tile = fg[chip, core].astype(F32)
                rows += [tile, pltpu.roll(tile, 64, 1)]
        turned = jnp.concatenate(rows, 0).T
        span = slice(part * 128, (part + 1) * 128)
        gs_o[:, span] = turned[0:24]
        gn_o[:, span] = turned[24:48]
        gb_o[:, span] = turned[48:49] + turned[49:50]

    for made in sent:
        made.wait_send()

    @pl.when(g < 15)
    def _():
        halo_up.wait_send()

    @pl.when(g > 0)
    def _():
        halo_down.wait_send()

    @pl.when(x != 0)
    def _():
        w_zero.wait_send()

    @pl.when(jnp.logical_not(stays))
    def _():
        r_zero.wait_send()

    for row in range(4):
        @pl.when(x != row)
        def _():
            terms[row].wait_send()

    assert used[0] <= SENDS and used[1] <= RECVS, used


OUTS = (
    jax.ShapeDtypeStruct((32, 1024), BF16),
    jax.ShapeDtypeStruct((COLS, 1024), F32),
    jax.ShapeDtypeStruct((COLS, 1024), F32),
    jax.ShapeDtypeStruct((1, 1024), F32),
)


def shards(features, adjacency, offsets, live, w_self, w_neigh, bias, targets):
    vmem = pl.BlockSpec(memory_space=pltpu.VMEM)
    hbm = pl.BlockSpec(memory_space=pltpu.HBM)
    inputs = [features.T, adjacency, offsets, live, w_self, w_neigh, bias.reshape(1, 1024), targets]
    hidden, grad_self, grad_neigh, grad_bias = pl.pallas_call(
        kernel,
        out_shape=OUTS,
        in_specs=[hbm] * 8,
        out_specs=(vmem,) * 4,
        scratch_shapes=[
            pltpu.VMEM((COLS, 1024), BF16),
            pltpu.VMEM((8, TILE, 256), BF16),
            pltpu.SMEM((8,), jnp.int32),
            pltpu.SMEM((8,), jnp.int32),
            pltpu.VMEM((COLS, 1024), BF16),
            pltpu.VMEM((COLS, 1024), BF16),
            pltpu.VMEM((1, 1024), F32),
            pltpu.VMEM((32, 1024), BF16),
            pltpu.VMEM((COLS, 1024), F32),
            pltpu.VMEM((PAIR, HALF), F32),
            pltpu.VMEM((768, 1280), BF16),
            pltpu.VMEM((768, 1024), BF16),
            pltpu.VMEM((8, TILE, 384), BF16),
            pltpu.VMEM((16, 32, 128), BF16),
            pltpu.VMEM((2, 16, 32, 128), BF16),
            pltpu.VMEM((4, 128, COLUMN), BF16),
            pltpu.VMEM((32, 1024), F32),
            pltpu.VMEM((4, 4, 32, 128), F32),
            pltpu.VMEM((4, 4, 32, 128), F32),
            pltpu.VMEM((4, 2, 16, 128), BF16),
            pltpu.VMEM((4, 2, 16, 128), BF16),
            pltpu.VMEM((16, 2, 16, 128), BF16),
            pltpu.SemaphoreType.DMA((8,)),
            pltpu.SemaphoreType.DMA((SENDS,)),
            pltpu.SemaphoreType.DMA((RECVS,)),
        ],
        compiler_params=pltpu.CompilerParams(
            collective_id=0, has_side_effects=True, vmem_limit_bytes=48 * 1024 * 1024
        ),
        cost_estimate=pl.CostEstimate(flops=10**9, bytes_accessed=10**7, transcendentals=32768),
    )(*[pltpu.with_memory_space_constraint(array, pltpu.HBM) for array in inputs])
    return hidden, grad_self, grad_neigh, grad_bias.reshape(1024)


def solution(mesh):
    in_specs = (
        P("grp", "feat"),
        P("grp", None, None),
        P("grp"),
        P("grp"),
        P("feat", None),
        P("feat", None),
        P(),
        P("feat", "grp"),
    )
    out_specs = (P("feat", "grp"), P("feat", None), P("feat", None), P())
    return jax.shard_map(shards, mesh=mesh, in_specs=in_specs, out_specs=out_specs, check_vma=False)
```

```python
import jax
import jax.numpy as jnp
from jax import lax
from jax.experimental import pallas as pl
from jax.experimental.pallas import tpu as pltpu
from jax.sharding import PartitionSpec as P

F32 = jnp.float32
BF16 = jnp.bfloat16
MESH = pl.DeviceIdType.MESH

COLS = 24
PAIR = 48
COLUMN = 4 * PAIR
HALF = 640
PART_A = 384
PART_B = HALF - PART_A
TILE = 128
SENDS = 96
RECVS = 72


def mod4(value):
    return lax.rem(value + 4, 4)


def kernel(
    feat_h, adj_h, off_h, live_h, ws_h, wn_h, bias_h, tgt_h,
    hid, gs_o, gn_o, gb_o,
    feat, adj, off, live, ws, wn, bias, tgt,
    wide, stage, xg, nb, band, wsend, wg, wt, pre_acc, rsend, ra, rbs, rb, fg,
    in_sem, send_sem, recv_sem,
):
    loads = [
        pltpu.make_async_copy(src, dst, in_sem.at[i])
        for i, (src, dst) in enumerate(
            [(feat_h, feat), (ws_h, ws), (wn_h, wn), (adj_h, adj), (off_h, off), (live_h, live),
             (bias_h, bias), (tgt_h, tgt)]
        )
    ]
    for load in loads:
        load.start()

    g = lax.axis_index("grp")
    f = lax.axis_index("feat")
    c = lax.rem(f, 2)
    p = lax.div(f, 2)
    y = lax.div(p, 4)
    zh = lax.rem(p, 4)
    x = lax.rem(g, 4)
    zl = lax.div(g, 4)
    other = 1 - c
    sign = 1 - 2 * c

    def device(group, chip, core):
        return (group, chip * 2 + core)

    partner = device(g, p, other)
    y_fwd = device(g, mod4(y + sign) * 4 + zh, c)
    y_bwd = device(g, mod4(y - sign) * 4 + zh, c)
    y_far = device(g, mod4(y + 2) * 4 + zh, c)
    z_fwd = device(g, y * 4 + mod4(zh + sign), c)
    z_bwd = device(g, y * 4 + mod4(zh - sign), c)
    stays = jnp.logical_and(zh == zl, jnp.logical_and(x == 0, y == 0))

    barrier = pltpu.get_barrier_semaphore()

    def tell(target):
        pl.semaphore_signal(barrier, inc=1, device_id=target, device_id_type=MESH)

    @pl.when(jnp.logical_and(c == 0, g > 0))
    def _():
        tell(device(g - 1, p, 0))
        tell(device(g - 1, p, 1))

    @pl.when(jnp.logical_and(c == 1, g < 15))
    def _():
        tell(device(g + 1, p, 0))
        tell(device(g + 1, p, 1))

    for target in (z_fwd, z_bwd, y_fwd, y_bwd, y_far, partner):
        tell(target)

    w_src_y = mod4(y + x)
    w_dst_y = mod4(y - x)
    r_chip = mod4(x - y) * 4 + zl
    for step in range(1, 4):
        tell(device(g, w_src_y * 4 + mod4(zh + step), c))
        tell(device(mod4(zl + step) * 4 + y, r_chip, 0))
        tell(device(mod4(zl + step) * 4 + y, r_chip, 1))

    @pl.when(x != 0)
    def _():
        tell(device(g, w_src_y * 4 + zh, c))

    tell(device(zl * 4 + y, r_chip, other))

    @pl.when(jnp.logical_not(stays))
    def _():
        tell(device(zl * 4 + y, r_chip, c))

    def tell_far(step, carry):
        tell(device(lax.rem(g + step, 16), p, c))
        return carry

    lax.fori_loop(1, 16, tell_far, 0)

    loads[0].wait()
    wide[...] = feat[...].astype(F32)

    @pl.when(c == 0)
    def _():
        stage[0:COLS, TILE:HALF] = wide[:, 0:512]

        @pl.when(g == 0)
        def _():
            stage[:, 0:TILE] = jnp.zeros((PAIR, TILE), F32)

    @pl.when(c == 1)
    def _():
        stage[COLS:PAIR, 0:512] = wide[:, 512:1024]

        @pl.when(g == 15)
        def _():
            stage[:, 512:HALF] = jnp.zeros((PAIR, TILE), F32)

    waits = (
        6 + 3 + 7 + 15
        + (x != 0).astype(jnp.int32)
        + jnp.logical_not(stays).astype(jnp.int32)
        + (g < 15).astype(jnp.int32)
        + (g > 0).astype(jnp.int32)
    )
    pl.semaphore_wait(barrier, waits)

    used = [0, 0]
    sent = []

    def slot(which, count=1):
        used[which] += count
        return used[which] - count

    def remote(src, dst, target, send, recv):
        return pltpu.make_async_remote_copy(
            src_ref=src, dst_ref=dst, send_sem=send_sem.at[send], recv_sem=recv_sem.at[recv],
            device_id=target, device_id_type=MESH,
        )

    def copy(src, dst, target, recv):
        made = remote(src, dst, target, slot(0), recv)
        made.start()
        sent.append(made)

    def start_unless(skip, made):
        @pl.when(jnp.logical_not(skip))
        def _():
            made.start()

    def await_bytes(ref, recv):
        pltpu.make_async_copy(ref, ref, recv_sem.at[recv]).wait()

    own_rows = pl.ds(pl.multiple_of(c * COLS, 8), COLS)
    other_rows = pl.ds(pl.multiple_of(other * COLS, 8), COLS)
    r_left, r_right, r_swap = slot(1, 2), slot(1, 2), slot(1)
    halo_up = remote(
        wide.at[:, 896:1024], stage.at[own_rows, 0:TILE], device(g + 1, p, 0), slot(0), r_left + c
    )
    halo_down = remote(
        wide.at[:, 0:TILE], stage.at[own_rows, 512:HALF], device(g - 1, p, 1), slot(0), r_right + c
    )

    @pl.when(g < 15)
    def _():
        halo_up.start()

    @pl.when(g > 0)
    def _():
        halo_down.start()

    copy(
        wide.at[:, pl.ds(pl.multiple_of(other * 512, 128), 512)],
        stage.at[own_rows, pl.ds(pl.multiple_of(c * TILE, 128), 512)],
        partner, r_swap,
    )

    loads[1].wait()
    loads[2].wait()
    lane = lax.broadcasted_iota(jnp.int32, (COLS, 128), 1)
    pad = jnp.zeros((32 - COLS, 128), F32)
    for pair in range(8):
        s_tile = ws[:, pair * 128:(pair + 1) * 128].astype(F32)
        n_tile = wn[:, pair * 128:(pair + 1) * 128].astype(F32)
        low = jnp.where(lane < 64, s_tile, pltpu.roll(n_tile, 64, 1))
        high = jnp.where(lane < 64, pltpu.roll(s_tile, 64, 1), n_tile)
        wsend[2 * pair] = jnp.concatenate([low, pad], 0).astype(BF16)
        wsend[2 * pair + 1] = jnp.concatenate([high, pad], 0).astype(BF16)

    r_w1 = slot(1, 4)
    for step in range(1, 4):
        chip = w_dst_y * 4 + mod4(zh + step)
        copy(wsend.at[chip], wg.at[c, p], device(g, chip, c), r_w1 + step)
    chip0 = w_dst_y * 4 + zh
    w_zero = remote(wsend.at[chip0], wg.at[c, p], device(g, chip0, c), slot(0), r_w1)

    @pl.when(x != 0)
    def _():
        w_zero.start()

    @pl.when(x == 0)
    def _():
        wg[c, p] = wsend[chip0]

    def block(by, bz, part):
        rows = pl.ds(pl.multiple_of((mod4(bz) * 4 + mod4(by)) * PAIR, 16), PAIR)
        start = {"all": 0, "a": other * PART_B, "b": c * PART_A}[part]
        width = {"all": HALF, "a": PART_A, "b": PART_B}[part]
        return xg.at[rows, pl.ds(pl.multiple_of(c * HALF + start, 128), width)]

    r_pair = slot(1, 4)

    def forward(by, bz, part, target, recv):
        view = block(by, bz, part)
        copy(view, view, target, recv)

    def share(by, bz, part):
        forward(by, bz, part, partner, r_pair + mod4(bz))

    r_z1 = slot(1, 4)
    r_z2 = slot(1, 2)
    r_y1 = slot(1, 12)
    r_y2 = slot(1, 6)
    r_y3 = slot(1, 6)

    await_bytes(stage.at[other_rows, pl.ds(pl.multiple_of(other * TILE, 128), 512)], r_swap)
    block(y, zh, "a")[...] = stage[:, pl.ds(pl.multiple_of(other * PART_B, 128), PART_A)].astype(BF16)
    forward(y, zh, "a", z_fwd, r_z1)
    forward(y, zh, "a", z_bwd, r_z1 + 3)

    @pl.when(jnp.logical_and(c == 0, g > 0))
    def _():
        await_bytes(stage.at[0:COLS, 0:TILE], r_left)
        await_bytes(stage.at[COLS:PAIR, 0:TILE], r_left + 1)

    @pl.when(jnp.logical_and(c == 1, g < 15))
    def _():
        await_bytes(stage.at[0:COLS, 512:HALF], r_right)
        await_bytes(stage.at[COLS:PAIR, 512:HALF], r_right + 1)

    block(y, zh, "b")[...] = stage[:, pl.ds(pl.multiple_of(c * PART_A, 128), PART_B)].astype(BF16)
    forward(y, zh, "b", z_bwd, r_z1 + 1)
    forward(y, zh, "b", z_fwd, r_z1 + 2)

    def column(number):
        return zh + sign * (0, -1, 1)[number]

    def send_y1(number, part):
        first = r_y1 + 4 * number + (0 if part == "a" else 2)
        forward(y, column(number), part, y_fwd, first)
        forward(y, column(number), part, y_bwd, first + 1)

    def take_y1(number):
        bz = column(number)
        first = r_y1 + 4 * number
        await_bytes(block(y - sign, bz, "a"), first)
        forward(y - sign, bz, "a", y_fwd, r_y2 + 2 * number)
        await_bytes(block(y + sign, bz, "b"), first + 3)
        forward(y + sign, bz, "b", y_bwd, r_y2 + 2 * number + 1)
        await_bytes(block(y - sign, bz, "b"), first + 2)
        share(y - sign, bz, "all")
        await_bytes(block(y + sign, bz, "a"), first + 1)
        share(y + sign, bz, "all")

    def take_y2(number):
        bz = column(number)
        await_bytes(block(y + 2, bz, "a"), r_y2 + 2 * number)
        share(y + 2, bz, "a")
        await_bytes(block(y + 2, bz, "b"), r_y2 + 2 * number + 1)
        share(y + 2, bz, "b")

    def send_y3(part):
        first = r_y3 + (0 if part == "a" else 3)
        forward(y, zh + 2, part, y_fwd, first)
        forward(y, zh + 2, part, y_bwd, first + 1)
        forward(y, zh + 2, part, y_far, first + 2)
        share(y, zh + 2, part)

    def take_y3(part):
        first = r_y3 + (0 if part == "a" else 3)
        for offset, by in enumerate((y - sign, y + sign, y + 2)):
            await_bytes(block(by, zh + 2, part), first + offset)
            share(by, zh + 2, part)

    send_y1(0, "a")
    send_y1(0, "b")
    share(y, zh, "all")

    for load in loads[3:6]:
        load.wait()
    for tile in range(8):
        dense = adj[tile].astype(F32)
        padded = jnp.concatenate([dense, jnp.zeros((TILE, TILE), F32)], 1)
        moved = pltpu.roll(padded, off[tile] - tile * TILE, 1)
        band[tile] = (moved * live[tile].astype(F32)).astype(BF16)

    for step in range(1, 4):
        await_bytes(wg.at[c, w_src_y * 4 + mod4(zh + step)], r_w1 + 4 - step)

    @pl.when(x != 0)
    def _():
        await_bytes(wg.at[c, w_src_y * 4 + zh], r_w1)

    r_w2 = slot(1, 4)
    part_w = wg.at[c, pl.ds(w_src_y * 4, 4)]
    for step in range(1, 4):
        copy(part_w, part_w, device(g - x + mod4(x + step), p, c), r_w2 + step)

    take_y1(0)

    for step in range(1, 4):
        await_bytes(wg.at[c, pl.ds(mod4(y + x - step) * 4, 4)], r_w2 + step)
    r_w3 = slot(1)
    copy(wg.at[c], wg.at[c], partner, r_w3)
    take_y2(0)

    await_bytes(block(y, zh - sign, "a"), r_z1)
    forward(y, zh - sign, "a", z_fwd, r_z2)
    send_y1(1, "a")
    await_bytes(block(y, zh + sign, "a"), r_z1 + 3)
    send_y1(2, "a")

    await_bytes(wg.at[other], r_w3)
    for col in range(4):
        rows = []
        for row in range(4):
            for core in range(2):
                rows.append(wg[core, row * 4 + col].astype(F32)[0:COLS])
        wt[col] = jnp.concatenate(rows, 0).T.astype(BF16)

    loads[6].wait()
    spot = lax.broadcasted_iota(jnp.int32, (32, 1024), 1)
    row = lax.broadcasted_iota(jnp.int32, (32, 1024), 0)
    bias_own = jnp.sum(
        jnp.where(spot == row + f * 32, jnp.broadcast_to(bias[...], (32, 1024)), 0.0),
        axis=1, keepdims=True,
    )
    pre_acc[...] = jnp.broadcast_to(bias_own, (32, 1024))

    def compute(bz):
        col = mod4(bz)
        rows = pl.ds(pl.multiple_of(col * COLUMN, 16), COLUMN)
        await_bytes(xg.at[rows, pl.ds(pl.multiple_of(other * HALF, 128), HALF)], r_pair + col)
        for tile in range(8):
            nb[rows, tile * TILE:(tile + 1) * TILE] = lax.dot_general(
                xg[rows, tile * TILE:tile * TILE + 3 * TILE], band[tile],
                (((1,), (1,)), ((), ())), preferred_element_type=F32,
            ).astype(BF16)
        ws_t = wt[col, pl.ds(pl.multiple_of(c * 32, 16), 32), :]
        wn_t = wt[col, pl.ds(pl.multiple_of(64 + c * 32, 16), 32), :]
        pre_acc[...] += (
            jnp.dot(ws_t, xg[rows, TILE:TILE + 1024], preferred_element_type=F32)
            + jnp.dot(wn_t, nb[rows, :], preferred_element_type=F32)
        )

    compute(zh)
    await_bytes(block(y, zh + sign, "b"), r_z1 + 1)
    forward(y, zh + sign, "b", z_bwd, r_z2 + 1)
    send_y1(2, "b")
    await_bytes(block(y, zh - sign, "b"), r_z1 + 2)
    send_y1(1, "b")
    share(y, zh - sign, "all")
    share(y, zh + sign, "all")
    take_y1(1)
    take_y1(2)
    await_bytes(block(y, zh + 2, "a"), r_z2)
    send_y3("a")
    await_bytes(block(y, zh + 2, "b"), r_z2 + 1)
    send_y3("b")
    take_y2(2)
    take_y2(1)
    compute(zh - 1)
    compute(zh + 1)
    take_y3("a")
    take_y3("b")
    compute(zh + 2)

    loads[7].wait()
    pre = pre_acc[...]
    gate = jax.nn.sigmoid(pre)
    act = pre * gate
    hid[...] = act.astype(BF16)
    delta = (act - tgt[...].astype(F32)) * (gate * (1.0 + pre * (1.0 - gate))) * (1.0 / 128.0)

    head = delta.astype(BF16)
    rest = (delta - head.astype(F32)).astype(BF16)
    both = jnp.concatenate([head] * 4 + [rest] * 4, 0)
    turn = (((1,), (1,)), ((), ()))
    lanes = lax.broadcasted_iota(jnp.int32, (32, 128), 1)
    spots = lax.rem(lanes, 64)
    bias_term = jnp.sum(delta, axis=1, keepdims=True)
    quarter = lax.div(lax.broadcasted_iota(jnp.int32, (PAIR, 128), 1), 32)
    blank = jnp.zeros((16, 128), F32)

    r_ra = slot(1, 4)
    terms = []
    for row in range(4):
        spans = [slice((col * 4 + row) * PAIR, (col * 4 + row + 1) * PAIR) for col in range(4)]
        left = jnp.concatenate(
            [xg[span, TILE:TILE + 1024] for span in spans] + [nb[span, :] for span in spans], 0
        )
        grad = lax.dot_general(left, both, turn, preferred_element_type=F32)
        grad = grad[:, 0:128] + grad[:, 128:256]

        def packed(first):
            parts = [grad[first + col * PAIR:first + (col + 1) * PAIR] for col in range(4)]
            low = jnp.where(quarter == 0, parts[0], parts[1])
            high = jnp.where(quarter == 2, parts[2], parts[3])
            return jnp.where(quarter < 2, low, high)

        own_term, nb_term = packed(0), packed(COLUMN)
        turned = jnp.concatenate(
            [own_term[0:COLS], nb_term[0:COLS], blank, own_term[COLS:PAIR], nb_term[COLS:PAIR], blank], 0
        ).T
        for col in range(4):
            rsend[row, col] = jnp.where(spots == 48, bias_term, turned[col * 32:(col + 1) * 32])
        terms.append(remote(rsend.at[row], ra.at[x], device(g - x + row, p, c), slot(0), r_ra + x))
        start_unless(x == row, terms[row])

    def with_bias(tile, low_total, high_total):
        lane_of = lax.broadcasted_iota(jnp.int32, tile.shape, 1)
        bias_sum = jnp.where(lane_of < 64, low_total, high_total)
        first = bias_sum.astype(BF16).astype(F32)
        tile = jnp.where(lax.rem(lane_of, 64) == 48, first, tile)
        return jnp.where(lax.rem(lane_of, 64) == 49, bias_sum - first, tile)

    for step in range(1, 4):
        from_x = mod4(x + step)
        await_bytes(ra.at[from_x], r_ra + from_x)
    xs = [mod4(x + step) for step in range(1, 4)]
    halves = lax.broadcasted_iota(jnp.int32, (16, 128), 1) < 64
    for col in range(4):
        summed = (rsend[x, col] + ra[xs[0], col]) + (ra[xs[1], col] + ra[xs[2], col])
        summed = with_bias(summed, summed[:, 48:49], summed[:, 48:49])
        top, bottom = summed[0:16], summed[16:32]
        rbs[col, 0] = jnp.where(halves, top, pltpu.roll(bottom, 64, 1)).astype(BF16)
        rbs[col, 1] = jnp.where(halves, pltpu.roll(top, 64, 1), bottom).astype(BF16)

    r_rb = slot(1)
    to_group = zh * 4 + mod4(y + x)
    for step in range(1, 4):
        col = mod4(zh + step)
        for core in range(2):
            copy(rbs.at[col, core], rb.at[zl, c], device(to_group, x * 4 + col, core), r_rb)
    copy(rbs.at[zh, other], rb.at[zl, c], device(to_group, x * 4 + zh, other), r_rb)
    r_zero = remote(rbs.at[zh, c], rb.at[zl, c], device(to_group, x * 4 + zh, c), slot(0), r_rb)
    start_unless(stays, r_zero)

    @pl.when(stays)
    def _():
        pltpu.make_async_copy(rbs.at[zh, c], rb.at[zl, c], recv_sem.at[r_rb]).start()

    await_bytes(rb, r_rb)
    for core in range(2):
        total = (rb[0, core].astype(F32) + rb[1, core].astype(F32)) + (
            rb[2, core].astype(F32) + rb[3, core].astype(F32)
        )
        fg[r_chip, core] = with_bias(
            total, total[:, 48:49] + total[:, 49:50], total[:, 112:113] + total[:, 113:114]
        ).astype(BF16)

    r_r2 = slot(1)
    for step in range(1, 16):
        copy(fg.at[r_chip], fg.at[r_chip], device(lax.rem(g + step, 16), p, c), r_r2)
    await_bytes(fg.at[0:15], r_r2)
    for part in range(8):
        rows = []
        for chip in (2 * part, 2 * part + 1):
            for core in range(2):
                tile = fg[chip, core].astype(F32)
                rows += [tile, pltpu.roll(tile, 64, 1)]
        turned = jnp.concatenate(rows, 0).T
        span = slice(part * 128, (part + 1) * 128)
        gs_o[:, span] = turned[0:24]
        gn_o[:, span] = turned[24:48]
        gb_o[:, span] = turned[48:49] + turned[49:50]

    for made in sent:
        made.wait_send()

    @pl.when(g < 15)
    def _():
        halo_up.wait_send()

    @pl.when(g > 0)
    def _():
        halo_down.wait_send()

    @pl.when(x != 0)
    def _():
        w_zero.wait_send()

    @pl.when(jnp.logical_not(stays))
    def _():
        r_zero.wait_send()

    for row in range(4):
        @pl.when(x != row)
        def _():
            terms[row].wait_send()

    assert used[0] <= SENDS and used[1] <= RECVS, used


OUTS = (
    jax.ShapeDtypeStruct((32, 1024), BF16),
    jax.ShapeDtypeStruct((COLS, 1024), F32),
    jax.ShapeDtypeStruct((COLS, 1024), F32),
    jax.ShapeDtypeStruct((1, 1024), F32),
)


def place(hid, gs, gn, gb, hid_o, gs_o, gn_o, gb_o, sem):
    pairs = [(hid, hid_o), (gs, gs_o), (gn, gn_o), (gb, gb_o)]
    moves = [pltpu.make_async_copy(src, dst, sem.at[i]) for i, (src, dst) in enumerate(pairs)]
    for move in moves:
        move.start()
    for move in moves:
        move.wait()


def shards(features, adjacency, offsets, live, w_self, w_neigh, bias, targets):
    vmem = pl.BlockSpec(memory_space=pltpu.VMEM)
    hbm = pl.BlockSpec(memory_space=pltpu.HBM)
    inputs = [features.T, adjacency, offsets, live, w_self, w_neigh, bias.reshape(1, 1024), targets]
    results = pl.pallas_call(
        kernel,
        out_shape=OUTS,
        in_specs=[hbm] * 8,
        out_specs=(vmem,) * 4,
        scratch_shapes=[
            pltpu.VMEM((COLS, 1024), BF16),
            pltpu.VMEM((8, TILE, 256), BF16),
            pltpu.SMEM((8,), jnp.int32),
            pltpu.SMEM((8,), jnp.int32),
            pltpu.VMEM((COLS, 1024), BF16),
            pltpu.VMEM((COLS, 1024), BF16),
            pltpu.VMEM((1, 1024), F32),
            pltpu.VMEM((32, 1024), BF16),
            pltpu.VMEM((COLS, 1024), F32),
            pltpu.VMEM((PAIR, HALF), F32),
            pltpu.VMEM((768, 1280), BF16),
            pltpu.VMEM((768, 1024), BF16),
            pltpu.VMEM((8, TILE, 384), BF16),
            pltpu.VMEM((16, 32, 128), BF16),
            pltpu.VMEM((2, 16, 32, 128), BF16),
            pltpu.VMEM((4, 128, COLUMN), BF16),
            pltpu.VMEM((32, 1024), F32),
            pltpu.VMEM((4, 4, 32, 128), F32),
            pltpu.VMEM((4, 4, 32, 128), F32),
            pltpu.VMEM((4, 2, 16, 128), BF16),
            pltpu.VMEM((4, 2, 16, 128), BF16),
            pltpu.VMEM((16, 2, 16, 128), BF16),
            pltpu.SemaphoreType.DMA((8,)),
            pltpu.SemaphoreType.DMA((SENDS,)),
            pltpu.SemaphoreType.DMA((RECVS,)),
        ],
        compiler_params=pltpu.CompilerParams(
            collective_id=0, has_side_effects=True, vmem_limit_bytes=48 * 1024 * 1024
        ),
        cost_estimate=pl.CostEstimate(flops=10**9, bytes_accessed=10**7, transcendentals=32768),
    )(*[pltpu.with_memory_space_constraint(array, pltpu.HBM) for array in inputs])
    hidden, grad_self, grad_neigh, grad_bias = pl.pallas_call(
        place,
        out_shape=OUTS,
        in_specs=[vmem] * 4,
        out_specs=(pl.BlockSpec(memory_space=pl.ANY),) * 4,
        scratch_shapes=[pltpu.SemaphoreType.DMA((4,))],
        compiler_params=pltpu.CompilerParams(vmem_limit_bytes=1024 * 1024),
    )(*[pltpu.with_memory_space_constraint(array, pltpu.VMEM) for array in results])
    return hidden, grad_self, grad_neigh, grad_bias.reshape(1024)


def solution(mesh):
    in_specs = (
        P("grp", "feat"),
        P("grp", None, None),
        P("grp"),
        P("grp"),
        P("feat", None),
        P("feat", None),
        P(),
        P("feat", "grp"),
    )
    out_specs = (P("feat", "grp"), P("feat", None), P("feat", None), P())
    return jax.shard_map(shards, mesh=mesh, in_specs=in_specs, out_specs=out_specs, check_vma=False)
```

```python
import jax
import jax.numpy as jnp
from jax import lax
from jax.experimental import pallas as pl
from jax.experimental.pallas import tpu as pltpu
from jax.sharding import PartitionSpec as P

F32 = jnp.float32
BF16 = jnp.bfloat16
MESH = pl.DeviceIdType.MESH

COLS = 24
PAIR = 48
COLUMN = 4 * PAIR
HALF = 640
PART_A = 384
PART_B = HALF - PART_A
TILE = 128
SENDS = 96
RECVS = 72


def mod4(value):
    return lax.rem(value + 4, 4)


def kernel(
    feat_h, adj_h, off_h, live_h, ws_h, wn_h, bias_h, tgt_h,
    hid, gs_o, gn_o, gb_o,
    feat, adj, off, live, ws, wn, bias, tgt,
    wide, stage, xg, nb, band, wsend, wg, wt, pre_acc, rsend, ra, rbs, rb, fg,
    in_sem, send_sem, recv_sem,
):
    loads = [
        pltpu.make_async_copy(src, dst, in_sem.at[i])
        for i, (src, dst) in enumerate(
            [(feat_h, feat), (ws_h, ws), (wn_h, wn), (adj_h, adj), (off_h, off), (live_h, live),
             (bias_h, bias), (tgt_h, tgt)]
        )
    ]
    for load in loads:
        load.start()

    g = lax.axis_index("grp")
    f = lax.axis_index("feat")
    c = lax.rem(f, 2)
    p = lax.div(f, 2)
    y = lax.div(p, 4)
    zh = lax.rem(p, 4)
    x = lax.rem(g, 4)
    zl = lax.div(g, 4)
    other = 1 - c
    sign = 1 - 2 * c

    def device(group, chip, core):
        return (group, chip * 2 + core)

    partner = device(g, p, other)
    y_fwd = device(g, mod4(y + sign) * 4 + zh, c)
    y_bwd = device(g, mod4(y - sign) * 4 + zh, c)
    y_far = device(g, mod4(y + 2) * 4 + zh, c)
    z_fwd = device(g, y * 4 + mod4(zh + sign), c)
    z_bwd = device(g, y * 4 + mod4(zh - sign), c)
    stays = jnp.logical_and(zh == zl, jnp.logical_and(x == 0, y == 0))

    barrier = pltpu.get_barrier_semaphore()

    def tell(target):
        pl.semaphore_signal(barrier, inc=1, device_id=target, device_id_type=MESH)

    @pl.when(jnp.logical_and(c == 0, g > 0))
    def _():
        tell(device(g - 1, p, 0))
        tell(device(g - 1, p, 1))

    @pl.when(jnp.logical_and(c == 1, g < 15))
    def _():
        tell(device(g + 1, p, 0))
        tell(device(g + 1, p, 1))

    for target in (z_fwd, z_bwd, y_fwd, y_bwd, y_far, partner):
        tell(target)

    w_src_y = mod4(y + x)
    w_dst_y = mod4(y - x)
    r_chip = mod4(x - y) * 4 + zl
    for step in range(1, 4):
        tell(device(g, w_src_y * 4 + mod4(zh + step), c))
        tell(device(mod4(zl + step) * 4 + y, r_chip, 0))
        tell(device(mod4(zl + step) * 4 + y, r_chip, 1))

    @pl.when(x != 0)
    def _():
        tell(device(g, w_src_y * 4 + zh, c))

    tell(device(zl * 4 + y, r_chip, other))

    @pl.when(jnp.logical_not(stays))
    def _():
        tell(device(zl * 4 + y, r_chip, c))

    def tell_far(step, carry):
        tell(device(lax.rem(g + step, 16), p, c))
        return carry

    lax.fori_loop(1, 16, tell_far, 0)

    loads[0].wait()
    wide[...] = feat[...].astype(F32)

    @pl.when(c == 0)
    def _():
        stage[0:COLS, TILE:HALF] = wide[:, 0:512]

        @pl.when(g == 0)
        def _():
            stage[:, 0:TILE] = jnp.zeros((PAIR, TILE), F32)

    @pl.when(c == 1)
    def _():
        stage[COLS:PAIR, 0:512] = wide[:, 512:1024]

        @pl.when(g == 15)
        def _():
            stage[:, 512:HALF] = jnp.zeros((PAIR, TILE), F32)

    waits = (
        6 + 3 + 7 + 15
        + (x != 0).astype(jnp.int32)
        + jnp.logical_not(stays).astype(jnp.int32)
        + (g < 15).astype(jnp.int32)
        + (g > 0).astype(jnp.int32)
    )
    pl.semaphore_wait(barrier, waits)

    used = [0, 0]
    sent = []

    def slot(which, count=1):
        used[which] += count
        return used[which] - count

    def remote(src, dst, target, send, recv):
        return pltpu.make_async_remote_copy(
            src_ref=src, dst_ref=dst, send_sem=send_sem.at[send], recv_sem=recv_sem.at[recv],
            device_id=target, device_id_type=MESH,
        )

    def copy(src, dst, target, recv):
        made = remote(src, dst, target, slot(0), recv)
        made.start()
        sent.append(made)

    def start_unless(skip, made):
        @pl.when(jnp.logical_not(skip))
        def _():
            made.start()

    def await_bytes(ref, recv):
        pltpu.make_async_copy(ref, ref, recv_sem.at[recv]).wait()

    own_rows = pl.ds(pl.multiple_of(c * COLS, 8), COLS)
    other_rows = pl.ds(pl.multiple_of(other * COLS, 8), COLS)
    r_left, r_right, r_swap = slot(1, 2), slot(1, 2), slot(1)
    halo_up = remote(
        wide.at[:, 896:1024], stage.at[own_rows, 0:TILE], device(g + 1, p, 0), slot(0), r_left + c
    )
    halo_down = remote(
        wide.at[:, 0:TILE], stage.at[own_rows, 512:HALF], device(g - 1, p, 1), slot(0), r_right + c
    )

    @pl.when(g < 15)
    def _():
        halo_up.start()

    @pl.when(g > 0)
    def _():
        halo_down.start()

    copy(
        wide.at[:, pl.ds(pl.multiple_of(other * 512, 128), 512)],
        stage.at[own_rows, pl.ds(pl.multiple_of(c * TILE, 128), 512)],
        partner, r_swap,
    )

    loads[1].wait()
    loads[2].wait()
    lane = lax.broadcasted_iota(jnp.int32, (COLS, 128), 1)
    pad = jnp.zeros((32 - COLS, 128), F32)
    for pair in range(8):
        s_tile = ws[:, pair * 128:(pair + 1) * 128].astype(F32)
        n_tile = wn[:, pair * 128:(pair + 1) * 128].astype(F32)
        low = jnp.where(lane < 64, s_tile, pltpu.roll(n_tile, 64, 1))
        high = jnp.where(lane < 64, pltpu.roll(s_tile, 64, 1), n_tile)
        wsend[2 * pair] = jnp.concatenate([low, pad], 0).astype(BF16)
        wsend[2 * pair + 1] = jnp.concatenate([high, pad], 0).astype(BF16)

    r_w1 = slot(1, 4)
    for step in range(1, 4):
        chip = w_dst_y * 4 + mod4(zh + step)
        copy(wsend.at[chip], wg.at[c, p], device(g, chip, c), r_w1 + step)
    chip0 = w_dst_y * 4 + zh
    w_zero = remote(wsend.at[chip0], wg.at[c, p], device(g, chip0, c), slot(0), r_w1)

    @pl.when(x != 0)
    def _():
        w_zero.start()

    @pl.when(x == 0)
    def _():
        wg[c, p] = wsend[chip0]

    def block(by, bz, part):
        rows = pl.ds(pl.multiple_of((mod4(bz) * 4 + mod4(by)) * PAIR, 16), PAIR)
        start = {"all": 0, "a": other * PART_B, "b": c * PART_A}[part]
        width = {"all": HALF, "a": PART_A, "b": PART_B}[part]
        return xg.at[rows, pl.ds(pl.multiple_of(c * HALF + start, 128), width)]

    r_pair = slot(1, 4)

    def forward(by, bz, part, target, recv):
        view = block(by, bz, part)
        copy(view, view, target, recv)

    def share(by, bz, part):
        forward(by, bz, part, partner, r_pair + mod4(bz))

    r_z1 = slot(1, 4)
    r_z2 = slot(1, 2)
    r_y1 = slot(1, 12)
    r_y2 = slot(1, 6)
    r_y3 = slot(1, 6)

    await_bytes(stage.at[other_rows, pl.ds(pl.multiple_of(other * TILE, 128), 512)], r_swap)
    block(y, zh, "a")[...] = stage[:, pl.ds(pl.multiple_of(other * PART_B, 128), PART_A)].astype(BF16)
    forward(y, zh, "a", z_fwd, r_z1)
    forward(y, zh, "a", z_bwd, r_z1 + 3)

    @pl.when(jnp.logical_and(c == 0, g > 0))
    def _():
        await_bytes(stage.at[0:COLS, 0:TILE], r_left)
        await_bytes(stage.at[COLS:PAIR, 0:TILE], r_left + 1)

    @pl.when(jnp.logical_and(c == 1, g < 15))
    def _():
        await_bytes(stage.at[0:COLS, 512:HALF], r_right)
        await_bytes(stage.at[COLS:PAIR, 512:HALF], r_right + 1)

    block(y, zh, "b")[...] = stage[:, pl.ds(pl.multiple_of(c * PART_A, 128), PART_B)].astype(BF16)
    forward(y, zh, "b", z_bwd, r_z1 + 1)
    forward(y, zh, "b", z_fwd, r_z1 + 2)

    def column(number):
        return zh + sign * (0, -1, 1)[number]

    def send_y1(number, part):
        first = r_y1 + 4 * number + (0 if part == "a" else 2)
        forward(y, column(number), part, y_fwd, first)
        forward(y, column(number), part, y_bwd, first + 1)

    def take_y1(number):
        bz = column(number)
        first = r_y1 + 4 * number
        await_bytes(block(y - sign, bz, "a"), first)
        forward(y - sign, bz, "a", y_fwd, r_y2 + 2 * number)
        await_bytes(block(y + sign, bz, "b"), first + 3)
        forward(y + sign, bz, "b", y_bwd, r_y2 + 2 * number + 1)
        await_bytes(block(y - sign, bz, "b"), first + 2)
        share(y - sign, bz, "all")
        await_bytes(block(y + sign, bz, "a"), first + 1)
        share(y + sign, bz, "all")

    def take_y2(number):
        bz = column(number)
        await_bytes(block(y + 2, bz, "a"), r_y2 + 2 * number)
        share(y + 2, bz, "a")
        await_bytes(block(y + 2, bz, "b"), r_y2 + 2 * number + 1)
        share(y + 2, bz, "b")

    def send_y3(part):
        first = r_y3 + (0 if part == "a" else 3)
        forward(y, zh + 2, part, y_fwd, first)
        forward(y, zh + 2, part, y_bwd, first + 1)
        forward(y, zh + 2, part, y_far, first + 2)
        share(y, zh + 2, part)

    def take_y3(part):
        first = r_y3 + (0 if part == "a" else 3)
        for offset, by in enumerate((y - sign, y + sign, y + 2)):
            await_bytes(block(by, zh + 2, part), first + offset)
            share(by, zh + 2, part)

    send_y1(0, "a")
    send_y1(0, "b")
    share(y, zh, "all")

    for load in loads[3:6]:
        load.wait()
    for tile in range(8):
        dense = adj[tile].astype(F32)
        padded = jnp.concatenate([dense, jnp.zeros((TILE, TILE), F32)], 1)
        moved = pltpu.roll(padded, off[tile] - tile * TILE, 1)
        band[tile] = (moved * live[tile].astype(F32)).astype(BF16)

    for step in range(1, 4):
        await_bytes(wg.at[c, w_src_y * 4 + mod4(zh + step)], r_w1 + 4 - step)

    @pl.when(x != 0)
    def _():
        await_bytes(wg.at[c, w_src_y * 4 + zh], r_w1)

    r_w2 = slot(1, 4)
    part_w = wg.at[c, pl.ds(w_src_y * 4, 4)]
    for step in range(1, 4):
        copy(part_w, part_w, device(g - x + mod4(x + step), p, c), r_w2 + step)

    take_y1(0)

    for step in range(1, 4):
        await_bytes(wg.at[c, pl.ds(mod4(y + x - step) * 4, 4)], r_w2 + step)
    r_w3 = slot(1)
    copy(wg.at[c], wg.at[c], partner, r_w3)
    take_y2(0)

    await_bytes(block(y, zh - sign, "a"), r_z1)
    forward(y, zh - sign, "a", z_fwd, r_z2)
    send_y1(1, "a")
    await_bytes(block(y, zh + sign, "a"), r_z1 + 3)
    send_y1(2, "a")
    await_bytes(block(y, zh + sign, "b"), r_z1 + 1)
    forward(y, zh + sign, "b", z_bwd, r_z2 + 1)
    send_y1(2, "b")
    await_bytes(block(y, zh - sign, "b"), r_z1 + 2)
    send_y1(1, "b")
    share(y, zh - sign, "all")
    share(y, zh + sign, "all")

    await_bytes(wg.at[other], r_w3)
    for col in range(4):
        rows = []
        for row in range(4):
            for core in range(2):
                rows.append(wg[core, row * 4 + col].astype(F32)[0:COLS])
        wt[col] = jnp.concatenate(rows, 0).T.astype(BF16)

    loads[6].wait()
    spot = lax.broadcasted_iota(jnp.int32, (32, 1024), 1)
    row = lax.broadcasted_iota(jnp.int32, (32, 1024), 0)
    bias_own = jnp.sum(
        jnp.where(spot == row + f * 32, jnp.broadcast_to(bias[...], (32, 1024)), 0.0),
        axis=1, keepdims=True,
    )
    pre_acc[...] = jnp.broadcast_to(bias_own, (32, 1024))

    def compute(bz):
        col = mod4(bz)
        rows = pl.ds(pl.multiple_of(col * COLUMN, 16), COLUMN)
        await_bytes(xg.at[rows, pl.ds(pl.multiple_of(other * HALF, 128), HALF)], r_pair + col)
        for tile in range(8):
            nb[rows, tile * TILE:(tile + 1) * TILE] = lax.dot_general(
                xg[rows, tile * TILE:tile * TILE + 3 * TILE], band[tile],
                (((1,), (1,)), ((), ())), preferred_element_type=F32,
            ).astype(BF16)
        ws_t = wt[col, pl.ds(pl.multiple_of(c * 32, 16), 32), :]
        wn_t = wt[col, pl.ds(pl.multiple_of(64 + c * 32, 16), 32), :]
        pre_acc[...] += (
            jnp.dot(ws_t, xg[rows, TILE:TILE + 1024], preferred_element_type=F32)
            + jnp.dot(wn_t, nb[rows, :], preferred_element_type=F32)
        )

    compute(zh)
    take_y1(1)
    take_y1(2)
    await_bytes(block(y, zh + 2, "a"), r_z2)
    send_y3("a")
    await_bytes(block(y, zh + 2, "b"), r_z2 + 1)
    send_y3("b")
    take_y2(2)
    take_y2(1)
    compute(zh - 1)
    compute(zh + 1)
    take_y3("a")
    take_y3("b")
    compute(zh + 2)

    loads[7].wait()
    pre = pre_acc[...]
    gate = jax.nn.sigmoid(pre)
    act = pre * gate
    hid[...] = act.astype(BF16)
    delta = (act - tgt[...].astype(F32)) * (gate * (1.0 + pre * (1.0 - gate))) * (1.0 / 128.0)

    head = delta.astype(BF16)
    rest = (delta - head.astype(F32)).astype(BF16)
    both = jnp.concatenate([head] * 4 + [rest] * 4, 0)
    turn = (((1,), (1,)), ((), ()))
    bias_term = jnp.sum(delta, axis=1, keepdims=True)
    quarter = lax.div(lax.broadcasted_iota(jnp.int32, (PAIR, 128), 1), 32)
    blank = jnp.zeros((16, 128), F32)

    def with_bias(tile, low_total, high_total):
        lane_of = lax.broadcasted_iota(jnp.int32, tile.shape, 1)
        bias_sum = jnp.where(lane_of < 64, low_total, high_total)
        first = bias_sum.astype(BF16).astype(F32)
        tile = jnp.where(lax.rem(lane_of, 64) == 48, first, tile)
        return jnp.where(lax.rem(lane_of, 64) == 49, bias_sum - first, tile)

    r_ra = slot(1, 4)
    terms = []
    for row in range(4):
        spans = [slice((col * 4 + row) * PAIR, (col * 4 + row + 1) * PAIR) for col in range(4)]
        left = jnp.concatenate(
            [xg[span, TILE:TILE + 1024] for span in spans] + [nb[span, :] for span in spans], 0
        )
        grad = lax.dot_general(left, both, turn, preferred_element_type=F32)
        grad = grad[:, 0:128] + grad[:, 128:256]

        def packed(first):
            parts = [grad[first + col * PAIR:first + (col + 1) * PAIR] for col in range(4)]
            low = jnp.where(quarter == 0, parts[0], parts[1])
            high = jnp.where(quarter == 2, parts[2], parts[3])
            return jnp.where(quarter < 2, low, high)

        own_term, nb_term = packed(0), packed(COLUMN)
        turned = jnp.concatenate(
            [own_term[0:COLS], nb_term[0:COLS], blank, own_term[COLS:PAIR], nb_term[COLS:PAIR], blank], 0
        ).T
        for col in range(4):
            tile = with_bias(turned[col * 32:(col + 1) * 32], bias_term, bias_term)
            rsend[row, col] = tile.astype(BF16)
        terms.append(remote(rsend.at[row], ra.at[x], device(g - x + row, p, c), slot(0), r_ra + x))
        start_unless(x == row, terms[row])

    for step in range(1, 4):
        from_x = mod4(x + step)
        await_bytes(ra.at[from_x], r_ra + from_x)
    xs = [mod4(x + step) for step in range(1, 4)]
    halves = lax.broadcasted_iota(jnp.int32, (16, 128), 1) < 64
    for col in range(4):
        summed = (rsend[x, col].astype(F32) + ra[xs[0], col].astype(F32)) + (
            ra[xs[1], col].astype(F32) + ra[xs[2], col].astype(F32)
        )
        bias_sum = summed[:, 48:49] + summed[:, 49:50]
        summed = with_bias(summed, bias_sum, bias_sum)
        top, bottom = summed[0:16], summed[16:32]
        rbs[col, 0] = jnp.where(halves, top, pltpu.roll(bottom, 64, 1)).astype(BF16)
        rbs[col, 1] = jnp.where(halves, pltpu.roll(top, 64, 1), bottom).astype(BF16)

    r_rb = slot(1)
    to_group = zh * 4 + mod4(y + x)
    for step in range(1, 4):
        col = mod4(zh + step)
        for core in range(2):
            copy(rbs.at[col, core], rb.at[zl, c], device(to_group, x * 4 + col, core), r_rb)
    copy(rbs.at[zh, other], rb.at[zl, c], device(to_group, x * 4 + zh, other), r_rb)
    r_zero = remote(rbs.at[zh, c], rb.at[zl, c], device(to_group, x * 4 + zh, c), slot(0), r_rb)
    start_unless(stays, r_zero)

    @pl.when(stays)
    def _():
        pltpu.make_async_copy(rbs.at[zh, c], rb.at[zl, c], recv_sem.at[r_rb]).start()

    await_bytes(rb, r_rb)
    for core in range(2):
        total = (rb[0, core].astype(F32) + rb[1, core].astype(F32)) + (
            rb[2, core].astype(F32) + rb[3, core].astype(F32)
        )
        fg[r_chip, core] = with_bias(
            total, total[:, 48:49] + total[:, 49:50], total[:, 112:113] + total[:, 113:114]
        ).astype(BF16)

    r_r2 = slot(1)
    for step in range(1, 16):
        copy(fg.at[r_chip], fg.at[r_chip], device(lax.rem(g + step, 16), p, c), r_r2)
    await_bytes(fg.at[0:15], r_r2)
    for part in range(8):
        rows = []
        for chip in (2 * part, 2 * part + 1):
            for core in range(2):
                tile = fg[chip, core].astype(F32)
                rows += [tile, pltpu.roll(tile, 64, 1)]
        turned = jnp.concatenate(rows, 0).T
        span = slice(part * 128, (part + 1) * 128)
        gs_o[:, span] = turned[0:24]
        gn_o[:, span] = turned[24:48]
        gb_o[:, span] = turned[48:49] + turned[49:50]

    for made in sent:
        made.wait_send()

    @pl.when(g < 15)
    def _():
        halo_up.wait_send()

    @pl.when(g > 0)
    def _():
        halo_down.wait_send()

    @pl.when(x != 0)
    def _():
        w_zero.wait_send()

    @pl.when(jnp.logical_not(stays))
    def _():
        r_zero.wait_send()

    for row in range(4):
        @pl.when(x != row)
        def _():
            terms[row].wait_send()

    assert used[0] <= SENDS and used[1] <= RECVS, used


OUTS = (
    jax.ShapeDtypeStruct((32, 1024), BF16),
    jax.ShapeDtypeStruct((COLS, 1024), F32),
    jax.ShapeDtypeStruct((COLS, 1024), F32),
    jax.ShapeDtypeStruct((1, 1024), F32),
)


def place(hid, gs, gn, gb, hid_o, gs_o, gn_o, gb_o, sem):
    pairs = [(hid, hid_o), (gs, gs_o), (gn, gn_o), (gb, gb_o)]
    moves = [pltpu.make_async_copy(src, dst, sem.at[i]) for i, (src, dst) in enumerate(pairs)]
    for move in moves:
        move.start()
    for move in moves:
        move.wait()


def shards(features, adjacency, offsets, live, w_self, w_neigh, bias, targets):
    vmem = pl.BlockSpec(memory_space=pltpu.VMEM)
    hbm = pl.BlockSpec(memory_space=pltpu.HBM)
    inputs = [features.T, adjacency, offsets, live, w_self, w_neigh, bias.reshape(1, 1024), targets]
    results = pl.pallas_call(
        kernel,
        out_shape=OUTS,
        in_specs=[hbm] * 8,
        out_specs=(vmem,) * 4,
        scratch_shapes=[
            pltpu.VMEM((COLS, 1024), BF16),
            pltpu.VMEM((8, TILE, 256), BF16),
            pltpu.SMEM((8,), jnp.int32),
            pltpu.SMEM((8,), jnp.int32),
            pltpu.VMEM((COLS, 1024), BF16),
            pltpu.VMEM((COLS, 1024), BF16),
            pltpu.VMEM((1, 1024), F32),
            pltpu.VMEM((32, 1024), BF16),
            pltpu.VMEM((COLS, 1024), F32),
            pltpu.VMEM((PAIR, HALF), F32),
            pltpu.VMEM((768, 1280), BF16),
            pltpu.VMEM((768, 1024), BF16),
            pltpu.VMEM((8, TILE, 384), BF16),
            pltpu.VMEM((16, 32, 128), BF16),
            pltpu.VMEM((2, 16, 32, 128), BF16),
            pltpu.VMEM((4, 128, COLUMN), BF16),
            pltpu.VMEM((32, 1024), F32),
            pltpu.VMEM((4, 4, 32, 128), BF16),
            pltpu.VMEM((4, 4, 32, 128), BF16),
            pltpu.VMEM((4, 2, 16, 128), BF16),
            pltpu.VMEM((4, 2, 16, 128), BF16),
            pltpu.VMEM((16, 2, 16, 128), BF16),
            pltpu.SemaphoreType.DMA((8,)),
            pltpu.SemaphoreType.DMA((SENDS,)),
            pltpu.SemaphoreType.DMA((RECVS,)),
        ],
        compiler_params=pltpu.CompilerParams(
            collective_id=0, has_side_effects=True, vmem_limit_bytes=48 * 1024 * 1024
        ),
        cost_estimate=pl.CostEstimate(flops=10**9, bytes_accessed=10**7, transcendentals=32768),
    )(*[pltpu.with_memory_space_constraint(array, pltpu.HBM) for array in inputs])
    hidden, grad_self, grad_neigh, grad_bias = pl.pallas_call(
        place,
        out_shape=OUTS,
        in_specs=[vmem] * 4,
        out_specs=(pl.BlockSpec(memory_space=pl.ANY),) * 4,
        scratch_shapes=[pltpu.SemaphoreType.DMA((4,))],
        compiler_params=pltpu.CompilerParams(vmem_limit_bytes=1024 * 1024),
    )(*[pltpu.with_memory_space_constraint(array, pltpu.VMEM) for array in results])
    return hidden, grad_self, grad_neigh, grad_bias.reshape(1024)


def solution(mesh):
    in_specs = (
        P("grp", "feat"),
        P("grp", None, None),
        P("grp"),
        P("grp"),
        P("feat", None),
        P("feat", None),
        P(),
        P("feat", "grp"),
    )
    out_specs = (P("feat", "grp"), P("feat", None), P("feat", None), P())
    return jax.shard_map(shards, mesh=mesh, in_specs=in_specs, out_specs=out_specs, check_vma=False)
```

```python
import jax
import jax.numpy as jnp
from jax import lax
from jax.experimental import pallas as pl
from jax.experimental.pallas import tpu as pltpu
from jax.sharding import PartitionSpec as P

F32 = jnp.float32
BF16 = jnp.bfloat16
MESH = pl.DeviceIdType.MESH

COLS = 24
PAIR = 48
COLUMN = 4 * PAIR
HALF = 640
PART_A = 384
PART_B = HALF - PART_A
TILE = 128
SENDS = 96
RECVS = 72


def mod4(value):
    return lax.rem(value + 4, 4)


def kernel(
    feat_h, adj_h, off_h, live_h, ws_h, wn_h, bias_h, tgt_h,
    hid, gs_o, gn_o, gb_o,
    feat, adj, off, live, ws, wn, bias, tgt,
    wide, stage, xg, nb, band, wsend, wg, wt, pre_acc, rsend, ra, rbs, rb, fg,
    in_sem, send_sem, recv_sem,
):
    loads = [
        pltpu.make_async_copy(src, dst, in_sem.at[i])
        for i, (src, dst) in enumerate(
            [(feat_h, feat), (ws_h, ws), (wn_h, wn), (adj_h, adj), (off_h, off), (live_h, live),
             (bias_h, bias), (tgt_h, tgt)]
        )
    ]
    for load in loads:
        load.start()

    g = lax.axis_index("grp")
    f = lax.axis_index("feat")
    c = lax.rem(f, 2)
    p = lax.div(f, 2)
    y = lax.div(p, 4)
    zh = lax.rem(p, 4)
    x = lax.rem(g, 4)
    zl = lax.div(g, 4)
    other = 1 - c
    sign = 1 - 2 * c

    def device(group, chip, core):
        return (group, chip * 2 + core)

    partner = device(g, p, other)
    y_fwd = device(g, mod4(y + sign) * 4 + zh, c)
    y_bwd = device(g, mod4(y - sign) * 4 + zh, c)
    y_far = device(g, mod4(y + 2) * 4 + zh, c)
    z_fwd = device(g, y * 4 + mod4(zh + sign), c)
    z_bwd = device(g, y * 4 + mod4(zh - sign), c)
    stays = jnp.logical_and(zh == zl, jnp.logical_and(x == 0, y == 0))

    barrier = pltpu.get_barrier_semaphore()

    def tell(target):
        pl.semaphore_signal(barrier, inc=1, device_id=target, device_id_type=MESH)

    @pl.when(jnp.logical_and(c == 0, g > 0))
    def _():
        tell(device(g - 1, p, 0))
        tell(device(g - 1, p, 1))

    @pl.when(jnp.logical_and(c == 1, g < 15))
    def _():
        tell(device(g + 1, p, 0))
        tell(device(g + 1, p, 1))

    for target in (z_fwd, z_bwd, y_fwd, y_bwd, y_far, partner):
        tell(target)

    w_src_y = mod4(y + x)
    w_dst_y = mod4(y - x)
    r_chip = mod4(x - y) * 4 + zl
    for step in range(1, 4):
        tell(device(g, w_src_y * 4 + mod4(zh + step), c))
        tell(device(mod4(zl + step) * 4 + y, r_chip, 0))
        tell(device(mod4(zl + step) * 4 + y, r_chip, 1))

    @pl.when(x != 0)
    def _():
        tell(device(g, w_src_y * 4 + zh, c))

    tell(device(zl * 4 + y, r_chip, other))

    @pl.when(jnp.logical_not(stays))
    def _():
        tell(device(zl * 4 + y, r_chip, c))

    def tell_far(step, carry):
        tell(device(lax.rem(g + step, 16), p, c))
        return carry

    lax.fori_loop(1, 16, tell_far, 0)

    loads[0].wait()
    wide[...] = feat[...].astype(F32)

    @pl.when(c == 0)
    def _():
        stage[0:COLS, TILE:HALF] = wide[:, 0:512]

        @pl.when(g == 0)
        def _():
            stage[:, 0:TILE] = jnp.zeros((PAIR, TILE), F32)

    @pl.when(c == 1)
    def _():
        stage[COLS:PAIR, 0:512] = wide[:, 512:1024]

        @pl.when(g == 15)
        def _():
            stage[:, 512:HALF] = jnp.zeros((PAIR, TILE), F32)

    waits = (
        6 + 3 + 7 + 15
        + (x != 0).astype(jnp.int32)
        + jnp.logical_not(stays).astype(jnp.int32)
        + (g < 15).astype(jnp.int32)
        + (g > 0).astype(jnp.int32)
    )
    pl.semaphore_wait(barrier, waits)

    used = [0, 0]
    sent = []

    def slot(which, count=1):
        used[which] += count
        return used[which] - count

    def remote(src, dst, target, send, recv):
        return pltpu.make_async_remote_copy(
            src_ref=src, dst_ref=dst, send_sem=send_sem.at[send], recv_sem=recv_sem.at[recv],
            device_id=target, device_id_type=MESH,
        )

    def copy(src, dst, target, recv):
        made = remote(src, dst, target, slot(0), recv)
        made.start()
        sent.append(made)

    def start_unless(skip, made):
        @pl.when(jnp.logical_not(skip))
        def _():
            made.start()

    def await_bytes(ref, recv):
        pltpu.make_async_copy(ref, ref, recv_sem.at[recv]).wait()

    own_rows = pl.ds(pl.multiple_of(c * COLS, 8), COLS)
    other_rows = pl.ds(pl.multiple_of(other * COLS, 8), COLS)
    r_left, r_right, r_swap = slot(1, 2), slot(1, 2), slot(1)
    halo_up = remote(
        wide.at[:, 896:1024], stage.at[own_rows, 0:TILE], device(g + 1, p, 0), slot(0), r_left + c
    )
    halo_down = remote(
        wide.at[:, 0:TILE], stage.at[own_rows, 512:HALF], device(g - 1, p, 1), slot(0), r_right + c
    )

    @pl.when(g < 15)
    def _():
        halo_up.start()

    @pl.when(g > 0)
    def _():
        halo_down.start()

    copy(
        wide.at[:, pl.ds(pl.multiple_of(other * 512, 128), 512)],
        stage.at[own_rows, pl.ds(pl.multiple_of(c * TILE, 128), 512)],
        partner, r_swap,
    )

    loads[1].wait()
    loads[2].wait()
    lane = lax.broadcasted_iota(jnp.int32, (COLS, 128), 1)
    pad = jnp.zeros((32 - COLS, 128), F32)
    for pair in range(8):
        s_tile = ws[:, pair * 128:(pair + 1) * 128].astype(F32)
        n_tile = wn[:, pair * 128:(pair + 1) * 128].astype(F32)
        low = jnp.where(lane < 64, s_tile, pltpu.roll(n_tile, 64, 1))
        high = jnp.where(lane < 64, pltpu.roll(s_tile, 64, 1), n_tile)
        wsend[2 * pair] = jnp.concatenate([low, pad], 0).astype(BF16)
        wsend[2 * pair + 1] = jnp.concatenate([high, pad], 0).astype(BF16)

    r_w1 = slot(1, 4)
    for step in range(1, 4):
        chip = w_dst_y * 4 + mod4(zh + step)
        copy(wsend.at[chip], wg.at[c, p], device(g, chip, c), r_w1 + step)
    chip0 = w_dst_y * 4 + zh
    w_zero = remote(wsend.at[chip0], wg.at[c, p], device(g, chip0, c), slot(0), r_w1)

    @pl.when(x != 0)
    def _():
        w_zero.start()

    @pl.when(x == 0)
    def _():
        wg[c, p] = wsend[chip0]

    def block(by, bz, part):
        rows = pl.ds(pl.multiple_of((mod4(bz) * 4 + mod4(by)) * PAIR, 16), PAIR)
        start = {"all": 0, "a": other * PART_B, "b": c * PART_A}[part]
        width = {"all": HALF, "a": PART_A, "b": PART_B}[part]
        return xg.at[rows, pl.ds(pl.multiple_of(c * HALF + start, 128), width)]

    r_pair = slot(1, 4)

    def forward(by, bz, part, target, recv):
        view = block(by, bz, part)
        copy(view, view, target, recv)

    def share(by, bz, part):
        forward(by, bz, part, partner, r_pair + mod4(bz))

    r_z1 = slot(1, 4)
    r_z2 = slot(1, 2)
    r_y1 = slot(1, 12)
    r_y2 = slot(1, 6)
    r_y3 = slot(1, 6)

    await_bytes(stage.at[other_rows, pl.ds(pl.multiple_of(other * TILE, 128), 512)], r_swap)
    block(y, zh, "a")[...] = stage[:, pl.ds(pl.multiple_of(other * PART_B, 128), PART_A)].astype(BF16)
    forward(y, zh, "a", z_fwd, r_z1)
    forward(y, zh, "a", z_bwd, r_z1 + 3)

    @pl.when(jnp.logical_and(c == 0, g > 0))
    def _():
        await_bytes(stage.at[0:COLS, 0:TILE], r_left)
        await_bytes(stage.at[COLS:PAIR, 0:TILE], r_left + 1)

    @pl.when(jnp.logical_and(c == 1, g < 15))
    def _():
        await_bytes(stage.at[0:COLS, 512:HALF], r_right)
        await_bytes(stage.at[COLS:PAIR, 512:HALF], r_right + 1)

    block(y, zh, "b")[...] = stage[:, pl.ds(pl.multiple_of(c * PART_A, 128), PART_B)].astype(BF16)
    forward(y, zh, "b", z_bwd, r_z1 + 1)
    forward(y, zh, "b", z_fwd, r_z1 + 2)

    def column(number):
        return zh + sign * (0, -1, 1)[number]

    def send_y1(number, part):
        first = r_y1 + 4 * number + (0 if part == "a" else 2)
        forward(y, column(number), part, y_fwd, first)
        forward(y, column(number), part, y_bwd, first + 1)

    def take_y1(number):
        bz = column(number)
        first = r_y1 + 4 * number
        await_bytes(block(y - sign, bz, "a"), first)
        forward(y - sign, bz, "a", y_fwd, r_y2 + 2 * number)
        await_bytes(block(y + sign, bz, "b"), first + 3)
        forward(y + sign, bz, "b", y_bwd, r_y2 + 2 * number + 1)
        await_bytes(block(y - sign, bz, "b"), first + 2)
        share(y - sign, bz, "all")
        await_bytes(block(y + sign, bz, "a"), first + 1)
        share(y + sign, bz, "all")

    def take_y2(number):
        bz = column(number)
        await_bytes(block(y + 2, bz, "a"), r_y2 + 2 * number)
        share(y + 2, bz, "a")
        await_bytes(block(y + 2, bz, "b"), r_y2 + 2 * number + 1)
        share(y + 2, bz, "b")

    def send_y3(part):
        first = r_y3 + (0 if part == "a" else 3)
        forward(y, zh + 2, part, y_fwd, first)
        forward(y, zh + 2, part, y_bwd, first + 1)
        forward(y, zh + 2, part, y_far, first + 2)
        share(y, zh + 2, part)

    def take_y3(part):
        first = r_y3 + (0 if part == "a" else 3)
        for offset, by in enumerate((y - sign, y + sign, y + 2)):
            await_bytes(block(by, zh + 2, part), first + offset)
            share(by, zh + 2, part)

    send_y1(0, "a")
    send_y1(0, "b")
    share(y, zh, "all")

    for load in loads[3:6]:
        load.wait()
    for tile in range(8):
        dense = adj[tile].astype(F32)
        padded = jnp.concatenate([dense, jnp.zeros((TILE, TILE), F32)], 1)
        moved = pltpu.roll(padded, off[tile] - tile * TILE, 1)
        band[tile] = (moved * live[tile].astype(F32)).astype(BF16)

    def neighbours(bz):
        col = mod4(bz)
        rows = pl.ds(pl.multiple_of(col * COLUMN, 16), COLUMN)
        await_bytes(xg.at[rows, pl.ds(pl.multiple_of(other * HALF, 128), HALF)], r_pair + col)
        for tile in range(8):
            nb[rows, tile * TILE:(tile + 1) * TILE] = lax.dot_general(
                xg[rows, tile * TILE:tile * TILE + 3 * TILE], band[tile],
                (((1,), (1,)), ((), ())), preferred_element_type=F32,
            ).astype(BF16)

    def products(bz):
        col = mod4(bz)
        rows = pl.ds(pl.multiple_of(col * COLUMN, 16), COLUMN)
        ws_t = wt[col, pl.ds(pl.multiple_of(c * 32, 16), 32), :]
        wn_t = wt[col, pl.ds(pl.multiple_of(64 + c * 32, 16), 32), :]
        pre_acc[...] += (
            jnp.dot(ws_t, xg[rows, TILE:TILE + 1024], preferred_element_type=F32)
            + jnp.dot(wn_t, nb[rows, :], preferred_element_type=F32)
        )

    take_y1(0)

    await_bytes(block(y, zh - sign, "a"), r_z1)
    forward(y, zh - sign, "a", z_fwd, r_z2)
    send_y1(1, "a")
    await_bytes(block(y, zh + sign, "a"), r_z1 + 3)
    send_y1(2, "a")

    for step in range(1, 4):
        await_bytes(wg.at[c, w_src_y * 4 + mod4(zh + step)], r_w1 + 4 - step)

    @pl.when(x != 0)
    def _():
        await_bytes(wg.at[c, w_src_y * 4 + zh], r_w1)

    r_w2 = slot(1, 4)
    part_w = wg.at[c, pl.ds(w_src_y * 4, 4)]
    for step in range(1, 4):
        copy(part_w, part_w, device(g - x + mod4(x + step), p, c), r_w2 + step)

    take_y2(0)
    await_bytes(block(y, zh + sign, "b"), r_z1 + 1)
    forward(y, zh + sign, "b", z_bwd, r_z2 + 1)
    send_y1(2, "b")
    await_bytes(block(y, zh - sign, "b"), r_z1 + 2)
    send_y1(1, "b")
    share(y, zh - sign, "all")
    share(y, zh + sign, "all")
    neighbours(zh)
    for step in range(1, 4):
        await_bytes(wg.at[c, pl.ds(mod4(y + x - step) * 4, 4)], r_w2 + step)
    r_w3 = slot(1)
    copy(wg.at[c], wg.at[c], partner, r_w3)
    take_y1(1)
    take_y1(2)
    await_bytes(block(y, zh + 2, "a"), r_z2)
    send_y3("a")
    await_bytes(block(y, zh + 2, "b"), r_z2 + 1)
    send_y3("b")
    take_y2(2)
    take_y2(1)

    await_bytes(wg.at[other], r_w3)
    for col in range(4):
        rows = []
        for row in range(4):
            for core in range(2):
                rows.append(wg[core, row * 4 + col].astype(F32)[0:COLS])
        wt[col] = jnp.concatenate(rows, 0).T.astype(BF16)
    loads[6].wait()
    spot = lax.broadcasted_iota(jnp.int32, (32, 1024), 1)
    row = lax.broadcasted_iota(jnp.int32, (32, 1024), 0)
    bias_own = jnp.sum(
        jnp.where(spot == row + f * 32, jnp.broadcast_to(bias[...], (32, 1024)), 0.0),
        axis=1, keepdims=True,
    )
    pre_acc[...] = jnp.broadcast_to(bias_own, (32, 1024))
    products(zh)
    neighbours(zh - 1)
    neighbours(zh + 1)
    products(zh - 1)
    products(zh + 1)
    take_y3("a")
    take_y3("b")
    neighbours(zh + 2)
    products(zh + 2)

    loads[7].wait()
    pre = pre_acc[...]
    gate = jax.nn.sigmoid(pre)
    act = pre * gate
    hid[...] = act.astype(BF16)
    delta = (act - tgt[...].astype(F32)) * (gate * (1.0 + pre * (1.0 - gate))) * (1.0 / 128.0)

    head = delta.astype(BF16)
    rest = (delta - head.astype(F32)).astype(BF16)
    both = jnp.concatenate([head] * 4 + [rest] * 4, 0)
    turn = (((1,), (1,)), ((), ()))
    bias_term = jnp.sum(delta, axis=1, keepdims=True)
    quarter = lax.div(lax.broadcasted_iota(jnp.int32, (PAIR, 128), 1), 32)
    blank = jnp.zeros((16, 128), F32)

    def with_bias(tile, low_total, high_total):
        lane_of = lax.broadcasted_iota(jnp.int32, tile.shape, 1)
        bias_sum = jnp.where(lane_of < 64, low_total, high_total)
        first = bias_sum.astype(BF16).astype(F32)
        tile = jnp.where(lax.rem(lane_of, 64) == 48, first, tile)
        return jnp.where(lax.rem(lane_of, 64) == 49, bias_sum - first, tile)

    r_ra = slot(1, 4)
    terms = []
    for row in range(4):
        spans = [slice((col * 4 + row) * PAIR, (col * 4 + row + 1) * PAIR) for col in range(4)]
        left = jnp.concatenate(
            [xg[span, TILE:TILE + 1024] for span in spans] + [nb[span, :] for span in spans], 0
        )
        grad = lax.dot_general(left, both, turn, preferred_element_type=F32)
        grad = grad[:, 0:128] + grad[:, 128:256]

        def packed(first):
            parts = [grad[first + col * PAIR:first + (col + 1) * PAIR] for col in range(4)]
            low = jnp.where(quarter == 0, parts[0], parts[1])
            high = jnp.where(quarter == 2, parts[2], parts[3])
            return jnp.where(quarter < 2, low, high)

        own_term, nb_term = packed(0), packed(COLUMN)
        turned = jnp.concatenate(
            [own_term[0:COLS], nb_term[0:COLS], blank, own_term[COLS:PAIR], nb_term[COLS:PAIR], blank], 0
        ).T
        for col in range(4):
            tile = with_bias(turned[col * 32:(col + 1) * 32], bias_term, bias_term)
            rsend[row, col] = tile.astype(BF16)
        terms.append(remote(rsend.at[row], ra.at[x], device(g - x + row, p, c), slot(0), r_ra + x))
        start_unless(x == row, terms[row])

    for step in range(1, 4):
        from_x = mod4(x + step)
        await_bytes(ra.at[from_x], r_ra + from_x)
    xs = [mod4(x + step) for step in range(1, 4)]
    halves = lax.broadcasted_iota(jnp.int32, (16, 128), 1) < 64
    for col in range(4):
        summed = (rsend[x, col].astype(F32) + ra[xs[0], col].astype(F32)) + (
            ra[xs[1], col].astype(F32) + ra[xs[2], col].astype(F32)
        )
        bias_sum = summed[:, 48:49] + summed[:, 49:50]
        summed = with_bias(summed, bias_sum, bias_sum)
        top, bottom = summed[0:16], summed[16:32]
        rbs[col, 0] = jnp.where(halves, top, pltpu.roll(bottom, 64, 1)).astype(BF16)
        rbs[col, 1] = jnp.where(halves, pltpu.roll(top, 64, 1), bottom).astype(BF16)

    r_rb = slot(1)
    to_group = zh * 4 + mod4(y + x)
    for step in range(1, 4):
        col = mod4(zh + step)
        for core in range(2):
            copy(rbs.at[col, core], rb.at[zl, c], device(to_group, x * 4 + col, core), r_rb)
    copy(rbs.at[zh, other], rb.at[zl, c], device(to_group, x * 4 + zh, other), r_rb)
    r_zero = remote(rbs.at[zh, c], rb.at[zl, c], device(to_group, x * 4 + zh, c), slot(0), r_rb)
    start_unless(stays, r_zero)

    @pl.when(stays)
    def _():
        pltpu.make_async_copy(rbs.at[zh, c], rb.at[zl, c], recv_sem.at[r_rb]).start()

    await_bytes(rb, r_rb)
    for core in range(2):
        total = (rb[0, core].astype(F32) + rb[1, core].astype(F32)) + (
            rb[2, core].astype(F32) + rb[3, core].astype(F32)
        )
        fg[r_chip, core] = with_bias(
            total, total[:, 48:49] + total[:, 49:50], total[:, 112:113] + total[:, 113:114]
        ).astype(BF16)

    r_r2 = slot(1)
    for step in range(1, 16):
        copy(fg.at[r_chip], fg.at[r_chip], device(lax.rem(g + step, 16), p, c), r_r2)
    await_bytes(fg.at[0:15], r_r2)
    for part in range(8):
        rows = []
        for chip in (2 * part, 2 * part + 1):
            for core in range(2):
                tile = fg[chip, core].astype(F32)
                rows += [tile, pltpu.roll(tile, 64, 1)]
        turned = jnp.concatenate(rows, 0).T
        span = slice(part * 128, (part + 1) * 128)
        gs_o[:, span] = turned[0:24]
        gn_o[:, span] = turned[24:48]
        gb_o[:, span] = turned[48:49] + turned[49:50]

    for made in sent:
        made.wait_send()

    @pl.when(g < 15)
    def _():
        halo_up.wait_send()

    @pl.when(g > 0)
    def _():
        halo_down.wait_send()

    @pl.when(x != 0)
    def _():
        w_zero.wait_send()

    @pl.when(jnp.logical_not(stays))
    def _():
        r_zero.wait_send()

    for row in range(4):
        @pl.when(x != row)
        def _():
            terms[row].wait_send()

    assert used[0] <= SENDS and used[1] <= RECVS, used


OUTS = (
    jax.ShapeDtypeStruct((32, 1024), BF16),
    jax.ShapeDtypeStruct((COLS, 1024), F32),
    jax.ShapeDtypeStruct((COLS, 1024), F32),
    jax.ShapeDtypeStruct((1, 1024), F32),
)


def place(hid, gs, gn, gb, hid_o, gs_o, gn_o, gb_o, sem):
    pairs = [(hid, hid_o), (gs, gs_o), (gn, gn_o), (gb, gb_o)]
    moves = [pltpu.make_async_copy(src, dst, sem.at[i]) for i, (src, dst) in enumerate(pairs)]
    for move in moves:
        move.start()
    for move in moves:
        move.wait()


def shards(features, adjacency, offsets, live, w_self, w_neigh, bias, targets):
    vmem = pl.BlockSpec(memory_space=pltpu.VMEM)
    hbm = pl.BlockSpec(memory_space=pltpu.HBM)
    inputs = [features.T, adjacency, offsets, live, w_self, w_neigh, bias.reshape(1, 1024), targets]
    results = pl.pallas_call(
        kernel,
        out_shape=OUTS,
        in_specs=[hbm] * 8,
        out_specs=(vmem,) * 4,
        scratch_shapes=[
            pltpu.VMEM((COLS, 1024), BF16),
            pltpu.VMEM((8, TILE, 256), BF16),
            pltpu.SMEM((8,), jnp.int32),
            pltpu.SMEM((8,), jnp.int32),
            pltpu.VMEM((COLS, 1024), BF16),
            pltpu.VMEM((COLS, 1024), BF16),
            pltpu.VMEM((1, 1024), F32),
            pltpu.VMEM((32, 1024), BF16),
            pltpu.VMEM((COLS, 1024), F32),
            pltpu.VMEM((PAIR, HALF), F32),
            pltpu.VMEM((768, 1280), BF16),
            pltpu.VMEM((768, 1024), BF16),
            pltpu.VMEM((8, TILE, 384), BF16),
            pltpu.VMEM((16, 32, 128), BF16),
            pltpu.VMEM((2, 16, 32, 128), BF16),
            pltpu.VMEM((4, 128, COLUMN), BF16),
            pltpu.VMEM((32, 1024), F32),
            pltpu.VMEM((4, 4, 32, 128), BF16),
            pltpu.VMEM((4, 4, 32, 128), BF16),
            pltpu.VMEM((4, 2, 16, 128), BF16),
            pltpu.VMEM((4, 2, 16, 128), BF16),
            pltpu.VMEM((16, 2, 16, 128), BF16),
            pltpu.SemaphoreType.DMA((8,)),
            pltpu.SemaphoreType.DMA((SENDS,)),
            pltpu.SemaphoreType.DMA((RECVS,)),
        ],
        compiler_params=pltpu.CompilerParams(
            collective_id=0, has_side_effects=True, vmem_limit_bytes=48 * 1024 * 1024
        ),
        cost_estimate=pl.CostEstimate(flops=10**9, bytes_accessed=10**7, transcendentals=32768),
    )(*[pltpu.with_memory_space_constraint(array, pltpu.HBM) for array in inputs])
    hidden, grad_self, grad_neigh, grad_bias = pl.pallas_call(
        place,
        out_shape=OUTS,
        in_specs=[vmem] * 4,
        out_specs=(pl.BlockSpec(memory_space=pl.ANY),) * 4,
        scratch_shapes=[pltpu.SemaphoreType.DMA((4,))],
        compiler_params=pltpu.CompilerParams(vmem_limit_bytes=1024 * 1024),
    )(*[pltpu.with_memory_space_constraint(array, pltpu.VMEM) for array in results])
    return hidden, grad_self, grad_neigh, grad_bias.reshape(1024)


def solution(mesh):
    in_specs = (
        P("grp", "feat"),
        P("grp", None, None),
        P("grp"),
        P("grp"),
        P("feat", None),
        P("feat", None),
        P(),
        P("feat", "grp"),
    )
    out_specs = (P("feat", "grp"), P("feat", None), P("feat", None), P())
    return jax.shard_map(shards, mesh=mesh, in_specs=in_specs, out_specs=out_specs, check_vma=False)
```

```python
import jax
import jax.numpy as jnp
from jax import lax
from jax.experimental import pallas as pl
from jax.experimental.pallas import tpu as pltpu
from jax.sharding import PartitionSpec as P

F32 = jnp.float32
BF16 = jnp.bfloat16
MESH = pl.DeviceIdType.MESH

COLS = 24
PAIR = 48
COLUMN = 4 * PAIR
HALF = 640
PART_A = 384
PART_B = HALF - PART_A
TILE = 128
SENDS = 96
RECVS = 72


def mod4(value):
    return lax.rem(value + 4, 4)


def kernel(
    feat_h, adj_h, off_h, live_h, ws_h, wn_h, bias_h, tgt_h,
    hid, gs_o, gn_o, gb_o,
    feat, adj, off, live, ws, wn, bias, tgt,
    wide, stage, xg, nb, band, wsend, wg, wt, pre_acc, rsend, ra, rbs, rb, fg,
    in_sem, send_sem, recv_sem,
):
    loads = [
        pltpu.make_async_copy(src, dst, in_sem.at[i])
        for i, (src, dst) in enumerate(
            [(feat_h, feat), (ws_h, ws), (wn_h, wn), (adj_h, adj), (off_h, off), (live_h, live),
             (bias_h, bias), (tgt_h, tgt)]
        )
    ]
    for load in loads:
        load.start()

    g = lax.axis_index("grp")
    f = lax.axis_index("feat")
    c = lax.rem(f, 2)
    p = lax.div(f, 2)
    y = lax.div(p, 4)
    zh = lax.rem(p, 4)
    x = lax.rem(g, 4)
    zl = lax.div(g, 4)
    other = 1 - c
    sign = 1 - 2 * c

    def device(group, chip, core):
        return (group, chip * 2 + core)

    partner = device(g, p, other)
    y_fwd = device(g, mod4(y + sign) * 4 + zh, c)
    y_bwd = device(g, mod4(y - sign) * 4 + zh, c)
    y_far = device(g, mod4(y + 2) * 4 + zh, c)
    z_fwd = device(g, y * 4 + mod4(zh + sign), c)
    z_bwd = device(g, y * 4 + mod4(zh - sign), c)
    stays = jnp.logical_and(zh == zl, jnp.logical_and(x == 0, y == 0))

    barrier = pltpu.get_barrier_semaphore()

    def tell(target):
        pl.semaphore_signal(barrier, inc=1, device_id=target, device_id_type=MESH)

    @pl.when(jnp.logical_and(c == 0, g > 0))
    def _():
        tell(device(g - 1, p, 0))
        tell(device(g - 1, p, 1))

    @pl.when(jnp.logical_and(c == 1, g < 15))
    def _():
        tell(device(g + 1, p, 0))
        tell(device(g + 1, p, 1))

    for target in (z_fwd, z_bwd, y_fwd, y_bwd, y_far, partner):
        tell(target)

    w_src_y = mod4(y + x)
    w_dst_y = mod4(y - x)
    r_chip = mod4(x - y) * 4 + zl
    for step in range(1, 4):
        tell(device(g, w_src_y * 4 + mod4(zh + step), c))
        tell(device(mod4(zl + step) * 4 + y, r_chip, 0))
        tell(device(mod4(zl + step) * 4 + y, r_chip, 1))

    @pl.when(x != 0)
    def _():
        tell(device(g, w_src_y * 4 + zh, c))

    tell(device(zl * 4 + y, r_chip, other))

    @pl.when(jnp.logical_not(stays))
    def _():
        tell(device(zl * 4 + y, r_chip, c))

    def tell_far(step, carry):
        tell(device(lax.rem(g + step, 16), p, c))
        return carry

    lax.fori_loop(1, 16, tell_far, 0)

    loads[0].wait()
    wide[...] = feat[...].astype(F32)

    @pl.when(c == 0)
    def _():
        stage[0:COLS, TILE:HALF] = wide[:, 0:512]

        @pl.when(g == 0)
        def _():
            stage[:, 0:TILE] = jnp.zeros((PAIR, TILE), F32)

    @pl.when(c == 1)
    def _():
        stage[COLS:PAIR, 0:512] = wide[:, 512:1024]

        @pl.when(g == 15)
        def _():
            stage[:, 512:HALF] = jnp.zeros((PAIR, TILE), F32)

    waits = (
        6 + 3 + 7 + 15
        + (x != 0).astype(jnp.int32)
        + jnp.logical_not(stays).astype(jnp.int32)
        + (g < 15).astype(jnp.int32)
        + (g > 0).astype(jnp.int32)
    )
    pl.semaphore_wait(barrier, waits)

    used = [0, 0]
    sent = []

    def slot(which, count=1):
        used[which] += count
        return used[which] - count

    def remote(src, dst, target, send, recv):
        return pltpu.make_async_remote_copy(
            src_ref=src, dst_ref=dst, send_sem=send_sem.at[send], recv_sem=recv_sem.at[recv],
            device_id=target, device_id_type=MESH,
        )

    def copy(src, dst, target, recv):
        made = remote(src, dst, target, slot(0), recv)
        made.start()
        sent.append(made)

    def start_unless(skip, made):
        @pl.when(jnp.logical_not(skip))
        def _():
            made.start()

    def await_bytes(ref, recv):
        pltpu.make_async_copy(ref, ref, recv_sem.at[recv]).wait()

    own_rows = pl.ds(pl.multiple_of(c * COLS, 8), COLS)
    other_rows = pl.ds(pl.multiple_of(other * COLS, 8), COLS)
    r_left, r_right, r_swap = slot(1, 2), slot(1, 2), slot(1)
    halo_up = remote(
        wide.at[:, 896:1024], stage.at[own_rows, 0:TILE], device(g + 1, p, 0), slot(0), r_left + c
    )
    halo_down = remote(
        wide.at[:, 0:TILE], stage.at[own_rows, 512:HALF], device(g - 1, p, 1), slot(0), r_right + c
    )

    @pl.when(g < 15)
    def _():
        halo_up.start()

    @pl.when(g > 0)
    def _():
        halo_down.start()

    copy(
        wide.at[:, pl.ds(pl.multiple_of(other * 512, 128), 512)],
        stage.at[own_rows, pl.ds(pl.multiple_of(c * TILE, 128), 512)],
        partner, r_swap,
    )

    loads[1].wait()
    loads[2].wait()
    lane = lax.broadcasted_iota(jnp.int32, (COLS, 128), 1)
    pad = jnp.zeros((32 - COLS, 128), F32)
    for pair in range(8):
        s_tile = ws[:, pair * 128:(pair + 1) * 128].astype(F32)
        n_tile = wn[:, pair * 128:(pair + 1) * 128].astype(F32)
        low = jnp.where(lane < 64, s_tile, pltpu.roll(n_tile, 64, 1))
        high = jnp.where(lane < 64, pltpu.roll(s_tile, 64, 1), n_tile)
        wsend[2 * pair] = jnp.concatenate([low, pad], 0).astype(BF16)
        wsend[2 * pair + 1] = jnp.concatenate([high, pad], 0).astype(BF16)

    r_w1 = slot(1, 4)
    for step in range(1, 4):
        chip = w_dst_y * 4 + mod4(zh + step)
        copy(wsend.at[chip], wg.at[c, p], device(g, chip, c), r_w1 + step)
    chip0 = w_dst_y * 4 + zh
    w_zero = remote(wsend.at[chip0], wg.at[c, p], device(g, chip0, c), slot(0), r_w1)

    @pl.when(x != 0)
    def _():
        w_zero.start()

    @pl.when(x == 0)
    def _():
        wg[c, p] = wsend[chip0]

    def block(by, bz, part):
        rows = pl.ds(pl.multiple_of((mod4(bz) * 4 + mod4(by)) * PAIR, 16), PAIR)
        start = {"all": 0, "a": other * PART_B, "b": c * PART_A}[part]
        width = {"all": HALF, "a": PART_A, "b": PART_B}[part]
        return xg.at[rows, pl.ds(pl.multiple_of(c * HALF + start, 128), width)]

    r_pair = slot(1, 4)

    def forward(by, bz, part, target, recv):
        view = block(by, bz, part)
        copy(view, view, target, recv)

    def share(by, bz, part):
        forward(by, bz, part, partner, r_pair + mod4(bz))

    r_z1 = slot(1, 4)
    r_z2 = slot(1, 2)
    r_y1 = slot(1, 12)
    r_y2 = slot(1, 6)
    r_y3 = slot(1, 6)

    def column(number):
        return zh + sign * (0, -1, 1)[number]

    def send_y1(number, part):
        first = r_y1 + 4 * number + (0 if part == "a" else 2)
        forward(y, column(number), part, y_fwd, first)
        forward(y, column(number), part, y_bwd, first + 1)

    def take_y1(number):
        bz = column(number)
        first = r_y1 + 4 * number
        await_bytes(block(y - sign, bz, "a"), first)
        forward(y - sign, bz, "a", y_fwd, r_y2 + 2 * number)
        await_bytes(block(y + sign, bz, "b"), first + 3)
        forward(y + sign, bz, "b", y_bwd, r_y2 + 2 * number + 1)
        await_bytes(block(y - sign, bz, "b"), first + 2)
        share(y - sign, bz, "all")
        await_bytes(block(y + sign, bz, "a"), first + 1)
        share(y + sign, bz, "all")

    def take_y2(number):
        bz = column(number)
        await_bytes(block(y + 2, bz, "a"), r_y2 + 2 * number)
        share(y + 2, bz, "a")
        await_bytes(block(y + 2, bz, "b"), r_y2 + 2 * number + 1)
        share(y + 2, bz, "b")

    def send_y3(part):
        first = r_y3 + (0 if part == "a" else 3)
        forward(y, zh + 2, part, y_fwd, first)
        forward(y, zh + 2, part, y_bwd, first + 1)
        forward(y, zh + 2, part, y_far, first + 2)
        share(y, zh + 2, part)

    def take_y3(part):
        first = r_y3 + (0 if part == "a" else 3)
        for offset, by in enumerate((y - sign, y + sign, y + 2)):
            await_bytes(block(by, zh + 2, part), first + offset)
            share(by, zh + 2, part)

    await_bytes(stage.at[other_rows, pl.ds(pl.multiple_of(other * TILE, 128), 512)], r_swap)
    block(y, zh, "a")[...] = stage[:, pl.ds(pl.multiple_of(other * PART_B, 128), PART_A)].astype(BF16)
    forward(y, zh, "a", z_fwd, r_z1)
    forward(y, zh, "a", z_bwd, r_z1 + 3)
    send_y1(0, "a")

    @pl.when(jnp.logical_and(c == 0, g > 0))
    def _():
        await_bytes(stage.at[0:COLS, 0:TILE], r_left)
        await_bytes(stage.at[COLS:PAIR, 0:TILE], r_left + 1)

    @pl.when(jnp.logical_and(c == 1, g < 15))
    def _():
        await_bytes(stage.at[0:COLS, 512:HALF], r_right)
        await_bytes(stage.at[COLS:PAIR, 512:HALF], r_right + 1)

    block(y, zh, "b")[...] = stage[:, pl.ds(pl.multiple_of(c * PART_A, 128), PART_B)].astype(BF16)
    forward(y, zh, "b", z_bwd, r_z1 + 1)
    forward(y, zh, "b", z_fwd, r_z1 + 2)

    send_y1(0, "b")
    share(y, zh, "all")

    for load in loads[3:6]:
        load.wait()
    for tile in range(8):
        dense = adj[tile].astype(F32)
        padded = jnp.concatenate([dense, jnp.zeros((TILE, TILE), F32)], 1)
        moved = pltpu.roll(padded, off[tile] - tile * TILE, 1)
        band[tile] = (moved * live[tile].astype(F32)).astype(BF16)

    def neighbours(bz):
        col = mod4(bz)
        rows = pl.ds(pl.multiple_of(col * COLUMN, 16), COLUMN)
        await_bytes(xg.at[rows, pl.ds(pl.multiple_of(other * HALF, 128), HALF)], r_pair + col)
        for tile in range(8):
            nb[rows, tile * TILE:(tile + 1) * TILE] = lax.dot_general(
                xg[rows, tile * TILE:tile * TILE + 3 * TILE], band[tile],
                (((1,), (1,)), ((), ())), preferred_element_type=F32,
            ).astype(BF16)

    def products(bz):
        col = mod4(bz)
        rows = pl.ds(pl.multiple_of(col * COLUMN, 16), COLUMN)
        ws_t = wt[col, pl.ds(pl.multiple_of(c * 32, 16), 32), :]
        wn_t = wt[col, pl.ds(pl.multiple_of(64 + c * 32, 16), 32), :]
        pre_acc[...] += (
            jnp.dot(ws_t, xg[rows, TILE:TILE + 1024], preferred_element_type=F32)
            + jnp.dot(wn_t, nb[rows, :], preferred_element_type=F32)
        )

    take_y1(0)

    await_bytes(block(y, zh - sign, "a"), r_z1)
    forward(y, zh - sign, "a", z_fwd, r_z2)
    send_y1(1, "a")
    await_bytes(block(y, zh + sign, "a"), r_z1 + 3)
    send_y1(2, "a")

    for step in range(1, 4):
        await_bytes(wg.at[c, w_src_y * 4 + mod4(zh + step)], r_w1 + 4 - step)

    @pl.when(x != 0)
    def _():
        await_bytes(wg.at[c, w_src_y * 4 + zh], r_w1)

    r_w2 = slot(1, 4)
    part_w = wg.at[c, pl.ds(w_src_y * 4, 4)]
    for step in range(1, 4):
        copy(part_w, part_w, device(g - x + mod4(x + step), p, c), r_w2 + step)

    take_y2(0)
    await_bytes(block(y, zh + sign, "b"), r_z1 + 1)
    forward(y, zh + sign, "b", z_bwd, r_z2 + 1)
    send_y1(2, "b")
    await_bytes(block(y, zh - sign, "b"), r_z1 + 2)
    send_y1(1, "b")
    share(y, zh - sign, "all")
    share(y, zh + sign, "all")
    neighbours(zh)
    for step in range(1, 4):
        await_bytes(wg.at[c, pl.ds(mod4(y + x - step) * 4, 4)], r_w2 + step)
    r_w3 = slot(1)
    copy(wg.at[c], wg.at[c], partner, r_w3)
    take_y1(1)
    take_y1(2)
    await_bytes(block(y, zh + 2, "a"), r_z2)
    send_y3("a")
    await_bytes(block(y, zh + 2, "b"), r_z2 + 1)
    send_y3("b")
    take_y2(2)
    take_y2(1)

    await_bytes(wg.at[other], r_w3)
    for col in range(4):
        rows = []
        for row in range(4):
            for core in range(2):
                rows.append(wg[core, row * 4 + col].astype(F32)[0:COLS])
        wt[col] = jnp.concatenate(rows, 0).T.astype(BF16)
    loads[6].wait()
    spot = lax.broadcasted_iota(jnp.int32, (32, 1024), 1)
    row = lax.broadcasted_iota(jnp.int32, (32, 1024), 0)
    bias_own = jnp.sum(
        jnp.where(spot == row + f * 32, jnp.broadcast_to(bias[...], (32, 1024)), 0.0),
        axis=1, keepdims=True,
    )
    pre_acc[...] = jnp.broadcast_to(bias_own, (32, 1024))
    products(zh)
    neighbours(zh - 1)
    neighbours(zh + 1)
    products(zh - 1)
    products(zh + 1)
    take_y3("a")
    take_y3("b")
    neighbours(zh + 2)
    products(zh + 2)

    loads[7].wait()
    pre = pre_acc[...]
    gate = jax.nn.sigmoid(pre)
    act = pre * gate
    hid[...] = act.astype(BF16)
    delta = (act - tgt[...].astype(F32)) * (gate * (1.0 + pre * (1.0 - gate))) * (1.0 / 128.0)

    head = delta.astype(BF16)
    rest = (delta - head.astype(F32)).astype(BF16)
    both = jnp.concatenate([head] * 4 + [rest] * 4, 0)
    turn = (((1,), (1,)), ((), ()))
    bias_term = jnp.sum(delta, axis=1, keepdims=True)
    quarter = lax.div(lax.broadcasted_iota(jnp.int32, (PAIR, 128), 1), 32)
    blank = jnp.zeros((16, 128), F32)

    def with_bias(tile, low_total, high_total):
        lane_of = lax.broadcasted_iota(jnp.int32, tile.shape, 1)
        bias_sum = jnp.where(lane_of < 64, low_total, high_total)
        first = bias_sum.astype(BF16).astype(F32)
        tile = jnp.where(lax.rem(lane_of, 64) == 48, first, tile)
        return jnp.where(lax.rem(lane_of, 64) == 49, bias_sum - first, tile)

    r_ra = slot(1, 4)
    for turn_of in range(1, 5):
        row = mod4(x + turn_of)
        spans = [
            pl.ds(pl.multiple_of((col * 4 + row) * PAIR, 16), PAIR) for col in range(4)
        ]
        left = jnp.concatenate(
            [xg[span, TILE:TILE + 1024] for span in spans] + [nb[span, :] for span in spans], 0
        )
        grad = lax.dot_general(left, both, turn, preferred_element_type=F32)
        grad = grad[:, 0:128] + grad[:, 128:256]

        def packed(first):
            parts = [grad[first + col * PAIR:first + (col + 1) * PAIR] for col in range(4)]
            low = jnp.where(quarter == 0, parts[0], parts[1])
            high = jnp.where(quarter == 2, parts[2], parts[3])
            return jnp.where(quarter < 2, low, high)

        own_term, nb_term = packed(0), packed(COLUMN)
        turned = jnp.concatenate(
            [own_term[0:COLS], nb_term[0:COLS], blank, own_term[COLS:PAIR], nb_term[COLS:PAIR], blank], 0
        ).T
        for col in range(4):
            tile = with_bias(turned[col * 32:(col + 1) * 32], bias_term, bias_term)
            rsend[row, col] = tile.astype(BF16)
        if turn_of < 4:
            copy(rsend.at[row], ra.at[turn_of], device(g - x + row, p, c), r_ra + turn_of)

    for turn_of in range(1, 4):
        await_bytes(ra.at[turn_of], r_ra + turn_of)

    r_rb = slot(1)
    to_group = zh * 4 + mod4(y + x)
    halves = lax.broadcasted_iota(jnp.int32, (16, 128), 1) < 64
    for step in (2, 1, 3, 0):
        col = mod4(zh + step)
        summed = (rsend[x, col].astype(F32) + ra[1, col].astype(F32)) + (
            ra[2, col].astype(F32) + ra[3, col].astype(F32)
        )
        bias_sum = summed[:, 48:49] + summed[:, 49:50]
        summed = with_bias(summed, bias_sum, bias_sum)
        top, bottom = summed[0:16], summed[16:32]
        rbs[col, 0] = jnp.where(halves, top, pltpu.roll(bottom, 64, 1)).astype(BF16)
        rbs[col, 1] = jnp.where(halves, pltpu.roll(top, 64, 1), bottom).astype(BF16)
        if step:
            for core in range(2):
                copy(rbs.at[col, core], rb.at[zl, c], device(to_group, x * 4 + col, core), r_rb)

    copy(rbs.at[zh, other], rb.at[zl, c], device(to_group, x * 4 + zh, other), r_rb)
    r_zero = remote(rbs.at[zh, c], rb.at[zl, c], device(to_group, x * 4 + zh, c), slot(0), r_rb)
    start_unless(stays, r_zero)

    @pl.when(stays)
    def _():
        pltpu.make_async_copy(rbs.at[zh, c], rb.at[zl, c], recv_sem.at[r_rb]).start()

    await_bytes(rb, r_rb)
    for core in range(2):
        total = (rb[0, core].astype(F32) + rb[1, core].astype(F32)) + (
            rb[2, core].astype(F32) + rb[3, core].astype(F32)
        )
        fg[r_chip, core] = with_bias(
            total, total[:, 48:49] + total[:, 49:50], total[:, 112:113] + total[:, 113:114]
        ).astype(BF16)

    r_r2 = slot(1, 4)
    for step in range(1, 16):
        far = lax.rem(g + step, 16)
        copy(fg.at[r_chip], fg.at[r_chip], device(far, p, c), r_r2 + mod4(x - lax.rem(far, 4)))
    for k in (0, 1, 3, 2):
        await_bytes(fg.at[0:(4 if k else 3)], r_r2 + k)
        for half in range(2):
            part = lax.rem(x - y + k + 4, 4) * 2 + half
            rows = []
            for chip in range(2):
                for core in range(2):
                    tile = fg[2 * part + chip, core].astype(F32)
                    rows += [tile, pltpu.roll(tile, 64, 1)]
            turned = jnp.concatenate(rows, 0).T
            span = pl.ds(pl.multiple_of(part * 128, 128), 128)
            gs_o[:, span] = turned[0:24]
            gn_o[:, span] = turned[24:48]
            gb_o[:, span] = turned[48:49] + turned[49:50]

    for made in sent:
        made.wait_send()

    @pl.when(g < 15)
    def _():
        halo_up.wait_send()

    @pl.when(g > 0)
    def _():
        halo_down.wait_send()

    @pl.when(x != 0)
    def _():
        w_zero.wait_send()

    @pl.when(jnp.logical_not(stays))
    def _():
        r_zero.wait_send()

    assert used[0] <= SENDS and used[1] <= RECVS, used


OUTS = (
    jax.ShapeDtypeStruct((32, 1024), BF16),
    jax.ShapeDtypeStruct((COLS, 1024), F32),
    jax.ShapeDtypeStruct((COLS, 1024), F32),
    jax.ShapeDtypeStruct((1, 1024), F32),
)


def place(hid, gs, gn, gb, hid_o, gs_o, gn_o, gb_o, sem):
    pairs = [(hid, hid_o), (gs, gs_o), (gn, gn_o), (gb, gb_o)]
    moves = [pltpu.make_async_copy(src, dst, sem.at[i]) for i, (src, dst) in enumerate(pairs)]
    for move in moves:
        move.start()
    for move in moves:
        move.wait()


def shards(features, adjacency, offsets, live, w_self, w_neigh, bias, targets):
    vmem = pl.BlockSpec(memory_space=pltpu.VMEM)
    hbm = pl.BlockSpec(memory_space=pltpu.HBM)
    inputs = [features.T, adjacency, offsets, live, w_self, w_neigh, bias.reshape(1, 1024), targets]
    results = pl.pallas_call(
        kernel,
        out_shape=OUTS,
        in_specs=[hbm] * 8,
        out_specs=(vmem,) * 4,
        scratch_shapes=[
            pltpu.VMEM((COLS, 1024), BF16),
            pltpu.VMEM((8, TILE, 256), BF16),
            pltpu.SMEM((8,), jnp.int32),
            pltpu.SMEM((8,), jnp.int32),
            pltpu.VMEM((COLS, 1024), BF16),
            pltpu.VMEM((COLS, 1024), BF16),
            pltpu.VMEM((1, 1024), F32),
            pltpu.VMEM((32, 1024), BF16),
            pltpu.VMEM((COLS, 1024), F32),
            pltpu.VMEM((PAIR, HALF), F32),
            pltpu.VMEM((768, 1280), BF16),
            pltpu.VMEM((768, 1024), BF16),
            pltpu.VMEM((8, TILE, 384), BF16),
            pltpu.VMEM((16, 32, 128), BF16),
            pltpu.VMEM((2, 16, 32, 128), BF16),
            pltpu.VMEM((4, 128, COLUMN), BF16),
            pltpu.VMEM((32, 1024), F32),
            pltpu.VMEM((4, 4, 32, 128), BF16),
            pltpu.VMEM((4, 4, 32, 128), BF16),
            pltpu.VMEM((4, 2, 16, 128), BF16),
            pltpu.VMEM((4, 2, 16, 128), BF16),
            pltpu.VMEM((16, 2, 16, 128), BF16),
            pltpu.SemaphoreType.DMA((8,)),
            pltpu.SemaphoreType.DMA((SENDS,)),
            pltpu.SemaphoreType.DMA((RECVS,)),
        ],
        compiler_params=pltpu.CompilerParams(
            collective_id=0, has_side_effects=True, vmem_limit_bytes=48 * 1024 * 1024
        ),
        cost_estimate=pl.CostEstimate(flops=10**9, bytes_accessed=10**7, transcendentals=32768),
    )(*[pltpu.with_memory_space_constraint(array, pltpu.HBM) for array in inputs])
    hidden, grad_self, grad_neigh, grad_bias = pl.pallas_call(
        place,
        out_shape=OUTS,
        in_specs=[vmem] * 4,
        out_specs=(pl.BlockSpec(memory_space=pl.ANY),) * 4,
        scratch_shapes=[pltpu.SemaphoreType.DMA((4,))],
        compiler_params=pltpu.CompilerParams(vmem_limit_bytes=1024 * 1024),
    )(*[pltpu.with_memory_space_constraint(array, pltpu.VMEM) for array in results])
    return hidden, grad_self, grad_neigh, grad_bias.reshape(1024)


def solution(mesh):
    in_specs = (
        P("grp", "feat"),
        P("grp", None, None),
        P("grp"),
        P("grp"),
        P("feat", None),
        P("feat", None),
        P(),
        P("feat", "grp"),
    )
    out_specs = (P("feat", "grp"), P("feat", None), P("feat", None), P())
    return jax.shard_map(shards, mesh=mesh, in_specs=in_specs, out_specs=out_specs, check_vma=False)
```

```python
import jax
import jax.numpy as jnp
from jax import lax
from jax.experimental import pallas as pl
from jax.experimental.pallas import tpu as pltpu
from jax.sharding import PartitionSpec as P

F32 = jnp.float32
BF16 = jnp.bfloat16
MESH = pl.DeviceIdType.MESH

COLS = 24
PAIR = 48
COLUMN = 4 * PAIR
HALF = 640
PART_A = 384
PART_B = HALF - PART_A
TILE = 128
SENDS = 96
RECVS = 72


def mod4(value):
    return lax.rem(value + 4, 4)


def kernel(
    feat_h, adj_h, off_h, live_h, ws_h, wn_h, bias_h, tgt_h,
    hid, gs_o, gn_o, gb_o,
    feat, adj, off, live, ws, wn, bias, tgt,
    wide, edge, xr, xg, nb, band, wsend, wg, wt, pre_acc, rsend, ra, rbs, rb, fg,
    in_sem, send_sem, recv_sem,
):
    loads = [
        pltpu.make_async_copy(src, dst, in_sem.at[i])
        for i, (src, dst) in enumerate(
            [(feat_h, feat), (ws_h, ws), (wn_h, wn), (adj_h, adj), (off_h, off), (live_h, live),
             (bias_h, bias), (tgt_h, tgt)]
        )
    ]
    for load in loads:
        load.start()

    g = lax.axis_index("grp")
    f = lax.axis_index("feat")
    c = lax.rem(f, 2)
    p = lax.div(f, 2)
    y = lax.div(p, 4)
    zh = lax.rem(p, 4)
    x = lax.rem(g, 4)
    zl = lax.div(g, 4)
    other = 1 - c
    sign = 1 - 2 * c

    def device(group, chip, core):
        return (group, chip * 2 + core)

    partner = device(g, p, other)
    y_fwd = device(g, mod4(y + sign) * 4 + zh, c)
    y_bwd = device(g, mod4(y - sign) * 4 + zh, c)
    y_far = device(g, mod4(y + 2) * 4 + zh, c)
    z_fwd = device(g, y * 4 + mod4(zh + sign), c)
    z_bwd = device(g, y * 4 + mod4(zh - sign), c)
    stays = jnp.logical_and(zh == zl, jnp.logical_and(x == 0, y == 0))

    barrier = pltpu.get_barrier_semaphore()

    def tell(target):
        pl.semaphore_signal(barrier, inc=1, device_id=target, device_id_type=MESH)

    for target in (z_fwd, z_bwd, y_fwd, y_bwd, y_far, partner):
        tell(target)

    w_src_y = mod4(y + x)
    w_dst_y = mod4(y - x)
    r_chip = mod4(x - y) * 4 + zl
    for step in range(1, 4):
        tell(device(g, w_src_y * 4 + mod4(zh + step), c))
        tell(device(mod4(zl + step) * 4 + y, r_chip, 0))
        tell(device(mod4(zl + step) * 4 + y, r_chip, 1))

    @pl.when(x != 0)
    def _():
        tell(device(g, w_src_y * 4 + zh, c))

    tell(device(zl * 4 + y, r_chip, other))

    @pl.when(jnp.logical_not(stays))
    def _():
        tell(device(zl * 4 + y, r_chip, c))

    def tell_far(step, carry):
        tell(device(lax.rem(g + step, 16), p, c))
        return carry

    lax.fori_loop(1, 16, tell_far, 0)

    loads[0].wait()
    wide[...] = feat[...].astype(F32)

    own_row = ((zh * 2 + c) * 4 + y) * PAIR
    own = pl.ds(pl.multiple_of(own_row, 16), PAIR)
    xr[own, 0:512] = jnp.concatenate([wide[:, 0:512], wide[:, 512:1024]], 0).astype(BF16)

    @pl.when(g == 0)
    def _():
        edge[0:COLS] = jnp.zeros((COLS, TILE), F32)

    @pl.when(g == 15)
    def _():
        edge[COLS:PAIR] = jnp.zeros((COLS, TILE), F32)

    waits = (
        6 + 3 + 7 + 15
        + (x != 0).astype(jnp.int32)
        + jnp.logical_not(stays).astype(jnp.int32)
    )
    pl.semaphore_wait(barrier, waits)

    used = [0, 0]
    sent = []

    def slot(which, count=1):
        used[which] += count
        return used[which] - count

    def remote(src, dst, target, send, recv):
        return pltpu.make_async_remote_copy(
            src_ref=src, dst_ref=dst, send_sem=send_sem.at[send], recv_sem=recv_sem.at[recv],
            device_id=target, device_id_type=MESH,
        )

    def copy(src, dst, target, recv):
        made = remote(src, dst, target, slot(0), recv)
        made.start()
        sent.append(made)

    def start_unless(skip, made):
        @pl.when(jnp.logical_not(skip))
        def _():
            made.start()

    def await_bytes(ref, recv):
        pltpu.make_async_copy(ref, ref, recv_sem.at[recv]).wait()

    r_left, r_right = slot(1), slot(1)
    halo_up = remote(
        wide.at[:, 896:1024], edge.at[0:COLS], device(g + 1, p, c), slot(0), r_left
    )
    halo_down = remote(
        wide.at[:, 0:TILE], edge.at[COLS:PAIR], device(g - 1, p, c), slot(0), r_right
    )

    @pl.when(g < 15)
    def _():
        halo_up.start()

    @pl.when(g > 0)
    def _():
        halo_down.start()

    def block(by, bz, part):
        first = (mod4(bz) * 2 + c) * 4 + mod4(by)
        start = {"all": 0, "a": 0, "b": PART_A}[part]
        width = {"all": HALF, "a": PART_A, "b": PART_B}[part]
        return xr.at[pl.ds(pl.multiple_of(first * PAIR, 16), PAIR), start:start + width]

    r_pair = slot(1, 4)

    def forward(by, bz, part, target, recv):
        view = block(by, bz, part)
        copy(view, view, target, recv)

    def share(by, bz, part):
        forward(by, bz, part, partner, r_pair + mod4(bz))

    r_z1 = slot(1, 4)
    r_z2 = slot(1, 2)
    r_y1 = slot(1, 12)
    r_y2 = slot(1, 6)
    r_y3 = slot(1, 6)

    def column(number):
        return zh + sign * (0, -1, 1)[number]

    def send_y1(number, part):
        first = r_y1 + 4 * number + (0 if part == "a" else 2)
        forward(y, column(number), part, y_fwd, first)
        forward(y, column(number), part, y_bwd, first + 1)

    def take_y1(number):
        bz = column(number)
        first = r_y1 + 4 * number
        await_bytes(block(y - sign, bz, "a"), first)
        forward(y - sign, bz, "a", y_fwd, r_y2 + 2 * number)
        await_bytes(block(y + sign, bz, "b"), first + 3)
        forward(y + sign, bz, "b", y_bwd, r_y2 + 2 * number + 1)
        await_bytes(block(y - sign, bz, "b"), first + 2)
        share(y - sign, bz, "all")
        await_bytes(block(y + sign, bz, "a"), first + 1)
        share(y + sign, bz, "all")

    def take_y2(number):
        bz = column(number)
        await_bytes(block(y + 2, bz, "a"), r_y2 + 2 * number)
        share(y + 2, bz, "a")
        await_bytes(block(y + 2, bz, "b"), r_y2 + 2 * number + 1)
        share(y + 2, bz, "b")

    def send_y3(part):
        first = r_y3 + (0 if part == "a" else 3)
        forward(y, zh + 2, part, y_fwd, first)
        forward(y, zh + 2, part, y_bwd, first + 1)
        forward(y, zh + 2, part, y_far, first + 2)
        share(y, zh + 2, part)

    def take_y3(part):
        first = r_y3 + (0 if part == "a" else 3)
        for offset, by in enumerate((y - sign, y + sign, y + 2)):
            await_bytes(block(by, zh + 2, part), first + offset)
            share(by, zh + 2, part)

    forward(y, zh, "a", z_fwd, r_z1)
    forward(y, zh, "a", z_bwd, r_z1 + 3)
    send_y1(0, "a")

    loads[1].wait()
    loads[2].wait()
    lane = lax.broadcasted_iota(jnp.int32, (COLS, 128), 1)
    pad = jnp.zeros((32 - COLS, 128), F32)
    for pair in range(8):
        s_tile = ws[:, pair * 128:(pair + 1) * 128].astype(F32)
        n_tile = wn[:, pair * 128:(pair + 1) * 128].astype(F32)
        low = jnp.where(lane < 64, s_tile, pltpu.roll(n_tile, 64, 1))
        high = jnp.where(lane < 64, pltpu.roll(s_tile, 64, 1), n_tile)
        wsend[2 * pair] = jnp.concatenate([low, pad], 0).astype(BF16)
        wsend[2 * pair + 1] = jnp.concatenate([high, pad], 0).astype(BF16)

    r_w1 = slot(1, 4)
    for step in range(1, 4):
        chip = w_dst_y * 4 + mod4(zh + step)
        copy(wsend.at[chip], wg.at[c, p], device(g, chip, c), r_w1 + step)
    chip0 = w_dst_y * 4 + zh
    w_zero = remote(wsend.at[chip0], wg.at[c, p], device(g, chip0, c), slot(0), r_w1)

    @pl.when(x != 0)
    def _():
        w_zero.start()

    @pl.when(x == 0)
    def _():
        wg[c, p] = wsend[chip0]

    @pl.when(g > 0)
    def _():
        await_bytes(edge.at[0:COLS], r_left)

    @pl.when(g < 15)
    def _():
        await_bytes(edge.at[COLS:PAIR], r_right)

    xr[own, 512:HALF] = edge[...].astype(BF16)
    forward(y, zh, "b", z_bwd, r_z1 + 1)
    forward(y, zh, "b", z_fwd, r_z1 + 2)

    send_y1(0, "b")
    share(y, zh, "all")

    for load in loads[3:6]:
        load.wait()
    for tile in range(8):
        dense = adj[tile].astype(F32)
        padded = jnp.concatenate([dense, jnp.zeros((TILE, TILE), F32)], 1)
        moved = pltpu.roll(padded, off[tile] - tile * TILE, 1)
        band[tile] = (moved * live[tile].astype(F32)).astype(BF16)

    def neighbours(bz):
        col = mod4(bz)
        rows = pl.ds(pl.multiple_of(col * COLUMN, 16), COLUMN)
        theirs = pl.ds(pl.multiple_of((col * 2 + other) * COLUMN, 16), COLUMN)
        await_bytes(xr.at[theirs], r_pair + col)
        for row in range(4):
            cores = []
            for core in range(2):
                first = ((col * 2 + core) * 4 + row) * PAIR
                cores.append(xr[pl.ds(pl.multiple_of(first, 16), PAIR), :].astype(F32))
            low = jnp.concatenate([half[0:COLS] for half in cores], 0).astype(BF16)
            high = jnp.concatenate([half[COLS:PAIR] for half in cores], 0).astype(BF16)
            here = pl.ds(pl.multiple_of((col * 4 + row) * PAIR, 16), PAIR)
            xg[here, 0:TILE] = low[:, 512:HALF]
            xg[here, TILE:HALF] = low[:, 0:512]
            xg[here, HALF:HALF + 512] = high[:, 0:512]
            xg[here, HALF + 512:2 * HALF] = high[:, 512:HALF]
        for tile in range(8):
            nb[rows, tile * TILE:(tile + 1) * TILE] = lax.dot_general(
                xg[rows, tile * TILE:tile * TILE + 3 * TILE], band[tile],
                (((1,), (1,)), ((), ())), preferred_element_type=F32,
            ).astype(BF16)

    def products(bz):
        col = mod4(bz)
        rows = pl.ds(pl.multiple_of(col * COLUMN, 16), COLUMN)
        ws_t = wt[col, pl.ds(pl.multiple_of(c * 32, 16), 32), :]
        wn_t = wt[col, pl.ds(pl.multiple_of(64 + c * 32, 16), 32), :]
        pre_acc[...] += (
            jnp.dot(ws_t, xg[rows, TILE:TILE + 1024], preferred_element_type=F32)
            + jnp.dot(wn_t, nb[rows, :], preferred_element_type=F32)
        )

    take_y1(0)

    await_bytes(block(y, zh - sign, "a"), r_z1)
    forward(y, zh - sign, "a", z_fwd, r_z2)
    send_y1(1, "a")
    await_bytes(block(y, zh + sign, "a"), r_z1 + 3)
    send_y1(2, "a")

    for step in range(1, 4):
        await_bytes(wg.at[c, w_src_y * 4 + mod4(zh + step)], r_w1 + 4 - step)

    @pl.when(x != 0)
    def _():
        await_bytes(wg.at[c, w_src_y * 4 + zh], r_w1)

    r_w2 = slot(1, 4)
    part_w = wg.at[c, pl.ds(w_src_y * 4, 4)]
    for step in range(1, 4):
        copy(part_w, part_w, device(g - x + mod4(x + step), p, c), r_w2 + step)

    take_y2(0)
    await_bytes(block(y, zh + sign, "b"), r_z1 + 1)
    forward(y, zh + sign, "b", z_bwd, r_z2 + 1)
    send_y1(2, "b")
    await_bytes(block(y, zh - sign, "b"), r_z1 + 2)
    send_y1(1, "b")
    share(y, zh - sign, "all")
    share(y, zh + sign, "all")
    neighbours(zh)
    for step in range(1, 4):
        await_bytes(wg.at[c, pl.ds(mod4(y + x - step) * 4, 4)], r_w2 + step)
    r_w3 = slot(1)
    copy(wg.at[c], wg.at[c], partner, r_w3)
    take_y1(1)
    take_y1(2)
    await_bytes(block(y, zh + 2, "a"), r_z2)
    send_y3("a")
    await_bytes(block(y, zh + 2, "b"), r_z2 + 1)
    send_y3("b")
    take_y2(2)
    take_y2(1)

    await_bytes(wg.at[other], r_w3)
    for col in range(4):
        rows = []
        for row in range(4):
            for core in range(2):
                rows.append(wg[core, row * 4 + col].astype(F32)[0:COLS])
        wt[col] = jnp.concatenate(rows, 0).T.astype(BF16)
    loads[6].wait()
    spot = lax.broadcasted_iota(jnp.int32, (32, 1024), 1)
    row = lax.broadcasted_iota(jnp.int32, (32, 1024), 0)
    bias_own = jnp.sum(
        jnp.where(spot == row + f * 32, jnp.broadcast_to(bias[...], (32, 1024)), 0.0),
        axis=1, keepdims=True,
    )
    pre_acc[...] = jnp.broadcast_to(bias_own, (32, 1024))
    products(zh)
    neighbours(zh - 1)
    neighbours(zh + 1)
    products(zh - 1)
    products(zh + 1)
    take_y3("a")
    take_y3("b")
    neighbours(zh + 2)
    products(zh + 2)

    loads[7].wait()
    pre = pre_acc[...]
    gate = jax.nn.sigmoid(pre)
    act = pre * gate
    hid[...] = act.astype(BF16)
    delta = (act - tgt[...].astype(F32)) * (gate * (1.0 + pre * (1.0 - gate))) * (1.0 / 128.0)

    head = delta.astype(BF16)
    rest = (delta - head.astype(F32)).astype(BF16)
    both = jnp.concatenate([head] * 4 + [rest] * 4, 0)
    turn = (((1,), (1,)), ((), ()))
    bias_term = jnp.sum(delta, axis=1, keepdims=True)
    quarter = lax.div(lax.broadcasted_iota(jnp.int32, (PAIR, 128), 1), 32)
    blank = jnp.zeros((16, 128), F32)

    def with_bias(tile, low_total, high_total):
        lane_of = lax.broadcasted_iota(jnp.int32, tile.shape, 1)
        bias_sum = jnp.where(lane_of < 64, low_total, high_total)
        first = bias_sum.astype(BF16).astype(F32)
        tile = jnp.where(lax.rem(lane_of, 64) == 48, first, tile)
        return jnp.where(lax.rem(lane_of, 64) == 49, bias_sum - first, tile)

    r_ra = slot(1, 4)
    for turn_of in range(1, 5):
        row = mod4(x + turn_of)
        spans = [
            pl.ds(pl.multiple_of((col * 4 + row) * PAIR, 16), PAIR) for col in range(4)
        ]
        left = jnp.concatenate(
            [xg[span, TILE:TILE + 1024] for span in spans] + [nb[span, :] for span in spans], 0
        )
        grad = lax.dot_general(left, both, turn, preferred_element_type=F32)
        grad = grad[:, 0:128] + grad[:, 128:256]

        def packed(first):
            parts = [grad[first + col * PAIR:first + (col + 1) * PAIR] for col in range(4)]
            low = jnp.where(quarter == 0, parts[0], parts[1])
            high = jnp.where(quarter == 2, parts[2], parts[3])
            return jnp.where(quarter < 2, low, high)

        own_term, nb_term = packed(0), packed(COLUMN)
        turned = jnp.concatenate(
            [own_term[0:COLS], nb_term[0:COLS], blank, own_term[COLS:PAIR], nb_term[COLS:PAIR], blank], 0
        ).T
        for col in range(4):
            tile = with_bias(turned[col * 32:(col + 1) * 32], bias_term, bias_term)
            rsend[row, col] = tile.astype(BF16)
        if turn_of < 4:
            copy(rsend.at[row], ra.at[turn_of], device(g - x + row, p, c), r_ra + turn_of)

    for turn_of in range(1, 4):
        await_bytes(ra.at[turn_of], r_ra + turn_of)

    r_rb = slot(1)
    to_group = zh * 4 + mod4(y + x)
    halves = lax.broadcasted_iota(jnp.int32, (16, 128), 1) < 64
    for step in (2, 1, 3, 0):
        col = mod4(zh + step)
        summed = (rsend[x, col].astype(F32) + ra[1, col].astype(F32)) + (
            ra[2, col].astype(F32) + ra[3, col].astype(F32)
        )
        bias_sum = summed[:, 48:49] + summed[:, 49:50]
        summed = with_bias(summed, bias_sum, bias_sum)
        top, bottom = summed[0:16], summed[16:32]
        rbs[col, 0] = jnp.where(halves, top, pltpu.roll(bottom, 64, 1)).astype(BF16)
        rbs[col, 1] = jnp.where(halves, pltpu.roll(top, 64, 1), bottom).astype(BF16)
        if step:
            for core in range(2):
                copy(rbs.at[col, core], rb.at[zl, c], device(to_group, x * 4 + col, core), r_rb)

    copy(rbs.at[zh, other], rb.at[zl, c], device(to_group, x * 4 + zh, other), r_rb)
    r_zero = remote(rbs.at[zh, c], rb.at[zl, c], device(to_group, x * 4 + zh, c), slot(0), r_rb)
    start_unless(stays, r_zero)

    @pl.when(stays)
    def _():
        pltpu.make_async_copy(rbs.at[zh, c], rb.at[zl, c], recv_sem.at[r_rb]).start()

    await_bytes(rb, r_rb)
    for core in range(2):
        total = (rb[0, core].astype(F32) + rb[1, core].astype(F32)) + (
            rb[2, core].astype(F32) + rb[3, core].astype(F32)
        )
        fg[r_chip, core] = with_bias(
            total, total[:, 48:49] + total[:, 49:50], total[:, 112:113] + total[:, 113:114]
        ).astype(BF16)

    r_r2 = slot(1, 4)
    for step in range(1, 16):
        far = lax.rem(g + step, 16)
        copy(fg.at[r_chip], fg.at[r_chip], device(far, p, c), r_r2 + mod4(x - lax.rem(far, 4)))
    for k in (0, 1, 3, 2):
        await_bytes(fg.at[0:(4 if k else 3)], r_r2 + k)
        for half in range(2):
            part = lax.rem(x - y + k + 4, 4) * 2 + half
            rows = []
            for chip in range(2):
                for core in range(2):
                    tile = fg[2 * part + chip, core].astype(F32)
                    rows += [tile, pltpu.roll(tile, 64, 1)]
            turned = jnp.concatenate(rows, 0).T
            span = pl.ds(pl.multiple_of(part * 128, 128), 128)
            gs_o[:, span] = turned[0:24]
            gn_o[:, span] = turned[24:48]
            gb_o[:, span] = turned[48:49] + turned[49:50]

    for made in sent:
        made.wait_send()

    @pl.when(g < 15)
    def _():
        halo_up.wait_send()

    @pl.when(g > 0)
    def _():
        halo_down.wait_send()

    @pl.when(x != 0)
    def _():
        w_zero.wait_send()

    @pl.when(jnp.logical_not(stays))
    def _():
        r_zero.wait_send()

    assert used[0] <= SENDS and used[1] <= RECVS, used


OUTS = (
    jax.ShapeDtypeStruct((32, 1024), BF16),
    jax.ShapeDtypeStruct((COLS, 1024), F32),
    jax.ShapeDtypeStruct((COLS, 1024), F32),
    jax.ShapeDtypeStruct((1, 1024), F32),
)


def place(hid, gs, gn, gb, hid_o, gs_o, gn_o, gb_o, sem):
    pairs = [(hid, hid_o), (gs, gs_o), (gn, gn_o), (gb, gb_o)]
    moves = [pltpu.make_async_copy(src, dst, sem.at[i]) for i, (src, dst) in enumerate(pairs)]
    for move in moves:
        move.start()
    for move in moves:
        move.wait()


def shards(features, adjacency, offsets, live, w_self, w_neigh, bias, targets):
    vmem = pl.BlockSpec(memory_space=pltpu.VMEM)
    hbm = pl.BlockSpec(memory_space=pltpu.HBM)
    inputs = [features.T, adjacency, offsets, live, w_self, w_neigh, bias.reshape(1, 1024), targets]
    results = pl.pallas_call(
        kernel,
        out_shape=OUTS,
        in_specs=[hbm] * 8,
        out_specs=(vmem,) * 4,
        scratch_shapes=[
            pltpu.VMEM((COLS, 1024), BF16),
            pltpu.VMEM((8, TILE, 256), BF16),
            pltpu.SMEM((8,), jnp.int32),
            pltpu.SMEM((8,), jnp.int32),
            pltpu.VMEM((COLS, 1024), BF16),
            pltpu.VMEM((COLS, 1024), BF16),
            pltpu.VMEM((1, 1024), F32),
            pltpu.VMEM((32, 1024), BF16),
            pltpu.VMEM((COLS, 1024), F32),
            pltpu.VMEM((PAIR, TILE), F32),
            pltpu.VMEM((1536, HALF), BF16),
            pltpu.VMEM((768, 1280), BF16),
            pltpu.VMEM((768, 1024), BF16),
            pltpu.VMEM((8, TILE, 384), BF16),
            pltpu.VMEM((16, 32, 128), BF16),
            pltpu.VMEM((2, 16, 32, 128), BF16),
            pltpu.VMEM((4, 128, COLUMN), BF16),
            pltpu.VMEM((32, 1024), F32),
            pltpu.VMEM((4, 4, 32, 128), BF16),
            pltpu.VMEM((4, 4, 32, 128), BF16),
            pltpu.VMEM((4, 2, 16, 128), BF16),
            pltpu.VMEM((4, 2, 16, 128), BF16),
            pltpu.VMEM((16, 2, 16, 128), BF16),
            pltpu.SemaphoreType.DMA((8,)),
            pltpu.SemaphoreType.DMA((SENDS,)),
            pltpu.SemaphoreType.DMA((RECVS,)),
        ],
        compiler_params=pltpu.CompilerParams(
            collective_id=0, has_side_effects=True, vmem_limit_bytes=48 * 1024 * 1024
        ),
        cost_estimate=pl.CostEstimate(flops=10**9, bytes_accessed=10**7, transcendentals=32768),
    )(*[pltpu.with_memory_space_constraint(array, pltpu.HBM) for array in inputs])
    hidden, grad_self, grad_neigh, grad_bias = pl.pallas_call(
        place,
        out_shape=OUTS,
        in_specs=[vmem] * 4,
        out_specs=(pl.BlockSpec(memory_space=pl.ANY),) * 4,
        scratch_shapes=[pltpu.SemaphoreType.DMA((4,))],
        compiler_params=pltpu.CompilerParams(vmem_limit_bytes=1024 * 1024),
    )(*[pltpu.with_memory_space_constraint(array, pltpu.VMEM) for array in results])
    return hidden, grad_self, grad_neigh, grad_bias.reshape(1024)


def solution(mesh):
    in_specs = (
        P("grp", "feat"),
        P("grp", None, None),
        P("grp"),
        P("grp"),
        P("feat", None),
        P("feat", None),
        P(),
        P("feat", "grp"),
    )
    out_specs = (P("feat", "grp"), P("feat", None), P("feat", None), P())
    return jax.shard_map(shards, mesh=mesh, in_specs=in_specs, out_specs=out_specs, check_vma=False)
```

```python
import jax
import jax.numpy as jnp
from jax import lax
from jax.experimental import pallas as pl
from jax.experimental.pallas import tpu as pltpu
from jax.sharding import PartitionSpec as P

F32 = jnp.float32
BF16 = jnp.bfloat16
MESH = pl.DeviceIdType.MESH

COLS = 24
PAIR = 48
COLUMN = 4 * PAIR
HALF = 640
PART_A = 384
PART_B = HALF - PART_A
TILE = 128
SENDS = 96
RECVS = 72


def mod4(value):
    return lax.rem(value + 4, 4)


def kernel(
    feat_h, adj_h, off_h, live_h, ws_h, wn_h, bias_h, tgt_h,
    hid, gs_o, gn_o, gb_o,
    feat, adj, off, live, ws, wn, bias, tgt,
    wide, stage, xg, nb, band, wsend, wg, wt, pre_acc, both, rsend, ra, rbs, rb, fg,
    in_sem, send_sem, recv_sem,
):
    loads = [
        pltpu.make_async_copy(src, dst, in_sem.at[i])
        for i, (src, dst) in enumerate(
            [(feat_h, feat), (ws_h, ws), (wn_h, wn), (adj_h, adj), (off_h, off), (live_h, live),
             (bias_h, bias), (tgt_h, tgt)]
        )
    ]
    for load in loads:
        load.start()

    g = lax.axis_index("grp")
    f = lax.axis_index("feat")
    c = lax.rem(f, 2)
    p = lax.div(f, 2)
    y = lax.div(p, 4)
    zh = lax.rem(p, 4)
    x = lax.rem(g, 4)
    zl = lax.div(g, 4)
    other = 1 - c
    sign = 1 - 2 * c

    def device(group, chip, core):
        return (group, chip * 2 + core)

    partner = device(g, p, other)
    y_fwd = device(g, mod4(y + sign) * 4 + zh, c)
    y_bwd = device(g, mod4(y - sign) * 4 + zh, c)
    y_far = device(g, mod4(y + 2) * 4 + zh, c)
    z_fwd = device(g, y * 4 + mod4(zh + sign), c)
    z_bwd = device(g, y * 4 + mod4(zh - sign), c)
    stays = jnp.logical_and(zh == zl, jnp.logical_and(x == 0, y == 0))

    barrier = pltpu.get_barrier_semaphore()

    def tell(target):
        pl.semaphore_signal(barrier, inc=1, device_id=target, device_id_type=MESH)

    @pl.when(jnp.logical_and(c == 0, g > 0))
    def _():
        tell(device(g - 1, p, 0))
        tell(device(g - 1, p, 1))

    @pl.when(jnp.logical_and(c == 1, g < 15))
    def _():
        tell(device(g + 1, p, 0))
        tell(device(g + 1, p, 1))

    for target in (z_fwd, z_bwd, y_fwd, y_bwd, y_far, partner):
        tell(target)

    w_src_y = mod4(y + x)
    w_dst_y = mod4(y - x)
    r_chip = mod4(x - y) * 4 + zl
    for step in range(1, 4):
        tell(device(g, w_src_y * 4 + mod4(zh + step), c))
        tell(device(mod4(zl + step) * 4 + y, r_chip, 0))
        tell(device(mod4(zl + step) * 4 + y, r_chip, 1))

    @pl.when(x != 0)
    def _():
        tell(device(g, w_src_y * 4 + zh, c))

    tell(device(zl * 4 + y, r_chip, other))

    @pl.when(jnp.logical_not(stays))
    def _():
        tell(device(zl * 4 + y, r_chip, c))

    def tell_far(step, carry):
        tell(device(lax.rem(g + step, 16), p, c))
        return carry

    lax.fori_loop(1, 16, tell_far, 0)

    loads[0].wait()
    wide[...] = feat[...].astype(F32)

    @pl.when(c == 0)
    def _():
        stage[0:COLS, TILE:HALF] = wide[:, 0:512]

        @pl.when(g == 0)
        def _():
            stage[:, 0:TILE] = jnp.zeros((PAIR, TILE), F32)

    @pl.when(c == 1)
    def _():
        stage[COLS:PAIR, 0:512] = wide[:, 512:1024]

        @pl.when(g == 15)
        def _():
            stage[:, 512:HALF] = jnp.zeros((PAIR, TILE), F32)

    waits = (
        6 + 3 + 7 + 15
        + (x != 0).astype(jnp.int32)
        + jnp.logical_not(stays).astype(jnp.int32)
        + (g < 15).astype(jnp.int32)
        + (g > 0).astype(jnp.int32)
    )
    pl.semaphore_wait(barrier, waits)

    used = [0, 0]
    sent = []

    def slot(which, count=1):
        used[which] += count
        return used[which] - count

    def remote(src, dst, target, send, recv):
        return pltpu.make_async_remote_copy(
            src_ref=src, dst_ref=dst, send_sem=send_sem.at[send], recv_sem=recv_sem.at[recv],
            device_id=target, device_id_type=MESH,
        )

    def copy(src, dst, target, recv):
        made = remote(src, dst, target, slot(0), recv)
        made.start()
        sent.append(made)

    def start_unless(skip, made):
        @pl.when(jnp.logical_not(skip))
        def _():
            made.start()

    def await_bytes(ref, recv):
        pltpu.make_async_copy(ref, ref, recv_sem.at[recv]).wait()

    own_rows = pl.ds(pl.multiple_of(c * COLS, 8), COLS)
    other_rows = pl.ds(pl.multiple_of(other * COLS, 8), COLS)
    r_left, r_right, r_swap = slot(1, 2), slot(1, 2), slot(1)
    halo_up = remote(
        wide.at[:, 896:1024], stage.at[own_rows, 0:TILE], device(g + 1, p, 0), slot(0), r_left + c
    )
    halo_down = remote(
        wide.at[:, 0:TILE], stage.at[own_rows, 512:HALF], device(g - 1, p, 1), slot(0), r_right + c
    )

    @pl.when(g < 15)
    def _():
        halo_up.start()

    @pl.when(g > 0)
    def _():
        halo_down.start()

    copy(
        wide.at[:, pl.ds(pl.multiple_of(other * 512, 128), 512)],
        stage.at[own_rows, pl.ds(pl.multiple_of(c * TILE, 128), 512)],
        partner, r_swap,
    )

    loads[1].wait()
    loads[2].wait()
    lane = lax.broadcasted_iota(jnp.int32, (COLS, 128), 1)
    pad = jnp.zeros((32 - COLS, 128), F32)
    for pair in range(8):
        s_tile = ws[:, pair * 128:(pair + 1) * 128].astype(F32)
        n_tile = wn[:, pair * 128:(pair + 1) * 128].astype(F32)
        low = jnp.where(lane < 64, s_tile, pltpu.roll(n_tile, 64, 1))
        high = jnp.where(lane < 64, pltpu.roll(s_tile, 64, 1), n_tile)
        wsend[2 * pair] = jnp.concatenate([low, pad], 0).astype(BF16)
        wsend[2 * pair + 1] = jnp.concatenate([high, pad], 0).astype(BF16)

    r_w1 = slot(1, 4)
    for step in range(1, 4):
        chip = w_dst_y * 4 + mod4(zh + step)
        copy(wsend.at[chip], wg.at[c, p], device(g, chip, c), r_w1 + step)
    chip0 = w_dst_y * 4 + zh
    w_zero = remote(wsend.at[chip0], wg.at[c, p], device(g, chip0, c), slot(0), r_w1)

    @pl.when(x != 0)
    def _():
        w_zero.start()

    @pl.when(x == 0)
    def _():
        wg[c, p] = wsend[chip0]

    def block(by, bz, part):
        rows = pl.ds(pl.multiple_of((mod4(bz) * 4 + mod4(by)) * PAIR, 16), PAIR)
        start = {"all": 0, "a": other * PART_B, "b": c * PART_A}[part]
        width = {"all": HALF, "a": PART_A, "b": PART_B}[part]
        return xg.at[rows, pl.ds(pl.multiple_of(c * HALF + start, 128), width)]

    r_pair = slot(1, 4)

    def forward(by, bz, part, target, recv):
        view = block(by, bz, part)
        copy(view, view, target, recv)

    def share(by, bz, part):
        forward(by, bz, part, partner, r_pair + mod4(bz))

    r_z1 = slot(1, 4)
    r_z2 = slot(1, 2)
    r_y1 = slot(1, 12)
    r_y2 = slot(1, 6)
    r_y3 = slot(1, 6)

    def column(number):
        return zh + sign * (0, -1, 1)[number]

    def send_y1(number, part):
        first = r_y1 + 4 * number + (0 if part == "a" else 2)
        forward(y, column(number), part, y_fwd, first)
        forward(y, column(number), part, y_bwd, first + 1)

    def take_y1(number):
        bz = column(number)
        first = r_y1 + 4 * number
        await_bytes(block(y - sign, bz, "a"), first)
        forward(y - sign, bz, "a", y_fwd, r_y2 + 2 * number)
        await_bytes(block(y + sign, bz, "b"), first + 3)
        forward(y + sign, bz, "b", y_bwd, r_y2 + 2 * number + 1)
        await_bytes(block(y - sign, bz, "b"), first + 2)
        share(y - sign, bz, "all")
        await_bytes(block(y + sign, bz, "a"), first + 1)
        share(y + sign, bz, "all")

    def take_y2(number):
        bz = column(number)
        await_bytes(block(y + 2, bz, "a"), r_y2 + 2 * number)
        share(y + 2, bz, "a")
        await_bytes(block(y + 2, bz, "b"), r_y2 + 2 * number + 1)
        share(y + 2, bz, "b")

    def send_y3(part):
        first = r_y3 + (0 if part == "a" else 3)
        forward(y, zh + 2, part, y_fwd, first)
        forward(y, zh + 2, part, y_bwd, first + 1)
        forward(y, zh + 2, part, y_far, first + 2)
        share(y, zh + 2, part)

    def take_y3(part):
        first = r_y3 + (0 if part == "a" else 3)
        for offset, by in enumerate((y - sign, y + sign, y + 2)):
            await_bytes(block(by, zh + 2, part), first + offset)
            share(by, zh + 2, part)

    await_bytes(stage.at[other_rows, pl.ds(pl.multiple_of(other * TILE, 128), 512)], r_swap)
    block(y, zh, "a")[...] = stage[:, pl.ds(pl.multiple_of(other * PART_B, 128), PART_A)].astype(BF16)
    forward(y, zh, "a", z_fwd, r_z1)
    forward(y, zh, "a", z_bwd, r_z1 + 3)
    send_y1(0, "a")

    @pl.when(jnp.logical_and(c == 0, g > 0))
    def _():
        await_bytes(stage.at[0:COLS, 0:TILE], r_left)
        await_bytes(stage.at[COLS:PAIR, 0:TILE], r_left + 1)

    @pl.when(jnp.logical_and(c == 1, g < 15))
    def _():
        await_bytes(stage.at[0:COLS, 512:HALF], r_right)
        await_bytes(stage.at[COLS:PAIR, 512:HALF], r_right + 1)

    block(y, zh, "b")[...] = stage[:, pl.ds(pl.multiple_of(c * PART_A, 128), PART_B)].astype(BF16)
    forward(y, zh, "b", z_bwd, r_z1 + 1)
    forward(y, zh, "b", z_fwd, r_z1 + 2)

    send_y1(0, "b")
    share(y, zh, "all")

    for load in loads[3:6]:
        load.wait()
    for tile in range(8):
        dense = adj[tile].astype(F32)
        padded = jnp.concatenate([dense, jnp.zeros((TILE, TILE), F32)], 1)
        moved = pltpu.roll(padded, off[tile] - tile * TILE, 1)
        band[tile] = (moved * live[tile].astype(F32)).T.astype(BF16)

    def neighbours(bz):
        col = mod4(bz)
        rows = pl.ds(pl.multiple_of(col * COLUMN, 16), COLUMN)
        await_bytes(xg.at[rows, pl.ds(pl.multiple_of(other * HALF, 128), HALF)], r_pair + col)
        for tile in range(8):
            nb[rows, tile * TILE:(tile + 1) * TILE] = jnp.dot(
                xg[rows, tile * TILE:tile * TILE + 3 * TILE], band[tile], preferred_element_type=F32
            ).astype(BF16)

    def products(bz):
        col = mod4(bz)
        rows = pl.ds(pl.multiple_of(col * COLUMN, 16), COLUMN)
        ws_t = wt[col, pl.ds(pl.multiple_of(c * 32, 16), 32), :]
        wn_t = wt[col, pl.ds(pl.multiple_of(64 + c * 32, 16), 32), :]
        pre_acc[...] += (
            jnp.dot(ws_t, xg[rows, TILE:TILE + 1024], preferred_element_type=F32)
            + jnp.dot(wn_t, nb[rows, :], preferred_element_type=F32)
        )

    take_y1(0)

    await_bytes(block(y, zh - sign, "a"), r_z1)
    forward(y, zh - sign, "a", z_fwd, r_z2)
    send_y1(1, "a")
    await_bytes(block(y, zh + sign, "a"), r_z1 + 3)
    send_y1(2, "a")

    for step in range(1, 4):
        await_bytes(wg.at[c, w_src_y * 4 + mod4(zh + step)], r_w1 + 4 - step)

    @pl.when(x != 0)
    def _():
        await_bytes(wg.at[c, w_src_y * 4 + zh], r_w1)

    r_w2 = slot(1, 4)
    part_w = wg.at[c, pl.ds(w_src_y * 4, 4)]
    for step in range(1, 4):
        copy(part_w, part_w, device(g - x + mod4(x + step), p, c), r_w2 + step)

    take_y2(0)
    await_bytes(block(y, zh + sign, "b"), r_z1 + 1)
    forward(y, zh + sign, "b", z_bwd, r_z2 + 1)
    send_y1(2, "b")
    await_bytes(block(y, zh - sign, "b"), r_z1 + 2)
    send_y1(1, "b")
    share(y, zh - sign, "all")
    share(y, zh + sign, "all")
    neighbours(zh)
    for step in range(1, 4):
        await_bytes(wg.at[c, pl.ds(mod4(y + x - step) * 4, 4)], r_w2 + step)
    r_w3 = slot(1)
    copy(wg.at[c], wg.at[c], partner, r_w3)
    take_y1(1)
    take_y1(2)
    await_bytes(block(y, zh + 2, "a"), r_z2)
    send_y3("a")
    await_bytes(block(y, zh + 2, "b"), r_z2 + 1)
    send_y3("b")
    take_y2(2)
    take_y2(1)

    await_bytes(wg.at[other], r_w3)
    for col in range(4):
        rows = []
        for row in range(4):
            for core in range(2):
                rows.append(wg[core, row * 4 + col].astype(F32)[0:COLS])
        wt[col] = jnp.concatenate(rows, 0).T.astype(BF16)
    loads[6].wait()
    spot = lax.broadcasted_iota(jnp.int32, (32, 1024), 1)
    row = lax.broadcasted_iota(jnp.int32, (32, 1024), 0)
    bias_own = jnp.sum(
        jnp.where(spot == row + f * 32, jnp.broadcast_to(bias[...], (32, 1024)), 0.0),
        axis=1, keepdims=True,
    )
    pre_acc[...] = jnp.broadcast_to(bias_own, (32, 1024))
    products(zh)
    neighbours(zh - 1)
    neighbours(zh + 1)
    products(zh - 1)
    products(zh + 1)
    take_y3("a")
    take_y3("b")
    neighbours(zh + 2)
    products(zh + 2)

    loads[7].wait()
    pre = pre_acc[...]
    gate = jax.nn.sigmoid(pre)
    act = pre * gate
    hid[...] = act.astype(BF16)
    delta = (act - tgt[...].astype(F32)) * (gate * (1.0 + pre * (1.0 - gate))) * (1.0 / 128.0)

    head = delta.astype(BF16).astype(F32)
    both[...] = jnp.concatenate([head, delta - head] * 2, 0).T.astype(BF16)
    bias_term = jnp.sum(delta, axis=1, keepdims=True)
    quarter = lax.div(lax.broadcasted_iota(jnp.int32, (PAIR, 128), 1), 32)
    blank = jnp.zeros((16, 128), F32)

    def with_bias(tile, low_total, high_total):
        lane_of = lax.broadcasted_iota(jnp.int32, tile.shape, 1)
        bias_sum = jnp.where(lane_of < 64, low_total, high_total)
        first = bias_sum.astype(BF16).astype(F32)
        tile = jnp.where(lax.rem(lane_of, 64) == 48, first, tile)
        return jnp.where(lax.rem(lane_of, 64) == 49, bias_sum - first, tile)

    r_ra = slot(1, 4)
    for turn_of in range(1, 5):
        row = mod4(x + turn_of)
        spans = [
            pl.ds(pl.multiple_of((col * 4 + row) * PAIR, 16), PAIR) for col in range(4)
        ]
        left = jnp.concatenate(
            [xg[span, TILE:TILE + 1024] for span in spans] + [nb[span, :] for span in spans], 0
        )
        grad = jnp.dot(left, both[...], preferred_element_type=F32)
        grad = grad + pltpu.roll(grad, 32, 1)

        def packed(first):
            parts = [grad[first + col * PAIR:first + (col + 1) * PAIR] for col in range(4)]
            low = jnp.where(quarter == 0, parts[0], parts[1])
            high = jnp.where(quarter == 2, parts[2], parts[3])
            return jnp.where(quarter < 2, low, high)

        own_term, nb_term = packed(0), packed(COLUMN)
        turned = jnp.concatenate(
            [own_term[0:COLS], nb_term[0:COLS], blank, own_term[COLS:PAIR], nb_term[COLS:PAIR], blank], 0
        ).T
        for col in range(4):
            tile = with_bias(turned[col * 32:(col + 1) * 32], bias_term, bias_term)
            rsend[row, col] = tile.astype(BF16)
        if turn_of < 4:
            copy(rsend.at[row], ra.at[turn_of], device(g - x + row, p, c), r_ra + turn_of)

    for turn_of in range(1, 4):
        await_bytes(ra.at[turn_of], r_ra + turn_of)

    r_rb = slot(1)
    to_group = zh * 4 + mod4(y + x)
    halves = lax.broadcasted_iota(jnp.int32, (16, 128), 1) < 64
    for step in (2, 1, 3, 0):
        col = mod4(zh + step)
        summed = (rsend[x, col].astype(F32) + ra[1, col].astype(F32)) + (
            ra[2, col].astype(F32) + ra[3, col].astype(F32)
        )
        bias_sum = summed[:, 48:49] + summed[:, 49:50]
        summed = with_bias(summed, bias_sum, bias_sum)
        top, bottom = summed[0:16], summed[16:32]
        rbs[col, 0] = jnp.where(halves, top, pltpu.roll(bottom, 64, 1)).astype(BF16)
        rbs[col, 1] = jnp.where(halves, pltpu.roll(top, 64, 1), bottom).astype(BF16)
        if step:
            for core in range(2):
                copy(rbs.at[col, core], rb.at[zl, c], device(to_group, x * 4 + col, core), r_rb)

    copy(rbs.at[zh, other], rb.at[zl, c], device(to_group, x * 4 + zh, other), r_rb)
    r_zero = remote(rbs.at[zh, c], rb.at[zl, c], device(to_group, x * 4 + zh, c), slot(0), r_rb)
    start_unless(stays, r_zero)

    @pl.when(stays)
    def _():
        pltpu.make_async_copy(rbs.at[zh, c], rb.at[zl, c], recv_sem.at[r_rb]).start()

    await_bytes(rb, r_rb)
    for core in range(2):
        total = (rb[0, core].astype(F32) + rb[1, core].astype(F32)) + (
            rb[2, core].astype(F32) + rb[3, core].astype(F32)
        )
        fg[r_chip, core] = with_bias(
            total, total[:, 48:49] + total[:, 49:50], total[:, 112:113] + total[:, 113:114]
        ).astype(BF16)

    r_r2 = slot(1, 4)
    for step in range(1, 16):
        far = lax.rem(g + step, 16)
        copy(fg.at[r_chip], fg.at[r_chip], device(far, p, c), r_r2 + mod4(x - lax.rem(far, 4)))
    for k in (0, 1, 3, 2):
        await_bytes(fg.at[0:(4 if k else 3)], r_r2 + k)
        for half in range(2):
            part = lax.rem(x - y + k + 4, 4) * 2 + half
            rows = []
            for chip in range(2):
                for core in range(2):
                    tile = fg[2 * part + chip, core].astype(F32)
                    rows += [tile, pltpu.roll(tile, 64, 1)]
            turned = jnp.concatenate(rows, 0).T
            span = pl.ds(pl.multiple_of(part * 128, 128), 128)
            gs_o[:, span] = turned[0:24]
            gn_o[:, span] = turned[24:48]
            gb_o[:, span] = turned[48:49] + turned[49:50]

    for made in sent:
        made.wait_send()

    @pl.when(g < 15)
    def _():
        halo_up.wait_send()

    @pl.when(g > 0)
    def _():
        halo_down.wait_send()

    @pl.when(x != 0)
    def _():
        w_zero.wait_send()

    @pl.when(jnp.logical_not(stays))
    def _():
        r_zero.wait_send()

    assert used[0] <= SENDS and used[1] <= RECVS, used


OUTS = (
    jax.ShapeDtypeStruct((32, 1024), BF16),
    jax.ShapeDtypeStruct((COLS, 1024), F32),
    jax.ShapeDtypeStruct((COLS, 1024), F32),
    jax.ShapeDtypeStruct((1, 1024), F32),
)


def place(hid, gs, gn, gb, hid_o, gs_o, gn_o, gb_o, sem):
    pairs = [(hid, hid_o), (gs, gs_o), (gn, gn_o), (gb, gb_o)]
    moves = [pltpu.make_async_copy(src, dst, sem.at[i]) for i, (src, dst) in enumerate(pairs)]
    for move in moves:
        move.start()
    for move in moves:
        move.wait()


def shards(features, adjacency, offsets, live, w_self, w_neigh, bias, targets):
    vmem = pl.BlockSpec(memory_space=pltpu.VMEM)
    hbm = pl.BlockSpec(memory_space=pltpu.HBM)
    inputs = [features.T, adjacency, offsets, live, w_self, w_neigh, bias.reshape(1, 1024), targets]
    results = pl.pallas_call(
        kernel,
        out_shape=OUTS,
        in_specs=[hbm] * 8,
        out_specs=(vmem,) * 4,
        scratch_shapes=[
            pltpu.VMEM((COLS, 1024), BF16),
            pltpu.VMEM((8, TILE, 256), BF16),
            pltpu.SMEM((8,), jnp.int32),
            pltpu.SMEM((8,), jnp.int32),
            pltpu.VMEM((COLS, 1024), BF16),
            pltpu.VMEM((COLS, 1024), BF16),
            pltpu.VMEM((1, 1024), F32),
            pltpu.VMEM((32, 1024), BF16),
            pltpu.VMEM((COLS, 1024), F32),
            pltpu.VMEM((PAIR, HALF), F32),
            pltpu.VMEM((768, 1280), BF16),
            pltpu.VMEM((768, 1024), BF16),
            pltpu.VMEM((8, 384, TILE), BF16),
            pltpu.VMEM((16, 32, 128), BF16),
            pltpu.VMEM((2, 16, 32, 128), BF16),
            pltpu.VMEM((4, 128, COLUMN), BF16),
            pltpu.VMEM((32, 1024), F32),
            pltpu.VMEM((1024, 128), BF16),
            pltpu.VMEM((4, 4, 32, 128), BF16),
            pltpu.VMEM((4, 4, 32, 128), BF16),
            pltpu.VMEM((4, 2, 16, 128), BF16),
            pltpu.VMEM((4, 2, 16, 128), BF16),
            pltpu.VMEM((16, 2, 16, 128), BF16),
            pltpu.SemaphoreType.DMA((8,)),
            pltpu.SemaphoreType.DMA((SENDS,)),
            pltpu.SemaphoreType.DMA((RECVS,)),
        ],
        compiler_params=pltpu.CompilerParams(
            collective_id=0, has_side_effects=True, vmem_limit_bytes=48 * 1024 * 1024
        ),
        cost_estimate=pl.CostEstimate(flops=10**9, bytes_accessed=10**7, transcendentals=32768),
    )(*[pltpu.with_memory_space_constraint(array, pltpu.HBM) for array in inputs])
    hidden, grad_self, grad_neigh, grad_bias = pl.pallas_call(
        place,
        out_shape=OUTS,
        in_specs=[vmem] * 4,
        out_specs=(pl.BlockSpec(memory_space=pl.ANY),) * 4,
        scratch_shapes=[pltpu.SemaphoreType.DMA((4,))],
        compiler_params=pltpu.CompilerParams(vmem_limit_bytes=1024 * 1024),
    )(*[pltpu.with_memory_space_constraint(array, pltpu.VMEM) for array in results])
    return hidden, grad_self, grad_neigh, grad_bias.reshape(1024)


def solution(mesh):
    in_specs = (
        P("grp", "feat"),
        P("grp", None, None),
        P("grp"),
        P("grp"),
        P("feat", None),
        P("feat", None),
        P(),
        P("feat", "grp"),
    )
    out_specs = (P("feat", "grp"), P("feat", None), P("feat", None), P())
    return jax.shard_map(shards, mesh=mesh, in_specs=in_specs, out_specs=out_specs, check_vma=False)
```

```python
import jax
import jax.numpy as jnp
from jax import lax
from jax.experimental import pallas as pl
from jax.experimental.pallas import tpu as pltpu
from jax.sharding import PartitionSpec as P

F32 = jnp.float32
BF16 = jnp.bfloat16
MESH = pl.DeviceIdType.MESH

COLS = 24
PAIR = 48
COLUMN = 4 * PAIR
HALF = 640
PART_A = 384
PART_B = HALF - PART_A
TILE = 128
SENDS = 96
RECVS = 72


def mod4(value):
    return lax.rem(value + 4, 4)


def kernel(
    feat_h, adj_h, off_h, live_h, ws_h, wn_h, bias_h, tgt_h,
    hid, gs_o, gn_o, gb_o,
    feat, adj, off, live, ws, wn, bias, tgt,
    wide, stage, xg, nb, band, wsend, wg, wt, pre_acc, rsend, ra, rbs, rb, fg,
    in_sem, send_sem, recv_sem,
):
    loads = [
        pltpu.make_async_copy(src, dst, in_sem.at[i])
        for i, (src, dst) in enumerate(
            [(feat_h, feat), (ws_h, ws), (wn_h, wn), (adj_h, adj), (off_h, off), (live_h, live),
             (bias_h, bias), (tgt_h, tgt)]
        )
    ]
    for load in loads:
        load.start()

    g = lax.axis_index("grp")
    f = lax.axis_index("feat")
    c = lax.rem(f, 2)
    p = lax.div(f, 2)
    y = lax.div(p, 4)
    zh = lax.rem(p, 4)
    x = lax.rem(g, 4)
    zl = lax.div(g, 4)
    other = 1 - c
    sign = 1 - 2 * c

    def device(group, chip, core):
        return (group, chip * 2 + core)

    partner = device(g, p, other)
    y_fwd = device(g, mod4(y + sign) * 4 + zh, c)
    y_bwd = device(g, mod4(y - sign) * 4 + zh, c)
    y_far = device(g, mod4(y + 2) * 4 + zh, c)
    z_fwd = device(g, y * 4 + mod4(zh + sign), c)
    z_bwd = device(g, y * 4 + mod4(zh - sign), c)
    stays = jnp.logical_and(zh == zl, jnp.logical_and(x == 0, y == 0))

    barrier = pltpu.get_barrier_semaphore()

    def tell(target):
        pl.semaphore_signal(barrier, inc=1, device_id=target, device_id_type=MESH)

    @pl.when(jnp.logical_and(c == 0, g > 0))
    def _():
        tell(device(g - 1, p, 0))
        tell(device(g - 1, p, 1))

    @pl.when(jnp.logical_and(c == 1, g < 15))
    def _():
        tell(device(g + 1, p, 0))
        tell(device(g + 1, p, 1))

    for target in (z_fwd, z_bwd, y_fwd, y_bwd, y_far, partner):
        tell(target)

    w_src_y = mod4(y + x)
    w_dst_y = mod4(y - x)
    r_chip = mod4(x - y) * 4 + zl
    for step in range(1, 4):
        tell(device(g, w_src_y * 4 + mod4(zh + step), c))
        tell(device(g - x + mod4(x + step), p, other))
        tell(device(mod4(zl + step) * 4 + y, r_chip, 0))
        tell(device(mod4(zl + step) * 4 + y, r_chip, 1))

    @pl.when(x != 0)
    def _():
        tell(device(g, w_src_y * 4 + zh, c))

    tell(device(zl * 4 + y, r_chip, other))

    @pl.when(jnp.logical_not(stays))
    def _():
        tell(device(zl * 4 + y, r_chip, c))

    def tell_far(step, carry):
        tell(device(lax.rem(g + step, 16), p, c))
        return carry

    lax.fori_loop(1, 16, tell_far, 0)

    loads[0].wait()
    wide[...] = feat[...].astype(F32)

    @pl.when(c == 0)
    def _():
        stage[0:COLS, TILE:HALF] = wide[:, 0:512]

        @pl.when(g == 0)
        def _():
            stage[:, 0:TILE] = jnp.zeros((PAIR, TILE), F32)

    @pl.when(c == 1)
    def _():
        stage[COLS:PAIR, 0:512] = wide[:, 512:1024]

        @pl.when(g == 15)
        def _():
            stage[:, 512:HALF] = jnp.zeros((PAIR, TILE), F32)

    waits = (
        6 + 3 + 7 + 15 + 3
        + (x != 0).astype(jnp.int32)
        + jnp.logical_not(stays).astype(jnp.int32)
        + (g < 15).astype(jnp.int32)
        + (g > 0).astype(jnp.int32)
    )
    pl.semaphore_wait(barrier, waits)

    used = [0, 0]
    sent = []

    def slot(which, count=1):
        used[which] += count
        return used[which] - count

    def remote(src, dst, target, send, recv):
        return pltpu.make_async_remote_copy(
            src_ref=src, dst_ref=dst, send_sem=send_sem.at[send], recv_sem=recv_sem.at[recv],
            device_id=target, device_id_type=MESH,
        )

    def copy(src, dst, target, recv):
        made = remote(src, dst, target, slot(0), recv)
        made.start()
        sent.append(made)

    def start_unless(skip, made):
        @pl.when(jnp.logical_not(skip))
        def _():
            made.start()

    def await_bytes(ref, recv):
        pltpu.make_async_copy(ref, ref, recv_sem.at[recv]).wait()

    own_rows = pl.ds(pl.multiple_of(c * COLS, 8), COLS)
    other_rows = pl.ds(pl.multiple_of(other * COLS, 8), COLS)
    r_left, r_right, r_swap = slot(1, 2), slot(1, 2), slot(1)
    halo_up = remote(
        wide.at[:, 896:1024], stage.at[own_rows, 0:TILE], device(g + 1, p, 0), slot(0), r_left + c
    )
    halo_down = remote(
        wide.at[:, 0:TILE], stage.at[own_rows, 512:HALF], device(g - 1, p, 1), slot(0), r_right + c
    )

    @pl.when(g < 15)
    def _():
        halo_up.start()

    @pl.when(g > 0)
    def _():
        halo_down.start()

    copy(
        wide.at[:, pl.ds(pl.multiple_of(other * 512, 128), 512)],
        stage.at[own_rows, pl.ds(pl.multiple_of(c * TILE, 128), 512)],
        partner, r_swap,
    )

    loads[1].wait()
    loads[2].wait()
    lane = lax.broadcasted_iota(jnp.int32, (COLS, 128), 1)
    pad = jnp.zeros((32 - COLS, 128), F32)
    for pair in range(8):
        s_tile = ws[:, pair * 128:(pair + 1) * 128].astype(F32)
        n_tile = wn[:, pair * 128:(pair + 1) * 128].astype(F32)
        low = jnp.where(lane < 64, s_tile, pltpu.roll(n_tile, 64, 1))
        high = jnp.where(lane < 64, pltpu.roll(s_tile, 64, 1), n_tile)
        wsend[2 * pair] = jnp.concatenate([low, pad], 0).astype(BF16)
        wsend[2 * pair + 1] = jnp.concatenate([high, pad], 0).astype(BF16)

    r_w1 = slot(1, 4)
    for step in range(1, 4):
        chip = w_dst_y * 4 + mod4(zh + step)
        copy(wsend.at[chip], wg.at[c, p], device(g, chip, c), r_w1 + step)
    chip0 = w_dst_y * 4 + zh
    w_zero = remote(wsend.at[chip0], wg.at[c, p], device(g, chip0, c), slot(0), r_w1)

    @pl.when(x != 0)
    def _():
        w_zero.start()

    @pl.when(x == 0)
    def _():
        wg[c, p] = wsend[chip0]

    def block(by, bz, part):
        rows = pl.ds(pl.multiple_of((mod4(bz) * 4 + mod4(by)) * PAIR, 16), PAIR)
        start = {"all": 0, "a": other * PART_B, "b": c * PART_A}[part]
        width = {"all": HALF, "a": PART_A, "b": PART_B}[part]
        return xg.at[rows, pl.ds(pl.multiple_of(c * HALF + start, 128), width)]

    r_pair = slot(1, 4)

    def forward(by, bz, part, target, recv):
        view = block(by, bz, part)
        copy(view, view, target, recv)

    def share(by, bz, part):
        forward(by, bz, part, partner, r_pair + mod4(bz))

    r_z1 = slot(1, 4)
    r_z2 = slot(1, 2)
    r_y1 = slot(1, 12)
    r_y2 = slot(1, 6)
    r_y3 = slot(1, 6)

    def column(number):
        return zh + sign * (0, -1, 1)[number]

    def send_y1(number, part):
        first = r_y1 + 4 * number + (0 if part == "a" else 2)
        forward(y, column(number), part, y_fwd, first)
        forward(y, column(number), part, y_bwd, first + 1)

    def take_y1(number):
        bz = column(number)
        first = r_y1 + 4 * number
        await_bytes(block(y - sign, bz, "a"), first)
        forward(y - sign, bz, "a", y_fwd, r_y2 + 2 * number)
        await_bytes(block(y + sign, bz, "b"), first + 3)
        forward(y + sign, bz, "b", y_bwd, r_y2 + 2 * number + 1)
        await_bytes(block(y - sign, bz, "b"), first + 2)
        share(y - sign, bz, "all")
        await_bytes(block(y + sign, bz, "a"), first + 1)
        share(y + sign, bz, "all")

    def take_y2(number):
        bz = column(number)
        await_bytes(block(y + 2, bz, "a"), r_y2 + 2 * number)
        share(y + 2, bz, "a")
        await_bytes(block(y + 2, bz, "b"), r_y2 + 2 * number + 1)
        share(y + 2, bz, "b")

    def send_y3(part):
        first = r_y3 + (0 if part == "a" else 3)
        forward(y, zh + 2, part, y_fwd, first)
        forward(y, zh + 2, part, y_bwd, first + 1)
        forward(y, zh + 2, part, y_far, first + 2)
        share(y, zh + 2, part)

    def take_y3(part):
        first = r_y3 + (0 if part == "a" else 3)
        for offset, by in enumerate((y - sign, y + sign, y + 2)):
            await_bytes(block(by, zh + 2, part), first + offset)
            share(by, zh + 2, part)

    await_bytes(stage.at[other_rows, pl.ds(pl.multiple_of(other * TILE, 128), 512)], r_swap)
    block(y, zh, "a")[...] = stage[:, pl.ds(pl.multiple_of(other * PART_B, 128), PART_A)].astype(BF16)
    forward(y, zh, "a", z_fwd, r_z1)
    forward(y, zh, "a", z_bwd, r_z1 + 3)
    send_y1(0, "a")

    @pl.when(jnp.logical_and(c == 0, g > 0))
    def _():
        await_bytes(stage.at[0:COLS, 0:TILE], r_left)
        await_bytes(stage.at[COLS:PAIR, 0:TILE], r_left + 1)

    @pl.when(jnp.logical_and(c == 1, g < 15))
    def _():
        await_bytes(stage.at[0:COLS, 512:HALF], r_right)
        await_bytes(stage.at[COLS:PAIR, 512:HALF], r_right + 1)

    block(y, zh, "b")[...] = stage[:, pl.ds(pl.multiple_of(c * PART_A, 128), PART_B)].astype(BF16)
    forward(y, zh, "b", z_bwd, r_z1 + 1)
    forward(y, zh, "b", z_fwd, r_z1 + 2)

    send_y1(0, "b")
    share(y, zh, "all")

    for load in loads[3:6]:
        load.wait()
    for tile in range(8):
        dense = adj[tile].astype(F32)
        padded = jnp.concatenate([dense, jnp.zeros((TILE, TILE), F32)], 1)
        moved = pltpu.roll(padded, off[tile] - tile * TILE, 1)
        band[tile] = (moved * live[tile].astype(F32)).astype(BF16)

    def neighbours(bz):
        col = mod4(bz)
        rows = pl.ds(pl.multiple_of(col * COLUMN, 16), COLUMN)
        await_bytes(xg.at[rows, pl.ds(pl.multiple_of(other * HALF, 128), HALF)], r_pair + col)
        for tile in range(8):
            nb[rows, tile * TILE:(tile + 1) * TILE] = lax.dot_general(
                xg[rows, tile * TILE:tile * TILE + 3 * TILE], band[tile],
                (((1,), (1,)), ((), ())), preferred_element_type=F32,
            ).astype(BF16)

    def products(bz):
        col = mod4(bz)
        rows = pl.ds(pl.multiple_of(col * COLUMN, 16), COLUMN)
        ws_t = wt[col, pl.ds(pl.multiple_of(c * 32, 16), 32), :]
        wn_t = wt[col, pl.ds(pl.multiple_of(64 + c * 32, 16), 32), :]
        pre_acc[...] += (
            jnp.dot(ws_t, xg[rows, TILE:TILE + 1024], preferred_element_type=F32)
            + jnp.dot(wn_t, nb[rows, :], preferred_element_type=F32)
        )

    take_y1(0)

    await_bytes(block(y, zh - sign, "a"), r_z1)
    forward(y, zh - sign, "a", z_fwd, r_z2)
    send_y1(1, "a")
    await_bytes(block(y, zh + sign, "a"), r_z1 + 3)
    send_y1(2, "a")

    for step in range(1, 4):
        await_bytes(wg.at[c, w_src_y * 4 + mod4(zh + step)], r_w1 + 4 - step)

    @pl.when(x != 0)
    def _():
        await_bytes(wg.at[c, w_src_y * 4 + zh], r_w1)

    r_w2 = slot(1, 2)
    part_w = wg.at[c, pl.ds(w_src_y * 4, 4)]
    copy(part_w, part_w, partner, r_w2 + c)
    for step in range(1, 4):
        for core in range(2):
            copy(part_w, part_w, device(g - x + mod4(x + step), p, core), r_w2 + c)

    take_y2(0)
    await_bytes(block(y, zh + sign, "b"), r_z1 + 1)
    forward(y, zh + sign, "b", z_bwd, r_z2 + 1)
    send_y1(2, "b")
    await_bytes(block(y, zh - sign, "b"), r_z1 + 2)
    send_y1(1, "b")
    share(y, zh - sign, "all")
    share(y, zh + sign, "all")
    neighbours(zh)
    take_y1(1)
    take_y1(2)
    await_bytes(block(y, zh + 2, "a"), r_z2)
    send_y3("a")
    await_bytes(block(y, zh + 2, "b"), r_z2 + 1)
    send_y3("b")
    take_y2(2)
    take_y2(1)

    neighbours(zh - 1)
    neighbours(zh + 1)
    take_y3("a")
    take_y3("b")

    await_bytes(wg.at[other], r_w2 + other)
    await_bytes(wg.at[c, 0:12], r_w2 + c)
    for col in range(4):
        rows = []
        for row in range(4):
            for core in range(2):
                rows.append(wg[core, row * 4 + col].astype(F32)[0:COLS])
        wt[col] = jnp.concatenate(rows, 0).T.astype(BF16)
    loads[6].wait()
    spot = lax.broadcasted_iota(jnp.int32, (32, 1024), 1)
    row = lax.broadcasted_iota(jnp.int32, (32, 1024), 0)
    bias_own = jnp.sum(
        jnp.where(spot == row + f * 32, jnp.broadcast_to(bias[...], (32, 1024)), 0.0),
        axis=1, keepdims=True,
    )
    pre_acc[...] = jnp.broadcast_to(bias_own, (32, 1024))
    products(zh)
    products(zh - 1)
    products(zh + 1)
    neighbours(zh + 2)
    products(zh + 2)

    loads[7].wait()
    pre = pre_acc[...]
    gate = jax.nn.sigmoid(pre)
    act = pre * gate
    hid[...] = act.astype(BF16)
    delta = (act - tgt[...].astype(F32)) * (gate * (1.0 + pre * (1.0 - gate))) * (1.0 / 128.0)

    head = delta.astype(BF16)
    rest = (delta - head.astype(F32)).astype(BF16)
    both = jnp.concatenate([head] * 4 + [rest] * 4, 0)
    turn = (((1,), (1,)), ((), ()))
    bias_term = jnp.sum(delta, axis=1, keepdims=True)
    quarter = lax.div(lax.broadcasted_iota(jnp.int32, (PAIR, 128), 1), 32)
    blank = jnp.zeros((16, 128), F32)

    def with_bias(tile, low_total, high_total):
        lane_of = lax.broadcasted_iota(jnp.int32, tile.shape, 1)
        bias_sum = jnp.where(lane_of < 64, low_total, high_total)
        first = bias_sum.astype(BF16).astype(F32)
        tile = jnp.where(lax.rem(lane_of, 64) == 48, first, tile)
        return jnp.where(lax.rem(lane_of, 64) == 49, bias_sum - first, tile)

    r_ra = slot(1, 4)
    for turn_of in range(1, 5):
        row = mod4(x + turn_of)
        spans = [
            pl.ds(pl.multiple_of((col * 4 + row) * PAIR, 16), PAIR) for col in range(4)
        ]
        left = jnp.concatenate(
            [xg[span, TILE:TILE + 1024] for span in spans] + [nb[span, :] for span in spans], 0
        )
        grad = lax.dot_general(left, both, turn, preferred_element_type=F32)
        grad = grad[:, 0:128] + grad[:, 128:256]

        def packed(first):
            parts = [grad[first + col * PAIR:first + (col + 1) * PAIR] for col in range(4)]
            low = jnp.where(quarter == 0, parts[0], parts[1])
            high = jnp.where(quarter == 2, parts[2], parts[3])
            return jnp.where(quarter < 2, low, high)

        own_term, nb_term = packed(0), packed(COLUMN)
        turned = jnp.concatenate(
            [own_term[0:COLS], nb_term[0:COLS], blank, own_term[COLS:PAIR], nb_term[COLS:PAIR], blank], 0
        ).T
        for col in range(4):
            tile = with_bias(turned[col * 32:(col + 1) * 32], bias_term, bias_term)
            rsend[row, col] = tile.astype(BF16)
        if turn_of < 4:
            copy(rsend.at[row], ra.at[turn_of], device(g - x + row, p, c), r_ra + turn_of)

    for turn_of in range(1, 4):
        await_bytes(ra.at[turn_of], r_ra + turn_of)

    r_rb = slot(1)
    to_group = zh * 4 + mod4(y + x)
    halves = lax.broadcasted_iota(jnp.int32, (16, 128), 1) < 64
    for step in (2, 1, 3, 0):
        col = mod4(zh + step)
        summed = (rsend[x, col].astype(F32) + ra[1, col].astype(F32)) + (
            ra[2, col].astype(F32) + ra[3, col].astype(F32)
        )
        bias_sum = summed[:, 48:49] + summed[:, 49:50]
        summed = with_bias(summed, bias_sum, bias_sum)
        top, bottom = summed[0:16], summed[16:32]
        rbs[col, 0] = jnp.where(halves, top, pltpu.roll(bottom, 64, 1)).astype(BF16)
        rbs[col, 1] = jnp.where(halves, pltpu.roll(top, 64, 1), bottom).astype(BF16)
        if step:
            for core in range(2):
                copy(rbs.at[col, core], rb.at[zl, c], device(to_group, x * 4 + col, core), r_rb)

    copy(rbs.at[zh, other], rb.at[zl, c], device(to_group, x * 4 + zh, other), r_rb)
    r_zero = remote(rbs.at[zh, c], rb.at[zl, c], device(to_group, x * 4 + zh, c), slot(0), r_rb)
    start_unless(stays, r_zero)

    @pl.when(stays)
    def _():
        pltpu.make_async_copy(rbs.at[zh, c], rb.at[zl, c], recv_sem.at[r_rb]).start()

    await_bytes(rb, r_rb)
    for core in range(2):
        total = (rb[0, core].astype(F32) + rb[1, core].astype(F32)) + (
            rb[2, core].astype(F32) + rb[3, core].astype(F32)
        )
        fg[r_chip, core] = with_bias(
            total, total[:, 48:49] + total[:, 49:50], total[:, 112:113] + total[:, 113:114]
        ).astype(BF16)

    r_r2 = slot(1, 4)
    for step in range(1, 16):
        far = lax.rem(g + step, 16)
        copy(fg.at[r_chip], fg.at[r_chip], device(far, p, c), r_r2 + mod4(x - lax.rem(far, 4)))
    for k in (0, 1, 3, 2):
        await_bytes(fg.at[0:(4 if k else 3)], r_r2 + k)
        for half in range(2):
            part = lax.rem(x - y + k + 4, 4) * 2 + half
            rows = []
            for chip in range(2):
                for core in range(2):
                    tile = fg[2 * part + chip, core].astype(F32)
                    rows += [tile, pltpu.roll(tile, 64, 1)]
            turned = jnp.concatenate(rows, 0).T
            span = pl.ds(pl.multiple_of(part * 128, 128), 128)
            gs_o[:, span] = turned[0:24]
            gn_o[:, span] = turned[24:48]
            gb_o[:, span] = turned[48:49] + turned[49:50]

    for made in sent:
        made.wait_send()

    @pl.when(g < 15)
    def _():
        halo_up.wait_send()

    @pl.when(g > 0)
    def _():
        halo_down.wait_send()

    @pl.when(x != 0)
    def _():
        w_zero.wait_send()

    @pl.when(jnp.logical_not(stays))
    def _():
        r_zero.wait_send()

    assert used[0] <= SENDS and used[1] <= RECVS, used


OUTS = (
    jax.ShapeDtypeStruct((32, 1024), BF16),
    jax.ShapeDtypeStruct((COLS, 1024), F32),
    jax.ShapeDtypeStruct((COLS, 1024), F32),
    jax.ShapeDtypeStruct((1, 1024), F32),
)


def place(hid, gs, gn, gb, hid_o, gs_o, gn_o, gb_o, sem):
    pairs = [(hid, hid_o), (gs, gs_o), (gn, gn_o), (gb, gb_o)]
    moves = [pltpu.make_async_copy(src, dst, sem.at[i]) for i, (src, dst) in enumerate(pairs)]
    for move in moves:
        move.start()
    for move in moves:
        move.wait()


def shards(features, adjacency, offsets, live, w_self, w_neigh, bias, targets):
    vmem = pl.BlockSpec(memory_space=pltpu.VMEM)
    hbm = pl.BlockSpec(memory_space=pltpu.HBM)
    inputs = [features.T, adjacency, offsets, live, w_self, w_neigh, bias.reshape(1, 1024), targets]
    results = pl.pallas_call(
        kernel,
        out_shape=OUTS,
        in_specs=[hbm] * 8,
        out_specs=(vmem,) * 4,
        scratch_shapes=[
            pltpu.VMEM((COLS, 1024), BF16),
            pltpu.VMEM((8, TILE, 256), BF16),
            pltpu.SMEM((8,), jnp.int32),
            pltpu.SMEM((8,), jnp.int32),
            pltpu.VMEM((COLS, 1024), BF16),
            pltpu.VMEM((COLS, 1024), BF16),
            pltpu.VMEM((1, 1024), F32),
            pltpu.VMEM((32, 1024), BF16),
            pltpu.VMEM((COLS, 1024), F32),
            pltpu.VMEM((PAIR, HALF), F32),
            pltpu.VMEM((768, 1280), BF16),
            pltpu.VMEM((768, 1024), BF16),
            pltpu.VMEM((8, TILE, 384), BF16),
            pltpu.VMEM((16, 32, 128), BF16),
            pltpu.VMEM((2, 16, 32, 128), BF16),
            pltpu.VMEM((4, 128, COLUMN), BF16),
            pltpu.VMEM((32, 1024), F32),
            pltpu.VMEM((4, 4, 32, 128), BF16),
            pltpu.VMEM((4, 4, 32, 128), BF16),
            pltpu.VMEM((4, 2, 16, 128), BF16),
            pltpu.VMEM((4, 2, 16, 128), BF16),
            pltpu.VMEM((16, 2, 16, 128), BF16),
            pltpu.SemaphoreType.DMA((8,)),
            pltpu.SemaphoreType.DMA((SENDS,)),
            pltpu.SemaphoreType.DMA((RECVS,)),
        ],
        compiler_params=pltpu.CompilerParams(
            collective_id=0, has_side_effects=True, vmem_limit_bytes=48 * 1024 * 1024
        ),
        cost_estimate=pl.CostEstimate(flops=10**9, bytes_accessed=10**7, transcendentals=32768),
    )(*[pltpu.with_memory_space_constraint(array, pltpu.HBM) for array in inputs])
    hidden, grad_self, grad_neigh, grad_bias = pl.pallas_call(
        place,
        out_shape=OUTS,
        in_specs=[vmem] * 4,
        out_specs=(pl.BlockSpec(memory_space=pl.ANY),) * 4,
        scratch_shapes=[pltpu.SemaphoreType.DMA((4,))],
        compiler_params=pltpu.CompilerParams(vmem_limit_bytes=1024 * 1024),
    )(*[pltpu.with_memory_space_constraint(array, pltpu.VMEM) for array in results])
    return hidden, grad_self, grad_neigh, grad_bias.reshape(1024)


def solution(mesh):
    in_specs = (
        P("grp", "feat"),
        P("grp", None, None),
        P("grp"),
        P("grp"),
        P("feat", None),
        P("feat", None),
        P(),
        P("feat", "grp"),
    )
    out_specs = (P("feat", "grp"), P("feat", None), P("feat", None), P())
    return jax.shard_map(shards, mesh=mesh, in_specs=in_specs, out_specs=out_specs, check_vma=False)
```

```python
import jax
import jax.numpy as jnp
from jax import lax
from jax.experimental import pallas as pl
from jax.experimental.pallas import tpu as pltpu
from jax.sharding import PartitionSpec as P

F32 = jnp.float32
BF16 = jnp.bfloat16
MESH = pl.DeviceIdType.MESH

COLS = 24
PAIR = 48
COLUMN = 4 * PAIR
HALF = 640
PART_A = 384
PART_B = HALF - PART_A
TILE = 128
SENDS = 96
RECVS = 72


def mod4(value):
    return lax.rem(value + 4, 4)


def kernel(
    feat_h, adj_h, off_h, live_h, ws_h, wn_h, bias_h, tgt_h,
    hid, gs_o, gn_o, gb_o,
    feat, adj, off, live, ws, wn, bias, tgt,
    wide, stage, xg, nb, band, wsend, wg, wt, pre_acc, rsend, ra, rbs, rb, fg,
    in_sem, send_sem, recv_sem,
):
    loads = [
        pltpu.make_async_copy(src, dst, in_sem.at[i])
        for i, (src, dst) in enumerate(
            [(feat_h, feat), (ws_h, ws), (wn_h, wn), (adj_h, adj), (off_h, off), (live_h, live),
             (bias_h, bias), (tgt_h, tgt)]
        )
    ]
    for load in loads:
        load.start()

    g = lax.axis_index("grp")
    f = lax.axis_index("feat")
    c = lax.rem(f, 2)
    p = lax.div(f, 2)
    y = lax.div(p, 4)
    zh = lax.rem(p, 4)
    x = lax.rem(g, 4)
    zl = lax.div(g, 4)
    other = 1 - c
    sign = 1 - 2 * c

    def device(group, chip, core):
        return (group, chip * 2 + core)

    partner = device(g, p, other)
    y_fwd = device(g, mod4(y + sign) * 4 + zh, c)
    y_bwd = device(g, mod4(y - sign) * 4 + zh, c)
    y_far = device(g, mod4(y + 2) * 4 + zh, c)
    z_fwd = device(g, y * 4 + mod4(zh + sign), c)
    z_bwd = device(g, y * 4 + mod4(zh - sign), c)
    stays = jnp.logical_and(zh == zl, jnp.logical_and(x == 0, y == 0))

    barrier = pltpu.get_barrier_semaphore()

    def tell(target):
        pl.semaphore_signal(barrier, inc=1, device_id=target, device_id_type=MESH)

    @pl.when(jnp.logical_and(c == 0, g > 0))
    def _():
        tell(device(g - 1, p, 0))
        tell(device(g - 1, p, 1))

    @pl.when(jnp.logical_and(c == 1, g < 15))
    def _():
        tell(device(g + 1, p, 0))
        tell(device(g + 1, p, 1))

    for target in (z_fwd, z_bwd, y_fwd, y_bwd, y_far, partner):
        tell(target)

    w_src_y = mod4(y + x)
    w_dst_y = mod4(y - x)
    r_chip = mod4(x - y) * 4 + zl
    for step in range(1, 4):
        tell(device(g, w_src_y * 4 + mod4(zh + step), c))
        tell(device(g - x + mod4(x + step), p, other))
        tell(device(mod4(zl + step) * 4 + y, r_chip, 0))
        tell(device(mod4(zl + step) * 4 + y, r_chip, 1))

    @pl.when(x != 0)
    def _():
        tell(device(g, w_src_y * 4 + zh, c))

    tell(device(zl * 4 + y, r_chip, other))

    @pl.when(jnp.logical_not(stays))
    def _():
        tell(device(zl * 4 + y, r_chip, c))

    def tell_far(step, carry):
        tell(device(lax.rem(g + step, 16), p, c))
        return carry

    lax.fori_loop(1, 16, tell_far, 0)

    loads[0].wait()
    wide[...] = feat[...].astype(F32)

    @pl.when(c == 0)
    def _():
        stage[0:COLS, TILE:HALF] = wide[:, 0:512]

        @pl.when(g == 0)
        def _():
            stage[:, 0:TILE] = jnp.zeros((PAIR, TILE), F32)

    @pl.when(c == 1)
    def _():
        stage[COLS:PAIR, 0:512] = wide[:, 512:1024]

        @pl.when(g == 15)
        def _():
            stage[:, 512:HALF] = jnp.zeros((PAIR, TILE), F32)

    waits = (
        6 + 3 + 7 + 15 + 3
        + (x != 0).astype(jnp.int32)
        + jnp.logical_not(stays).astype(jnp.int32)
        + (g < 15).astype(jnp.int32)
        + (g > 0).astype(jnp.int32)
    )
    pl.semaphore_wait(barrier, waits)

    used = [0, 0]
    sent = []

    def slot(which, count=1):
        used[which] += count
        return used[which] - count

    def remote(src, dst, target, send, recv):
        return pltpu.make_async_remote_copy(
            src_ref=src, dst_ref=dst, send_sem=send_sem.at[send], recv_sem=recv_sem.at[recv],
            device_id=target, device_id_type=MESH,
        )

    def copy(src, dst, target, recv):
        made = remote(src, dst, target, slot(0), recv)
        made.start()
        sent.append(made)

    def start_unless(skip, made):
        @pl.when(jnp.logical_not(skip))
        def _():
            made.start()

    def drain(first, last):
        for made in sent[first:last]:
            made.wait_send()

    def await_bytes(ref, recv):
        pltpu.make_async_copy(ref, ref, recv_sem.at[recv]).wait()

    own_rows = pl.ds(pl.multiple_of(c * COLS, 8), COLS)
    other_rows = pl.ds(pl.multiple_of(other * COLS, 8), COLS)
    r_left, r_right, r_swap = slot(1, 2), slot(1, 2), slot(1)
    halo_up = remote(
        wide.at[:, 896:1024], stage.at[own_rows, 0:TILE], device(g + 1, p, 0), slot(0), r_left + c
    )
    halo_down = remote(
        wide.at[:, 0:TILE], stage.at[own_rows, 512:HALF], device(g - 1, p, 1), slot(0), r_right + c
    )

    @pl.when(g < 15)
    def _():
        halo_up.start()

    @pl.when(g > 0)
    def _():
        halo_down.start()

    copy(
        wide.at[:, pl.ds(pl.multiple_of(other * 512, 128), 512)],
        stage.at[own_rows, pl.ds(pl.multiple_of(c * TILE, 128), 512)],
        partner, r_swap,
    )

    loads[1].wait()
    loads[2].wait()
    lane = lax.broadcasted_iota(jnp.int32, (COLS, 128), 1)
    pad = jnp.zeros((32 - COLS, 128), F32)
    for pair in range(8):
        s_tile = ws[:, pair * 128:(pair + 1) * 128].astype(F32)
        n_tile = wn[:, pair * 128:(pair + 1) * 128].astype(F32)
        low = jnp.where(lane < 64, s_tile, pltpu.roll(n_tile, 64, 1))
        high = jnp.where(lane < 64, pltpu.roll(s_tile, 64, 1), n_tile)
        wsend[2 * pair] = jnp.concatenate([low, pad], 0).astype(BF16)
        wsend[2 * pair + 1] = jnp.concatenate([high, pad], 0).astype(BF16)

    r_w1 = slot(1, 4)
    for step in range(1, 4):
        chip = w_dst_y * 4 + mod4(zh + step)
        copy(wsend.at[chip], wg.at[c, p], device(g, chip, c), r_w1 + step)
    chip0 = w_dst_y * 4 + zh
    w_zero = remote(wsend.at[chip0], wg.at[c, p], device(g, chip0, c), slot(0), r_w1)

    @pl.when(x != 0)
    def _():
        w_zero.start()

    @pl.when(x == 0)
    def _():
        wg[c, p] = wsend[chip0]

    def block(by, bz, part):
        rows = pl.ds(pl.multiple_of((mod4(bz) * 4 + mod4(by)) * PAIR, 16), PAIR)
        start = {"all": 0, "a": other * PART_B, "b": c * PART_A}[part]
        width = {"all": HALF, "a": PART_A, "b": PART_B}[part]
        return xg.at[rows, pl.ds(pl.multiple_of(c * HALF + start, 128), width)]

    r_pair = slot(1, 4)

    def forward(by, bz, part, target, recv):
        view = block(by, bz, part)
        copy(view, view, target, recv)

    def share(by, bz, part):
        forward(by, bz, part, partner, r_pair + mod4(bz))

    r_z1 = slot(1, 4)
    r_z2 = slot(1, 2)
    r_y1 = slot(1, 12)
    r_y2 = slot(1, 6)
    r_y3 = slot(1, 6)

    def column(number):
        return zh + sign * (0, -1, 1)[number]

    def send_y1(number, part):
        first = r_y1 + 4 * number + (0 if part == "a" else 2)
        forward(y, column(number), part, y_fwd, first)
        forward(y, column(number), part, y_bwd, first + 1)

    def take_y1(number):
        bz = column(number)
        first = r_y1 + 4 * number
        await_bytes(block(y - sign, bz, "a"), first)
        forward(y - sign, bz, "a", y_fwd, r_y2 + 2 * number)
        await_bytes(block(y + sign, bz, "b"), first + 3)
        forward(y + sign, bz, "b", y_bwd, r_y2 + 2 * number + 1)
        await_bytes(block(y - sign, bz, "b"), first + 2)
        share(y - sign, bz, "all")
        await_bytes(block(y + sign, bz, "a"), first + 1)
        share(y + sign, bz, "all")

    def take_y2(number):
        bz = column(number)
        await_bytes(block(y + 2, bz, "a"), r_y2 + 2 * number)
        share(y + 2, bz, "a")
        await_bytes(block(y + 2, bz, "b"), r_y2 + 2 * number + 1)
        share(y + 2, bz, "b")

    def send_y3(part):
        first = r_y3 + (0 if part == "a" else 3)
        forward(y, zh + 2, part, y_fwd, first)
        forward(y, zh + 2, part, y_bwd, first + 1)
        forward(y, zh + 2, part, y_far, first + 2)
        share(y, zh + 2, part)

    def take_y3(part):
        first = r_y3 + (0 if part == "a" else 3)
        for offset, by in enumerate((y - sign, y + sign, y + 2)):
            await_bytes(block(by, zh + 2, part), first + offset)
            share(by, zh + 2, part)

    await_bytes(stage.at[other_rows, pl.ds(pl.multiple_of(other * TILE, 128), 512)], r_swap)
    block(y, zh, "a")[...] = stage[:, pl.ds(pl.multiple_of(other * PART_B, 128), PART_A)].astype(BF16)
    forward(y, zh, "a", z_fwd, r_z1)
    forward(y, zh, "a", z_bwd, r_z1 + 3)
    send_y1(0, "a")

    @pl.when(jnp.logical_and(c == 0, g > 0))
    def _():
        await_bytes(stage.at[0:COLS, 0:TILE], r_left)
        await_bytes(stage.at[COLS:PAIR, 0:TILE], r_left + 1)

    @pl.when(jnp.logical_and(c == 1, g < 15))
    def _():
        await_bytes(stage.at[0:COLS, 512:HALF], r_right)
        await_bytes(stage.at[COLS:PAIR, 512:HALF], r_right + 1)

    block(y, zh, "b")[...] = stage[:, pl.ds(pl.multiple_of(c * PART_A, 128), PART_B)].astype(BF16)
    forward(y, zh, "b", z_bwd, r_z1 + 1)
    forward(y, zh, "b", z_fwd, r_z1 + 2)

    send_y1(0, "b")
    share(y, zh, "all")

    for load in loads[3:6]:
        load.wait()
    for tile in range(8):
        dense = adj[tile].astype(F32)
        padded = jnp.concatenate([dense, jnp.zeros((TILE, TILE), F32)], 1)
        moved = pltpu.roll(padded, off[tile] - tile * TILE, 1)
        band[tile] = (moved * live[tile].astype(F32)).astype(BF16)

    def neighbours(bz):
        col = mod4(bz)
        rows = pl.ds(pl.multiple_of(col * COLUMN, 16), COLUMN)
        await_bytes(xg.at[rows, pl.ds(pl.multiple_of(other * HALF, 128), HALF)], r_pair + col)
        for tile in range(8):
            nb[rows, tile * TILE:(tile + 1) * TILE] = lax.dot_general(
                xg[rows, tile * TILE:tile * TILE + 3 * TILE], band[tile],
                (((1,), (1,)), ((), ())), preferred_element_type=F32,
            ).astype(BF16)

    def products(bz):
        col = mod4(bz)
        rows = pl.ds(pl.multiple_of(col * COLUMN, 16), COLUMN)
        ws_t = wt[col, pl.ds(pl.multiple_of(c * 32, 16), 32), :]
        wn_t = wt[col, pl.ds(pl.multiple_of(64 + c * 32, 16), 32), :]
        pre_acc[...] += (
            jnp.dot(ws_t, xg[rows, TILE:TILE + 1024], preferred_element_type=F32)
            + jnp.dot(wn_t, nb[rows, :], preferred_element_type=F32)
        )

    take_y1(0)

    await_bytes(block(y, zh - sign, "a"), r_z1)
    forward(y, zh - sign, "a", z_fwd, r_z2)
    send_y1(1, "a")
    await_bytes(block(y, zh + sign, "a"), r_z1 + 3)
    send_y1(2, "a")

    for step in range(1, 4):
        await_bytes(wg.at[c, w_src_y * 4 + mod4(zh + step)], r_w1 + 4 - step)

    @pl.when(x != 0)
    def _():
        await_bytes(wg.at[c, w_src_y * 4 + zh], r_w1)

    r_w2 = slot(1, 2)
    part_w = wg.at[c, pl.ds(w_src_y * 4, 4)]
    copy(part_w, part_w, partner, r_w2 + c)
    for step in range(1, 4):
        for core in range(2):
            copy(part_w, part_w, device(g - x + mod4(x + step), p, core), r_w2 + c)

    take_y2(0)
    await_bytes(block(y, zh + sign, "b"), r_z1 + 1)
    forward(y, zh + sign, "b", z_bwd, r_z2 + 1)
    send_y1(2, "b")
    await_bytes(block(y, zh - sign, "b"), r_z1 + 2)
    send_y1(1, "b")
    share(y, zh - sign, "all")
    share(y, zh + sign, "all")
    neighbours(zh)
    take_y1(1)
    take_y1(2)
    await_bytes(block(y, zh + 2, "a"), r_z2)
    send_y3("a")
    await_bytes(block(y, zh + 2, "b"), r_z2 + 1)
    send_y3("b")
    take_y2(2)
    take_y2(1)

    neighbours(zh - 1)
    neighbours(zh + 1)
    take_y3("a")
    take_y3("b")

    await_bytes(wg.at[other], r_w2 + other)
    await_bytes(wg.at[c, 0:12], r_w2 + c)
    for col in range(4):
        rows = []
        for row in range(4):
            for core in range(2):
                rows.append(wg[core, row * 4 + col].astype(F32)[0:COLS])
        wt[col] = jnp.concatenate(rows, 0).T.astype(BF16)
    loads[6].wait()
    spot = lax.broadcasted_iota(jnp.int32, (32, 1024), 1)
    row = lax.broadcasted_iota(jnp.int32, (32, 1024), 0)
    bias_own = jnp.sum(
        jnp.where(spot == row + f * 32, jnp.broadcast_to(bias[...], (32, 1024)), 0.0),
        axis=1, keepdims=True,
    )
    pre_acc[...] = jnp.broadcast_to(bias_own, (32, 1024))
    products(zh)
    products(zh - 1)
    products(zh + 1)
    neighbours(zh + 2)
    products(zh + 2)

    loads[7].wait()
    pre = pre_acc[...]
    gate = jax.nn.sigmoid(pre)
    act = pre * gate
    hid[...] = act.astype(BF16)
    delta = (act - tgt[...].astype(F32)) * (gate * (1.0 + pre * (1.0 - gate))) * (1.0 / 128.0)

    head = delta.astype(BF16)
    rest = (delta - head.astype(F32)).astype(BF16)
    both = jnp.concatenate([head] * 4 + [rest] * 4, 0)
    turn = (((1,), (1,)), ((), ()))
    bias_term = jnp.sum(delta, axis=1, keepdims=True)
    quarter = lax.div(lax.broadcasted_iota(jnp.int32, (PAIR, 128), 1), 32)
    blank = jnp.zeros((16, 128), F32)

    def with_bias(tile, low_total, high_total):
        lane_of = lax.broadcasted_iota(jnp.int32, tile.shape, 1)
        bias_sum = jnp.where(lane_of < 64, low_total, high_total)
        first = bias_sum.astype(BF16).astype(F32)
        tile = jnp.where(lax.rem(lane_of, 64) == 48, first, tile)
        return jnp.where(lax.rem(lane_of, 64) == 49, bias_sum - first, tile)

    r_ra = slot(1, 4)
    for turn_of in range(1, 5):
        row = mod4(x + turn_of)
        spans = [
            pl.ds(pl.multiple_of((col * 4 + row) * PAIR, 16), PAIR) for col in range(4)
        ]
        left = jnp.concatenate(
            [xg[span, TILE:TILE + 1024] for span in spans] + [nb[span, :] for span in spans], 0
        )
        grad = lax.dot_general(left, both, turn, preferred_element_type=F32)
        grad = grad[:, 0:128] + grad[:, 128:256]

        def packed(first):
            parts = [grad[first + col * PAIR:first + (col + 1) * PAIR] for col in range(4)]
            low = jnp.where(quarter == 0, parts[0], parts[1])
            high = jnp.where(quarter == 2, parts[2], parts[3])
            return jnp.where(quarter < 2, low, high)

        own_term, nb_term = packed(0), packed(COLUMN)
        turned = jnp.concatenate(
            [own_term[0:COLS], nb_term[0:COLS], blank, own_term[COLS:PAIR], nb_term[COLS:PAIR], blank], 0
        ).T
        for col in range(4):
            tile = with_bias(turned[col * 32:(col + 1) * 32], bias_term, bias_term)
            rsend[row, col] = tile.astype(BF16)
        if turn_of < 4:
            copy(rsend.at[row], ra.at[turn_of], device(g - x + row, p, c), r_ra + turn_of)

    before_x = len(sent) - 3
    drain(0, before_x)

    @pl.when(g < 15)
    def _():
        halo_up.wait_send()

    @pl.when(g > 0)
    def _():
        halo_down.wait_send()

    @pl.when(x != 0)
    def _():
        w_zero.wait_send()

    for turn_of in range(1, 4):
        await_bytes(ra.at[turn_of], r_ra + turn_of)

    r_rb = slot(1)
    to_group = zh * 4 + mod4(y + x)
    halves = lax.broadcasted_iota(jnp.int32, (16, 128), 1) < 64
    for step in (2, 1, 3, 0):
        col = mod4(zh + step)
        summed = (rsend[x, col].astype(F32) + ra[1, col].astype(F32)) + (
            ra[2, col].astype(F32) + ra[3, col].astype(F32)
        )
        bias_sum = summed[:, 48:49] + summed[:, 49:50]
        summed = with_bias(summed, bias_sum, bias_sum)
        top, bottom = summed[0:16], summed[16:32]
        rbs[col, 0] = jnp.where(halves, top, pltpu.roll(bottom, 64, 1)).astype(BF16)
        rbs[col, 1] = jnp.where(halves, pltpu.roll(top, 64, 1), bottom).astype(BF16)
        if step:
            for core in range(2):
                copy(rbs.at[col, core], rb.at[zl, c], device(to_group, x * 4 + col, core), r_rb)

    copy(rbs.at[zh, other], rb.at[zl, c], device(to_group, x * 4 + zh, other), r_rb)
    r_zero = remote(rbs.at[zh, c], rb.at[zl, c], device(to_group, x * 4 + zh, c), slot(0), r_rb)
    start_unless(stays, r_zero)

    @pl.when(stays)
    def _():
        pltpu.make_async_copy(rbs.at[zh, c], rb.at[zl, c], recv_sem.at[r_rb]).start()

    drain(before_x, None)
    await_bytes(rb, r_rb)
    for core in range(2):
        total = (rb[0, core].astype(F32) + rb[1, core].astype(F32)) + (
            rb[2, core].astype(F32) + rb[3, core].astype(F32)
        )
        fg[r_chip, core] = with_bias(
            total, total[:, 48:49] + total[:, 49:50], total[:, 112:113] + total[:, 113:114]
        ).astype(BF16)

    r_r2, s_r2 = slot(1, 4), slot(0)
    for step in range(1, 16):
        far = lax.rem(g + step, 16)
        remote(
            fg.at[r_chip], fg.at[r_chip], device(far, p, c), s_r2, r_r2 + mod4(x - lax.rem(far, 4))
        ).start()

    @pl.when(jnp.logical_not(stays))
    def _():
        r_zero.wait_send()

    for k in (0, 1, 3, 2):
        if k == 2:
            pltpu.make_async_copy(fg.at[0:15], fg.at[0:15], send_sem.at[s_r2]).wait()
        await_bytes(fg.at[0:(4 if k else 3)], r_r2 + k)
        for half in range(2):
            part = lax.rem(x - y + k + 4, 4) * 2 + half
            rows = []
            for chip in range(2):
                for core in range(2):
                    tile = fg[2 * part + chip, core].astype(F32)
                    rows += [tile, pltpu.roll(tile, 64, 1)]
            turned = jnp.concatenate(rows, 0).T
            span = pl.ds(pl.multiple_of(part * 128, 128), 128)
            gs_o[:, span] = turned[0:24]
            gn_o[:, span] = turned[24:48]
            gb_o[:, span] = turned[48:49] + turned[49:50]

    assert used[0] <= SENDS and used[1] <= RECVS, used


OUTS = (
    jax.ShapeDtypeStruct((32, 1024), BF16),
    jax.ShapeDtypeStruct((COLS, 1024), F32),
    jax.ShapeDtypeStruct((COLS, 1024), F32),
    jax.ShapeDtypeStruct((1, 1024), F32),
)


def place(hid, gs, gn, gb, hid_o, gs_o, gn_o, gb_o, sem):
    pairs = [(hid, hid_o), (gs, gs_o), (gn, gn_o), (gb, gb_o)]
    moves = [pltpu.make_async_copy(src, dst, sem.at[i]) for i, (src, dst) in enumerate(pairs)]
    for move in moves:
        move.start()
    for move in moves:
        move.wait()


def shards(features, adjacency, offsets, live, w_self, w_neigh, bias, targets):
    vmem = pl.BlockSpec(memory_space=pltpu.VMEM)
    hbm = pl.BlockSpec(memory_space=pltpu.HBM)
    inputs = [features.T, adjacency, offsets, live, w_self, w_neigh, bias.reshape(1, 1024), targets]
    results = pl.pallas_call(
        kernel,
        out_shape=OUTS,
        in_specs=[hbm] * 8,
        out_specs=(vmem,) * 4,
        scratch_shapes=[
            pltpu.VMEM((COLS, 1024), BF16),
            pltpu.VMEM((8, TILE, 256), BF16),
            pltpu.SMEM((8,), jnp.int32),
            pltpu.SMEM((8,), jnp.int32),
            pltpu.VMEM((COLS, 1024), BF16),
            pltpu.VMEM((COLS, 1024), BF16),
            pltpu.VMEM((1, 1024), F32),
            pltpu.VMEM((32, 1024), BF16),
            pltpu.VMEM((COLS, 1024), F32),
            pltpu.VMEM((PAIR, HALF), F32),
            pltpu.VMEM((768, 1280), BF16),
            pltpu.VMEM((768, 1024), BF16),
            pltpu.VMEM((8, TILE, 384), BF16),
            pltpu.VMEM((16, 32, 128), BF16),
            pltpu.VMEM((2, 16, 32, 128), BF16),
            pltpu.VMEM((4, 128, COLUMN), BF16),
            pltpu.VMEM((32, 1024), F32),
            pltpu.VMEM((4, 4, 32, 128), BF16),
            pltpu.VMEM((4, 4, 32, 128), BF16),
            pltpu.VMEM((4, 2, 16, 128), BF16),
            pltpu.VMEM((4, 2, 16, 128), BF16),
            pltpu.VMEM((16, 2, 16, 128), BF16),
            pltpu.SemaphoreType.DMA((8,)),
            pltpu.SemaphoreType.DMA((SENDS,)),
            pltpu.SemaphoreType.DMA((RECVS,)),
        ],
        compiler_params=pltpu.CompilerParams(
            collective_id=0, has_side_effects=True, vmem_limit_bytes=48 * 1024 * 1024
        ),
        cost_estimate=pl.CostEstimate(flops=10**9, bytes_accessed=10**7, transcendentals=32768),
    )(*[pltpu.with_memory_space_constraint(array, pltpu.HBM) for array in inputs])
    hidden, grad_self, grad_neigh, grad_bias = pl.pallas_call(
        place,
        out_shape=OUTS,
        in_specs=[vmem] * 4,
        out_specs=(pl.BlockSpec(memory_space=pl.ANY),) * 4,
        scratch_shapes=[pltpu.SemaphoreType.DMA((4,))],
        compiler_params=pltpu.CompilerParams(vmem_limit_bytes=1024 * 1024),
    )(*[pltpu.with_memory_space_constraint(array, pltpu.VMEM) for array in results])
    return hidden, grad_self, grad_neigh, grad_bias.reshape(1024)


def solution(mesh):
    in_specs = (
        P("grp", "feat"),
        P("grp", None, None),
        P("grp"),
        P("grp"),
        P("feat", None),
        P("feat", None),
        P(),
        P("feat", "grp"),
    )
    out_specs = (P("feat", "grp"), P("feat", None), P("feat", None), P())
    return jax.shard_map(shards, mesh=mesh, in_specs=in_specs, out_specs=out_specs, check_vma=False)
```

```python
import jax
import jax.numpy as jnp
from jax import lax
from jax.experimental import pallas as pl
from jax.experimental.pallas import tpu as pltpu
from jax.sharding import PartitionSpec as P

F32 = jnp.float32
BF16 = jnp.bfloat16
MESH = pl.DeviceIdType.MESH

COLS = 24
PAIR = 48
COLUMN = 4 * PAIR
HALF = 640
PART_A = 384
PART_B = HALF - PART_A
TILE = 128
SENDS = 96
RECVS = 72


def mod4(value):
    return lax.rem(value + 4, 4)


def kernel(
    feat_h, adj_h, off_h, live_h, ws_h, wn_h, bias_h, tgt_h,
    hid, gs_o, gn_o, gb_o,
    feat, adj, off, live, ws, wn, bias, tgt,
    wide, stage, xg, nb, band, wsend, wg, wt, pre_acc, rsend, ra, rbs, rb, fg,
    in_sem, send_sem, recv_sem,
):
    loads = [
        pltpu.make_async_copy(src, dst, in_sem.at[i])
        for i, (src, dst) in enumerate(
            [(feat_h, feat), (ws_h, ws), (wn_h, wn), (adj_h, adj), (off_h, off), (live_h, live),
             (bias_h, bias), (tgt_h, tgt)]
        )
    ]
    for load in loads:
        load.start()

    g = lax.axis_index("grp")
    f = lax.axis_index("feat")
    c = lax.rem(f, 2)
    p = lax.div(f, 2)
    y = lax.div(p, 4)
    zh = lax.rem(p, 4)
    x = lax.rem(g, 4)
    zl = lax.div(g, 4)
    other = 1 - c
    sign = 1 - 2 * c

    def device(group, chip, core):
        return (group, chip * 2 + core)

    partner = device(g, p, other)
    y_fwd = device(g, mod4(y + sign) * 4 + zh, c)
    y_bwd = device(g, mod4(y - sign) * 4 + zh, c)
    z_fwd = device(g, y * 4 + mod4(zh + sign), c)
    z_bwd = device(g, y * 4 + mod4(zh - sign), c)
    stays = jnp.logical_and(zh == zl, jnp.logical_and(x == 0, y == 0))

    barrier = pltpu.get_barrier_semaphore()

    def tell(target):
        pl.semaphore_signal(barrier, inc=1, device_id=target, device_id_type=MESH)

    @pl.when(jnp.logical_and(c == 0, g > 0))
    def _():
        tell(device(g - 1, p, 0))
        tell(device(g - 1, p, 1))

    @pl.when(jnp.logical_and(c == 1, g < 15))
    def _():
        tell(device(g + 1, p, 0))
        tell(device(g + 1, p, 1))

    for target in (z_fwd, z_bwd, y_fwd, y_bwd, partner):
        tell(target)

    w_src_y = mod4(y + x)
    w_dst_y = mod4(y - x)
    r_chip = mod4(x - y) * 4 + zl
    for step in range(1, 4):
        tell(device(g, w_src_y * 4 + mod4(zh + step), c))
        tell(device(g - x + mod4(x + step), p, other))
        tell(device(mod4(zl + step) * 4 + y, r_chip, 0))
        tell(device(mod4(zl + step) * 4 + y, r_chip, 1))

    @pl.when(x != 0)
    def _():
        tell(device(g, w_src_y * 4 + zh, c))

    tell(device(zl * 4 + y, r_chip, other))

    @pl.when(jnp.logical_not(stays))
    def _():
        tell(device(zl * 4 + y, r_chip, c))

    def tell_far(step, carry):
        tell(device(lax.rem(g + step, 16), p, c))
        return carry

    lax.fori_loop(1, 16, tell_far, 0)

    loads[0].wait()
    wide[...] = feat[...].astype(F32)

    @pl.when(c == 0)
    def _():
        stage[0:COLS, TILE:HALF] = wide[:, 0:512]

        @pl.when(g == 0)
        def _():
            stage[:, 0:TILE] = jnp.zeros((PAIR, TILE), F32)

    @pl.when(c == 1)
    def _():
        stage[COLS:PAIR, 0:512] = wide[:, 512:1024]

        @pl.when(g == 15)
        def _():
            stage[:, 512:HALF] = jnp.zeros((PAIR, TILE), F32)

    waits = (
        5 + 3 + 7 + 15 + 3
        + (x != 0).astype(jnp.int32)
        + jnp.logical_not(stays).astype(jnp.int32)
        + (g < 15).astype(jnp.int32)
        + (g > 0).astype(jnp.int32)
    )
    pl.semaphore_wait(barrier, waits)

    used = [0, 0]
    sent = []

    def slot(which, count=1):
        used[which] += count
        return used[which] - count

    def remote(src, dst, target, send, recv):
        return pltpu.make_async_remote_copy(
            src_ref=src, dst_ref=dst, send_sem=send_sem.at[send], recv_sem=recv_sem.at[recv],
            device_id=target, device_id_type=MESH,
        )

    def copy(src, dst, target, recv):
        made = remote(src, dst, target, slot(0), recv)
        made.start()
        sent.append(made)

    def start_unless(skip, made):
        @pl.when(jnp.logical_not(skip))
        def _():
            made.start()

    def drain(first, last):
        for made in sent[first:last]:
            made.wait_send()

    def await_bytes(ref, recv):
        pltpu.make_async_copy(ref, ref, recv_sem.at[recv]).wait()

    own_rows = pl.ds(pl.multiple_of(c * COLS, 8), COLS)
    other_rows = pl.ds(pl.multiple_of(other * COLS, 8), COLS)
    r_left, r_right, r_swap = slot(1, 2), slot(1, 2), slot(1)
    halo_up = remote(
        wide.at[:, 896:1024], stage.at[own_rows, 0:TILE], device(g + 1, p, 0), slot(0), r_left + c
    )
    halo_down = remote(
        wide.at[:, 0:TILE], stage.at[own_rows, 512:HALF], device(g - 1, p, 1), slot(0), r_right + c
    )

    @pl.when(g < 15)
    def _():
        halo_up.start()

    @pl.when(g > 0)
    def _():
        halo_down.start()

    copy(
        wide.at[:, pl.ds(pl.multiple_of(other * 512, 128), 512)],
        stage.at[own_rows, pl.ds(pl.multiple_of(c * TILE, 128), 512)],
        partner, r_swap,
    )

    loads[1].wait()
    loads[2].wait()
    lane = lax.broadcasted_iota(jnp.int32, (COLS, 128), 1)
    pad = jnp.zeros((32 - COLS, 128), F32)
    for pair in range(8):
        s_tile = ws[:, pair * 128:(pair + 1) * 128].astype(F32)
        n_tile = wn[:, pair * 128:(pair + 1) * 128].astype(F32)
        low = jnp.where(lane < 64, s_tile, pltpu.roll(n_tile, 64, 1))
        high = jnp.where(lane < 64, pltpu.roll(s_tile, 64, 1), n_tile)
        wsend[2 * pair] = jnp.concatenate([low, pad], 0).astype(BF16)
        wsend[2 * pair + 1] = jnp.concatenate([high, pad], 0).astype(BF16)

    r_w1 = slot(1, 4)
    for step in range(1, 4):
        chip = w_dst_y * 4 + mod4(zh + step)
        copy(wsend.at[chip], wg.at[c, p], device(g, chip, c), r_w1 + step)
    chip0 = w_dst_y * 4 + zh
    w_zero = remote(wsend.at[chip0], wg.at[c, p], device(g, chip0, c), slot(0), r_w1)

    @pl.when(x != 0)
    def _():
        w_zero.start()

    @pl.when(x == 0)
    def _():
        wg[c, p] = wsend[chip0]

    def block(by, bz, part):
        rows = pl.ds(pl.multiple_of((mod4(bz) * 4 + mod4(by)) * PAIR, 16), PAIR)
        start = {"all": 0, "a": other * PART_B, "b": c * PART_A}[part]
        width = {"all": HALF, "a": PART_A, "b": PART_B}[part]
        return xg.at[rows, pl.ds(pl.multiple_of(c * HALF + start, 128), width)]

    r_pair = slot(1, 4)

    def forward(by, bz, part, target, recv):
        view = block(by, bz, part)
        copy(view, view, target, recv)

    def share(by, bz, part):
        forward(by, bz, part, partner, r_pair + mod4(bz))

    r_z1 = slot(1, 4)
    r_z2 = slot(1, 2)
    r_y1 = slot(1, 16)
    r_y2 = slot(1, 8)

    def column(number):
        return zh + 2 if number == 3 else zh + sign * (0, -1, 1)[number]

    def send_y1(number, part):
        first = r_y1 + 4 * number + (0 if part == "a" else 2)
        forward(y, column(number), part, y_fwd, first)
        forward(y, column(number), part, y_bwd, first + 1)

    def take_y1(number):
        bz = column(number)
        first = r_y1 + 4 * number
        await_bytes(block(y - sign, bz, "a"), first)
        forward(y - sign, bz, "a", y_fwd, r_y2 + 2 * number)
        await_bytes(block(y + sign, bz, "b"), first + 3)
        forward(y + sign, bz, "b", y_bwd, r_y2 + 2 * number + 1)
        await_bytes(block(y - sign, bz, "b"), first + 2)
        share(y - sign, bz, "all")
        await_bytes(block(y + sign, bz, "a"), first + 1)
        share(y + sign, bz, "all")

    def take_y2(number):
        bz = column(number)
        await_bytes(block(y + 2, bz, "a"), r_y2 + 2 * number)
        share(y + 2, bz, "a")
        await_bytes(block(y + 2, bz, "b"), r_y2 + 2 * number + 1)
        share(y + 2, bz, "b")

    await_bytes(stage.at[other_rows, pl.ds(pl.multiple_of(other * TILE, 128), 512)], r_swap)
    block(y, zh, "a")[...] = stage[:, pl.ds(pl.multiple_of(other * PART_B, 128), PART_A)].astype(BF16)
    forward(y, zh, "a", z_fwd, r_z1)
    forward(y, zh, "a", z_bwd, r_z1 + 3)
    send_y1(0, "a")

    @pl.when(jnp.logical_and(c == 0, g > 0))
    def _():
        await_bytes(stage.at[0:COLS, 0:TILE], r_left)
        await_bytes(stage.at[COLS:PAIR, 0:TILE], r_left + 1)

    @pl.when(jnp.logical_and(c == 1, g < 15))
    def _():
        await_bytes(stage.at[0:COLS, 512:HALF], r_right)
        await_bytes(stage.at[COLS:PAIR, 512:HALF], r_right + 1)

    block(y, zh, "b")[...] = stage[:, pl.ds(pl.multiple_of(c * PART_A, 128), PART_B)].astype(BF16)
    forward(y, zh, "b", z_bwd, r_z1 + 1)
    forward(y, zh, "b", z_fwd, r_z1 + 2)

    send_y1(0, "b")
    share(y, zh, "all")

    for load in loads[3:6]:
        load.wait()
    for tile in range(8):
        dense = adj[tile].astype(F32)
        padded = jnp.concatenate([dense, jnp.zeros((TILE, TILE), F32)], 1)
        moved = pltpu.roll(padded, off[tile] - tile * TILE, 1)
        band[tile] = (moved * live[tile].astype(F32)).astype(BF16)

    def neighbours(bz):
        col = mod4(bz)
        rows = pl.ds(pl.multiple_of(col * COLUMN, 16), COLUMN)
        await_bytes(xg.at[rows, pl.ds(pl.multiple_of(other * HALF, 128), HALF)], r_pair + col)
        for tile in range(8):
            nb[rows, tile * TILE:(tile + 1) * TILE] = lax.dot_general(
                xg[rows, tile * TILE:tile * TILE + 3 * TILE], band[tile],
                (((1,), (1,)), ((), ())), preferred_element_type=F32,
            ).astype(BF16)

    def products(bz):
        col = mod4(bz)
        rows = pl.ds(pl.multiple_of(col * COLUMN, 16), COLUMN)
        ws_t = wt[col, pl.ds(pl.multiple_of(c * 32, 16), 32), :]
        wn_t = wt[col, pl.ds(pl.multiple_of(64 + c * 32, 16), 32), :]
        pre_acc[...] += (
            jnp.dot(ws_t, xg[rows, TILE:TILE + 1024], preferred_element_type=F32)
            + jnp.dot(wn_t, nb[rows, :], preferred_element_type=F32)
        )

    take_y1(0)

    await_bytes(block(y, zh - sign, "a"), r_z1)
    forward(y, zh - sign, "a", z_fwd, r_z2)
    send_y1(1, "a")
    await_bytes(block(y, zh + sign, "a"), r_z1 + 3)
    send_y1(2, "a")

    for step in range(1, 4):
        await_bytes(wg.at[c, w_src_y * 4 + mod4(zh + step)], r_w1 + 4 - step)

    @pl.when(x != 0)
    def _():
        await_bytes(wg.at[c, w_src_y * 4 + zh], r_w1)

    r_w2 = slot(1, 2)
    part_w = wg.at[c, pl.ds(w_src_y * 4, 4)]
    copy(part_w, part_w, partner, r_w2 + c)
    for step in range(1, 4):
        for core in range(2):
            copy(part_w, part_w, device(g - x + mod4(x + step), p, core), r_w2 + c)

    take_y2(0)
    await_bytes(block(y, zh + sign, "b"), r_z1 + 1)
    forward(y, zh + sign, "b", z_bwd, r_z2 + 1)
    send_y1(2, "b")
    await_bytes(block(y, zh - sign, "b"), r_z1 + 2)
    send_y1(1, "b")
    share(y, zh - sign, "all")
    share(y, zh + sign, "all")
    neighbours(zh)
    take_y1(1)
    take_y1(2)
    await_bytes(block(y, zh + 2, "a"), r_z2)
    send_y1(3, "a")
    await_bytes(block(y, zh + 2, "b"), r_z2 + 1)
    send_y1(3, "b")
    share(y, zh + 2, "all")
    take_y2(2)
    take_y2(1)
    neighbours(zh - 1)
    take_y1(3)
    neighbours(zh + 1)
    take_y2(3)

    await_bytes(wg.at[other], r_w2 + other)
    await_bytes(wg.at[c, 0:12], r_w2 + c)
    for col in range(4):
        rows = []
        for row in range(4):
            for core in range(2):
                rows.append(wg[core, row * 4 + col].astype(F32)[0:COLS])
        wt[col] = jnp.concatenate(rows, 0).T.astype(BF16)
    loads[6].wait()
    spot = lax.broadcasted_iota(jnp.int32, (32, 1024), 1)
    row = lax.broadcasted_iota(jnp.int32, (32, 1024), 0)
    bias_own = jnp.sum(
        jnp.where(spot == row + f * 32, jnp.broadcast_to(bias[...], (32, 1024)), 0.0),
        axis=1, keepdims=True,
    )
    pre_acc[...] = jnp.broadcast_to(bias_own, (32, 1024))
    products(zh)
    products(zh - 1)
    products(zh + 1)
    neighbours(zh + 2)
    products(zh + 2)

    loads[7].wait()
    pre = pre_acc[...]
    gate = jax.nn.sigmoid(pre)
    act = pre * gate
    hid[...] = act.astype(BF16)
    delta = (act - tgt[...].astype(F32)) * (gate * (1.0 + pre * (1.0 - gate))) * (1.0 / 128.0)

    head = delta.astype(BF16)
    rest = (delta - head.astype(F32)).astype(BF16)
    both = jnp.concatenate([head] * 4 + [rest] * 4, 0)
    turn = (((1,), (1,)), ((), ()))
    bias_term = jnp.sum(delta, axis=1, keepdims=True)
    quarter = lax.div(lax.broadcasted_iota(jnp.int32, (PAIR, 128), 1), 32)
    blank = jnp.zeros((16, 128), F32)

    def with_bias(tile, low_total, high_total):
        lane_of = lax.broadcasted_iota(jnp.int32, tile.shape, 1)
        bias_sum = jnp.where(lane_of < 64, low_total, high_total)
        first = bias_sum.astype(BF16).astype(F32)
        tile = jnp.where(lax.rem(lane_of, 64) == 48, first, tile)
        return jnp.where(lax.rem(lane_of, 64) == 49, bias_sum - first, tile)

    r_ra = slot(1, 4)
    for turn_of in range(1, 5):
        row = mod4(x + turn_of)
        spans = [
            pl.ds(pl.multiple_of((col * 4 + row) * PAIR, 16), PAIR) for col in range(4)
        ]
        left = jnp.concatenate(
            [xg[span, TILE:TILE + 1024] for span in spans] + [nb[span, :] for span in spans], 0
        )
        grad = lax.dot_general(left, both, turn, preferred_element_type=F32)
        grad = grad[:, 0:128] + grad[:, 128:256]

        def packed(first):
            parts = [grad[first + col * PAIR:first + (col + 1) * PAIR] for col in range(4)]
            low = jnp.where(quarter == 0, parts[0], parts[1])
            high = jnp.where(quarter == 2, parts[2], parts[3])
            return jnp.where(quarter < 2, low, high)

        own_term, nb_term = packed(0), packed(COLUMN)
        turned = jnp.concatenate(
            [own_term[0:COLS], nb_term[0:COLS], blank, own_term[COLS:PAIR], nb_term[COLS:PAIR], blank], 0
        ).T
        for col in range(4):
            tile = with_bias(turned[col * 32:(col + 1) * 32], bias_term, bias_term)
            rsend[row, col] = tile.astype(BF16)
        if turn_of < 4:
            copy(rsend.at[row], ra.at[turn_of], device(g - x + row, p, c), r_ra + turn_of)

    before_x = len(sent) - 3
    drain(0, before_x)

    @pl.when(g < 15)
    def _():
        halo_up.wait_send()

    @pl.when(g > 0)
    def _():
        halo_down.wait_send()

    @pl.when(x != 0)
    def _():
        w_zero.wait_send()

    for turn_of in range(1, 4):
        await_bytes(ra.at[turn_of], r_ra + turn_of)

    r_rb = slot(1)
    to_group = zh * 4 + mod4(y + x)
    halves = lax.broadcasted_iota(jnp.int32, (16, 128), 1) < 64
    for step in (2, 1, 3, 0):
        col = mod4(zh + step)
        summed = (rsend[x, col].astype(F32) + ra[1, col].astype(F32)) + (
            ra[2, col].astype(F32) + ra[3, col].astype(F32)
        )
        bias_sum = summed[:, 48:49] + summed[:, 49:50]
        summed = with_bias(summed, bias_sum, bias_sum)
        top, bottom = summed[0:16], summed[16:32]
        rbs[col, 0] = jnp.where(halves, top, pltpu.roll(bottom, 64, 1)).astype(BF16)
        rbs[col, 1] = jnp.where(halves, pltpu.roll(top, 64, 1), bottom).astype(BF16)
        if step:
            for core in range(2):
                copy(rbs.at[col, core], rb.at[zl, c], device(to_group, x * 4 + col, core), r_rb)

    copy(rbs.at[zh, other], rb.at[zl, c], device(to_group, x * 4 + zh, other), r_rb)
    r_zero = remote(rbs.at[zh, c], rb.at[zl, c], device(to_group, x * 4 + zh, c), slot(0), r_rb)
    start_unless(stays, r_zero)

    @pl.when(stays)
    def _():
        pltpu.make_async_copy(rbs.at[zh, c], rb.at[zl, c], recv_sem.at[r_rb]).start()

    drain(before_x, None)
    await_bytes(rb, r_rb)
    for core in range(2):
        total = (rb[0, core].astype(F32) + rb[1, core].astype(F32)) + (
            rb[2, core].astype(F32) + rb[3, core].astype(F32)
        )
        fg[r_chip, core] = with_bias(
            total, total[:, 48:49] + total[:, 49:50], total[:, 112:113] + total[:, 113:114]
        ).astype(BF16)

    r_r2, s_r2 = slot(1, 4), slot(0)
    for step in range(1, 16):
        far = lax.rem(g + step, 16)
        remote(
            fg.at[r_chip], fg.at[r_chip], device(far, p, c), s_r2, r_r2 + mod4(x - lax.rem(far, 4))
        ).start()

    @pl.when(jnp.logical_not(stays))
    def _():
        r_zero.wait_send()

    for k in (0, 1, 3, 2):
        if k == 2:
            pltpu.make_async_copy(fg.at[0:15], fg.at[0:15], send_sem.at[s_r2]).wait()
        await_bytes(fg.at[0:(4 if k else 3)], r_r2 + k)
        for half in range(2):
            part = lax.rem(x - y + k + 4, 4) * 2 + half
            rows = []
            for chip in range(2):
                for core in range(2):
                    tile = fg[2 * part + chip, core].astype(F32)
                    rows += [tile, pltpu.roll(tile, 64, 1)]
            turned = jnp.concatenate(rows, 0).T
            span = pl.ds(pl.multiple_of(part * 128, 128), 128)
            gs_o[:, span] = turned[0:24]
            gn_o[:, span] = turned[24:48]
            gb_o[:, span] = turned[48:49] + turned[49:50]

    assert used[0] <= SENDS and used[1] <= RECVS, used


OUTS = (
    jax.ShapeDtypeStruct((32, 1024), BF16),
    jax.ShapeDtypeStruct((COLS, 1024), F32),
    jax.ShapeDtypeStruct((COLS, 1024), F32),
    jax.ShapeDtypeStruct((1, 1024), F32),
)


def place(hid, gs, gn, gb, hid_o, gs_o, gn_o, gb_o, sem):
    pairs = [(hid, hid_o), (gs, gs_o), (gn, gn_o), (gb, gb_o)]
    moves = [pltpu.make_async_copy(src, dst, sem.at[i]) for i, (src, dst) in enumerate(pairs)]
    for move in moves:
        move.start()
    for move in moves:
        move.wait()


def shards(features, adjacency, offsets, live, w_self, w_neigh, bias, targets):
    vmem = pl.BlockSpec(memory_space=pltpu.VMEM)
    hbm = pl.BlockSpec(memory_space=pltpu.HBM)
    inputs = [features.T, adjacency, offsets, live, w_self, w_neigh, bias.reshape(1, 1024), targets]
    results = pl.pallas_call(
        kernel,
        out_shape=OUTS,
        in_specs=[hbm] * 8,
        out_specs=(vmem,) * 4,
        scratch_shapes=[
            pltpu.VMEM((COLS, 1024), BF16),
            pltpu.VMEM((8, TILE, 256), BF16),
            pltpu.SMEM((8,), jnp.int32),
            pltpu.SMEM((8,), jnp.int32),
            pltpu.VMEM((COLS, 1024), BF16),
            pltpu.VMEM((COLS, 1024), BF16),
            pltpu.VMEM((1, 1024), F32),
            pltpu.VMEM((32, 1024), BF16),
            pltpu.VMEM((COLS, 1024), F32),
            pltpu.VMEM((PAIR, HALF), F32),
            pltpu.VMEM((768, 1280), BF16),
            pltpu.VMEM((768, 1024), BF16),
            pltpu.VMEM((8, TILE, 384), BF16),
            pltpu.VMEM((16, 32, 128), BF16),
            pltpu.VMEM((2, 16, 32, 128), BF16),
            pltpu.VMEM((4, 128, COLUMN), BF16),
            pltpu.VMEM((32, 1024), F32),
            pltpu.VMEM((4, 4, 32, 128), BF16),
            pltpu.VMEM((4, 4, 32, 128), BF16),
            pltpu.VMEM((4, 2, 16, 128), BF16),
            pltpu.VMEM((4, 2, 16, 128), BF16),
            pltpu.VMEM((16, 2, 16, 128), BF16),
            pltpu.SemaphoreType.DMA((8,)),
            pltpu.SemaphoreType.DMA((SENDS,)),
            pltpu.SemaphoreType.DMA((RECVS,)),
        ],
        compiler_params=pltpu.CompilerParams(
            collective_id=0, has_side_effects=True, vmem_limit_bytes=48 * 1024 * 1024
        ),
        cost_estimate=pl.CostEstimate(flops=10**9, bytes_accessed=10**7, transcendentals=32768),
    )(*[pltpu.with_memory_space_constraint(array, pltpu.HBM) for array in inputs])
    hidden, grad_self, grad_neigh, grad_bias = pl.pallas_call(
        place,
        out_shape=OUTS,
        in_specs=[vmem] * 4,
        out_specs=(pl.BlockSpec(memory_space=pl.ANY),) * 4,
        scratch_shapes=[pltpu.SemaphoreType.DMA((4,))],
        compiler_params=pltpu.CompilerParams(vmem_limit_bytes=1024 * 1024),
    )(*[pltpu.with_memory_space_constraint(array, pltpu.VMEM) for array in results])
    return hidden, grad_self, grad_neigh, grad_bias.reshape(1024)


def solution(mesh):
    in_specs = (
        P("grp", "feat"),
        P("grp", None, None),
        P("grp"),
        P("grp"),
        P("feat", None),
        P("feat", None),
        P(),
        P("feat", "grp"),
    )
    out_specs = (P("feat", "grp"), P("feat", None), P("feat", None), P())
    return jax.shard_map(shards, mesh=mesh, in_specs=in_specs, out_specs=out_specs, check_vma=False)
```

```python
import jax
import jax.numpy as jnp
from jax import lax
from jax.experimental import pallas as pl
from jax.experimental.pallas import tpu as pltpu
from jax.sharding import PartitionSpec as P

F32 = jnp.float32
BF16 = jnp.bfloat16
MESH = pl.DeviceIdType.MESH

COLS = 24
PAIR = 48
COLUMN = 4 * PAIR
HALF = 640
PART_A = 384
PART_B = HALF - PART_A
TILE = 128
SENDS = 96
RECVS = 72


def mod4(value):
    return lax.rem(value + 4, 4)


def kernel(
    feat_h, adj_h, off_h, live_h, ws_h, wn_h, bias_h, tgt_h,
    hid, gs_o, gn_o, gb_o,
    feat, adj, off, live, ws, wn, bias, tgt,
    wide, stage, xg, nb, band, wsend, wg, wt, pre_acc, rsend, ra, rbs, rb, fg,
    in_sem, send_sem, recv_sem,
):
    loads = [
        pltpu.make_async_copy(src, dst, in_sem.at[i])
        for i, (src, dst) in enumerate(
            [(feat_h, feat), (ws_h, ws), (wn_h, wn), (adj_h, adj), (off_h, off), (live_h, live),
             (bias_h, bias), (tgt_h, tgt)]
        )
    ]
    for load in loads:
        load.start()

    g = lax.axis_index("grp")
    f = lax.axis_index("feat")
    c = lax.rem(f, 2)
    p = lax.div(f, 2)
    y = lax.div(p, 4)
    zh = lax.rem(p, 4)
    x = lax.rem(g, 4)
    zl = lax.div(g, 4)
    other = 1 - c
    sign = 1 - 2 * c

    def device(group, chip, core):
        return (group, chip * 2 + core)

    partner = device(g, p, other)
    y_fwd = device(g, mod4(y + sign) * 4 + zh, c)
    y_bwd = device(g, mod4(y - sign) * 4 + zh, c)
    y_far = device(g, mod4(y + 2) * 4 + zh, c)
    z_fwd = device(g, y * 4 + mod4(zh + sign), c)
    z_bwd = device(g, y * 4 + mod4(zh - sign), c)
    stays = jnp.logical_and(zh == zl, jnp.logical_and(x == 0, y == 0))

    barrier = pltpu.get_barrier_semaphore()

    def tell(target):
        pl.semaphore_signal(barrier, inc=1, device_id=target, device_id_type=MESH)

    @pl.when(jnp.logical_and(c == 0, g > 0))
    def _():
        tell(device(g - 1, p, 0))
        tell(device(g - 1, p, 1))

    @pl.when(jnp.logical_and(c == 1, g < 15))
    def _():
        tell(device(g + 1, p, 0))
        tell(device(g + 1, p, 1))

    for target in (z_fwd, z_bwd, y_fwd, y_bwd, y_far, partner):
        tell(target)

    w_src_y = mod4(y + x)
    w_dst_y = mod4(y - x)
    r_chip = mod4(x - y) * 4 + zl
    for step in range(1, 4):
        tell(device(g, w_src_y * 4 + mod4(zh + step), c))
        tell(device(g - x + mod4(x + step), p, other))
        tell(device(mod4(zl + step) * 4 + y, r_chip, 0))
        tell(device(mod4(zl + step) * 4 + y, r_chip, 1))

    @pl.when(x != 0)
    def _():
        tell(device(g, w_src_y * 4 + zh, c))

    tell(device(zl * 4 + y, r_chip, other))

    @pl.when(jnp.logical_not(stays))
    def _():
        tell(device(zl * 4 + y, r_chip, c))

    def tell_far(step, carry):
        tell(device(lax.rem(g + step, 16), p, c))
        return carry

    lax.fori_loop(1, 16, tell_far, 0)

    loads[0].wait()
    wide[...] = feat[...].astype(F32)

    @pl.when(c == 0)
    def _():
        stage[0:COLS, TILE:HALF] = wide[:, 0:512]

        @pl.when(g == 0)
        def _():
            stage[:, 0:TILE] = jnp.zeros((PAIR, TILE), F32)

    @pl.when(c == 1)
    def _():
        stage[COLS:PAIR, 0:512] = wide[:, 512:1024]

        @pl.when(g == 15)
        def _():
            stage[:, 512:HALF] = jnp.zeros((PAIR, TILE), F32)

    waits = (
        6 + 3 + 7 + 15 + 3
        + (x != 0).astype(jnp.int32)
        + jnp.logical_not(stays).astype(jnp.int32)
        + (g < 15).astype(jnp.int32)
        + (g > 0).astype(jnp.int32)
    )
    pl.semaphore_wait(barrier, waits)

    used = [0, 0]
    sent = []

    def slot(which, count=1):
        used[which] += count
        return used[which] - count

    def remote(src, dst, target, send, recv):
        return pltpu.make_async_remote_copy(
            src_ref=src, dst_ref=dst, send_sem=send_sem.at[send], recv_sem=recv_sem.at[recv],
            device_id=target, device_id_type=MESH,
        )

    def copy(src, dst, target, recv):
        made = remote(src, dst, target, slot(0), recv)
        made.start()
        sent.append(made)

    def start_unless(skip, made):
        @pl.when(jnp.logical_not(skip))
        def _():
            made.start()

    def drain(first, last):
        for made in sent[first:last]:
            made.wait_send()

    def await_bytes(ref, recv):
        pltpu.make_async_copy(ref, ref, recv_sem.at[recv]).wait()

    own_rows = pl.ds(pl.multiple_of(c * COLS, 8), COLS)
    other_rows = pl.ds(pl.multiple_of(other * COLS, 8), COLS)
    r_left, r_right, r_swap = slot(1, 2), slot(1, 2), slot(1)
    halo_up = remote(
        wide.at[:, 896:1024], stage.at[own_rows, 0:TILE], device(g + 1, p, 0), slot(0), r_left + c
    )
    halo_down = remote(
        wide.at[:, 0:TILE], stage.at[own_rows, 512:HALF], device(g - 1, p, 1), slot(0), r_right + c
    )

    @pl.when(g < 15)
    def _():
        halo_up.start()

    @pl.when(g > 0)
    def _():
        halo_down.start()

    copy(
        wide.at[:, pl.ds(pl.multiple_of(other * 512, 128), 512)],
        stage.at[own_rows, pl.ds(pl.multiple_of(c * TILE, 128), 512)],
        partner, r_swap,
    )

    loads[1].wait()
    loads[2].wait()
    lane = lax.broadcasted_iota(jnp.int32, (COLS, 128), 1)
    pad = jnp.zeros((32 - COLS, 128), F32)
    for pair in range(8):
        s_tile = ws[:, pair * 128:(pair + 1) * 128].astype(F32)
        n_tile = wn[:, pair * 128:(pair + 1) * 128].astype(F32)
        low = jnp.where(lane < 64, s_tile, pltpu.roll(n_tile, 64, 1))
        high = jnp.where(lane < 64, pltpu.roll(s_tile, 64, 1), n_tile)
        wsend[2 * pair] = jnp.concatenate([low, pad], 0).astype(BF16)
        wsend[2 * pair + 1] = jnp.concatenate([high, pad], 0).astype(BF16)

    r_w1 = slot(1, 4)
    for step in range(1, 4):
        chip = w_dst_y * 4 + mod4(zh + step)
        copy(wsend.at[chip], wg.at[c, p], device(g, chip, c), r_w1 + step)
    chip0 = w_dst_y * 4 + zh
    w_zero = remote(wsend.at[chip0], wg.at[c, p], device(g, chip0, c), slot(0), r_w1)

    @pl.when(x != 0)
    def _():
        w_zero.start()

    @pl.when(x == 0)
    def _():
        wg[c, p] = wsend[chip0]

    def block(by, bz, part):
        rows = pl.ds(pl.multiple_of((mod4(bz) * 4 + mod4(by)) * PAIR, 16), PAIR)
        start = {"all": 0, "a": other * PART_B, "b": c * PART_A}[part]
        width = {"all": HALF, "a": PART_A, "b": PART_B}[part]
        return xg.at[rows, pl.ds(pl.multiple_of(c * HALF + start, 128), width)]

    r_pair = slot(1, 4)

    def forward(by, bz, part, target, recv):
        view = block(by, bz, part)
        copy(view, view, target, recv)

    def share(by, bz, part):
        forward(by, bz, part, partner, r_pair + mod4(bz))

    r_z1 = slot(1, 4)
    r_z2 = slot(1, 2)
    r_y1 = slot(1, 12)
    r_y2 = slot(1, 6)
    r_y3 = slot(1, 6)

    def column(number):
        return zh + sign * (0, -1, 1)[number]

    def send_y1(number, part):
        first = r_y1 + 4 * number + (0 if part == "a" else 2)
        forward(y, column(number), part, y_fwd, first)
        forward(y, column(number), part, y_bwd, first + 1)

    def take_y1(number):
        bz = column(number)
        first = r_y1 + 4 * number
        await_bytes(block(y - sign, bz, "a"), first)
        forward(y - sign, bz, "a", y_fwd, r_y2 + 2 * number)
        await_bytes(block(y + sign, bz, "b"), first + 3)
        forward(y + sign, bz, "b", y_bwd, r_y2 + 2 * number + 1)
        await_bytes(block(y - sign, bz, "b"), first + 2)
        share(y - sign, bz, "all")
        await_bytes(block(y + sign, bz, "a"), first + 1)
        share(y + sign, bz, "all")

    def take_y2(number):
        bz = column(number)
        await_bytes(block(y + 2, bz, "a"), r_y2 + 2 * number)
        share(y + 2, bz, "a")
        await_bytes(block(y + 2, bz, "b"), r_y2 + 2 * number + 1)
        share(y + 2, bz, "b")

    def send_y3(part):
        first = r_y3 + (0 if part == "a" else 3)
        forward(y, zh + 2, part, y_fwd, first)
        forward(y, zh + 2, part, y_bwd, first + 1)
        forward(y, zh + 2, part, y_far, first + 2)
        share(y, zh + 2, part)

    def take_y3(part):
        first = r_y3 + (0 if part == "a" else 3)
        for offset, by in enumerate((y - sign, y + sign, y + 2)):
            await_bytes(block(by, zh + 2, part), first + offset)
            share(by, zh + 2, part)

    await_bytes(stage.at[other_rows, pl.ds(pl.multiple_of(other * TILE, 128), 512)], r_swap)
    block(y, zh, "a")[...] = stage[:, pl.ds(pl.multiple_of(other * PART_B, 128), PART_A)].astype(BF16)
    forward(y, zh, "a", z_fwd, r_z1)
    send_y1(0, "a")

    @pl.when(jnp.logical_and(c == 0, g > 0))
    def _():
        await_bytes(stage.at[0:COLS, 0:TILE], r_left)
        await_bytes(stage.at[COLS:PAIR, 0:TILE], r_left + 1)

    @pl.when(jnp.logical_and(c == 1, g < 15))
    def _():
        await_bytes(stage.at[0:COLS, 512:HALF], r_right)
        await_bytes(stage.at[COLS:PAIR, 512:HALF], r_right + 1)

    block(y, zh, "b")[...] = stage[:, pl.ds(pl.multiple_of(c * PART_A, 128), PART_B)].astype(BF16)
    forward(y, zh, "b", z_bwd, r_z1 + 1)
    forward(y, zh, "a", z_bwd, r_z1 + 3)
    forward(y, zh, "b", z_fwd, r_z1 + 2)

    send_y1(0, "b")
    share(y, zh, "all")

    for load in loads[3:6]:
        load.wait()
    for tile in range(8):
        dense = adj[tile].astype(F32)
        padded = jnp.concatenate([dense, jnp.zeros((TILE, TILE), F32)], 1)
        moved = pltpu.roll(padded, off[tile] - tile * TILE, 1)
        band[tile] = (moved * live[tile].astype(F32)).astype(BF16)

    def neighbours(bz):
        col = mod4(bz)
        rows = pl.ds(pl.multiple_of(col * COLUMN, 16), COLUMN)
        await_bytes(xg.at[rows, pl.ds(pl.multiple_of(other * HALF, 128), HALF)], r_pair + col)
        for tile in range(8):
            nb[rows, tile * TILE:(tile + 1) * TILE] = lax.dot_general(
                xg[rows, tile * TILE:tile * TILE + 3 * TILE], band[tile],
                (((1,), (1,)), ((), ())), preferred_element_type=F32,
            ).astype(BF16)

    def products(bz):
        col = mod4(bz)
        rows = pl.ds(pl.multiple_of(col * COLUMN, 16), COLUMN)
        ws_t = wt[col, pl.ds(pl.multiple_of(c * 32, 16), 32), :]
        wn_t = wt[col, pl.ds(pl.multiple_of(64 + c * 32, 16), 32), :]
        pre_acc[...] += (
            jnp.dot(ws_t, xg[rows, TILE:TILE + 1024], preferred_element_type=F32)
            + jnp.dot(wn_t, nb[rows, :], preferred_element_type=F32)
        )

    take_y1(0)

    await_bytes(block(y, zh - sign, "a"), r_z1)
    forward(y, zh - sign, "a", z_fwd, r_z2)
    send_y1(1, "a")
    await_bytes(block(y, zh + sign, "b"), r_z1 + 1)
    forward(y, zh + sign, "b", z_bwd, r_z2 + 1)
    send_y1(2, "b")

    for step in range(1, 4):
        await_bytes(wg.at[c, w_src_y * 4 + mod4(zh + step)], r_w1 + 4 - step)

    @pl.when(x != 0)
    def _():
        await_bytes(wg.at[c, w_src_y * 4 + zh], r_w1)

    r_w2 = slot(1, 2)
    part_w = wg.at[c, pl.ds(w_src_y * 4, 4)]
    copy(part_w, part_w, partner, r_w2 + c)
    for step in range(1, 4):
        for core in range(2):
            copy(part_w, part_w, device(g - x + mod4(x + step), p, core), r_w2 + c)

    take_y2(0)
    await_bytes(block(y, zh + sign, "a"), r_z1 + 3)
    send_y1(2, "a")
    await_bytes(block(y, zh - sign, "b"), r_z1 + 2)
    send_y1(1, "b")
    share(y, zh - sign, "all")
    share(y, zh + sign, "all")
    neighbours(zh)
    take_y1(1)
    take_y1(2)
    await_bytes(block(y, zh + 2, "a"), r_z2)
    send_y3("a")
    await_bytes(block(y, zh + 2, "b"), r_z2 + 1)
    send_y3("b")
    take_y2(2)
    take_y2(1)

    neighbours(zh - 1)
    neighbours(zh + 1)
    take_y3("a")
    take_y3("b")

    await_bytes(wg.at[other], r_w2 + other)
    await_bytes(wg.at[c, 0:12], r_w2 + c)
    for col in range(4):
        rows = []
        for row in range(4):
            for core in range(2):
                rows.append(wg[core, row * 4 + col].astype(F32)[0:COLS])
        wt[col] = jnp.concatenate(rows, 0).T.astype(BF16)
    loads[6].wait()
    spot = lax.broadcasted_iota(jnp.int32, (32, 1024), 1)
    row = lax.broadcasted_iota(jnp.int32, (32, 1024), 0)
    bias_own = jnp.sum(
        jnp.where(spot == row + f * 32, jnp.broadcast_to(bias[...], (32, 1024)), 0.0),
        axis=1, keepdims=True,
    )
    pre_acc[...] = jnp.broadcast_to(bias_own, (32, 1024))
    products(zh)
    products(zh - 1)
    products(zh + 1)
    neighbours(zh + 2)
    products(zh + 2)

    loads[7].wait()
    pre = pre_acc[...]
    gate = jax.nn.sigmoid(pre)
    act = pre * gate
    hid[...] = act.astype(BF16)
    delta = (act - tgt[...].astype(F32)) * (gate * (1.0 + pre * (1.0 - gate))) * (1.0 / 128.0)

    head = delta.astype(BF16)
    rest = (delta - head.astype(F32)).astype(BF16)
    both = jnp.concatenate([head] * 4 + [rest] * 4, 0)
    turn = (((1,), (1,)), ((), ()))
    bias_term = jnp.sum(delta, axis=1, keepdims=True)
    quarter = lax.div(lax.broadcasted_iota(jnp.int32, (PAIR, 128), 1), 32)
    blank = jnp.zeros((16, 128), F32)

    def with_bias(tile, low_total, high_total):
        lane_of = lax.broadcasted_iota(jnp.int32, tile.shape, 1)
        bias_sum = jnp.where(lane_of < 64, low_total, high_total)
        first = bias_sum.astype(BF16).astype(F32)
        tile = jnp.where(lax.rem(lane_of, 64) == 48, first, tile)
        return jnp.where(lax.rem(lane_of, 64) == 49, bias_sum - first, tile)

    r_ra = slot(1, 4)
    for turn_of in range(1, 5):
        row = mod4(x + turn_of)
        spans = [
            pl.ds(pl.multiple_of((col * 4 + row) * PAIR, 16), PAIR) for col in range(4)
        ]
        left = jnp.concatenate(
            [xg[span, TILE:TILE + 1024] for span in spans] + [nb[span, :] for span in spans], 0
        )
        grad = lax.dot_general(left, both, turn, preferred_element_type=F32)
        grad = grad[:, 0:128] + grad[:, 128:256]

        def packed(first):
            parts = [grad[first + col * PAIR:first + (col + 1) * PAIR] for col in range(4)]
            low = jnp.where(quarter == 0, parts[0], parts[1])
            high = jnp.where(quarter == 2, parts[2], parts[3])
            return jnp.where(quarter < 2, low, high)

        own_term, nb_term = packed(0), packed(COLUMN)
        turned = jnp.concatenate(
            [own_term[0:COLS], nb_term[0:COLS], blank, own_term[COLS:PAIR], nb_term[COLS:PAIR], blank], 0
        ).T
        for col in range(4):
            tile = with_bias(turned[col * 32:(col + 1) * 32], bias_term, bias_term)
            rsend[row, col] = tile.astype(BF16)
        if turn_of < 4:
            copy(rsend.at[row], ra.at[turn_of], device(g - x + row, p, c), r_ra + turn_of)

    before_x = len(sent) - 3
    drain(0, before_x)

    @pl.when(g < 15)
    def _():
        halo_up.wait_send()

    @pl.when(g > 0)
    def _():
        halo_down.wait_send()

    @pl.when(x != 0)
    def _():
        w_zero.wait_send()

    for turn_of in range(1, 4):
        await_bytes(ra.at[turn_of], r_ra + turn_of)

    r_rb = slot(1)
    to_group = zh * 4 + mod4(y + x)
    halves = lax.broadcasted_iota(jnp.int32, (16, 128), 1) < 64
    for step in (2, 1, 3, 0):
        col = mod4(zh + step)
        summed = (rsend[x, col].astype(F32) + ra[1, col].astype(F32)) + (
            ra[2, col].astype(F32) + ra[3, col].astype(F32)
        )
        bias_sum = summed[:, 48:49] + summed[:, 49:50]
        summed = with_bias(summed, bias_sum, bias_sum)
        top, bottom = summed[0:16], summed[16:32]
        rbs[col, 0] = jnp.where(halves, top, pltpu.roll(bottom, 64, 1)).astype(BF16)
        rbs[col, 1] = jnp.where(halves, pltpu.roll(top, 64, 1), bottom).astype(BF16)
        if step:
            for core in range(2):
                copy(rbs.at[col, core], rb.at[zl, c], device(to_group, x * 4 + col, core), r_rb)

    copy(rbs.at[zh, other], rb.at[zl, c], device(to_group, x * 4 + zh, other), r_rb)
    r_zero = remote(rbs.at[zh, c], rb.at[zl, c], device(to_group, x * 4 + zh, c), slot(0), r_rb)
    start_unless(stays, r_zero)

    @pl.when(stays)
    def _():
        pltpu.make_async_copy(rbs.at[zh, c], rb.at[zl, c], recv_sem.at[r_rb]).start()

    drain(before_x, None)
    await_bytes(rb, r_rb)
    for core in range(2):
        total = (rb[0, core].astype(F32) + rb[1, core].astype(F32)) + (
            rb[2, core].astype(F32) + rb[3, core].astype(F32)
        )
        fg[r_chip, core] = with_bias(
            total, total[:, 48:49] + total[:, 49:50], total[:, 112:113] + total[:, 113:114]
        ).astype(BF16)

    r_r2, s_r2 = slot(1, 4), slot(0)
    for step in range(1, 16):
        far = lax.rem(g + step, 16)
        remote(
            fg.at[r_chip], fg.at[r_chip], device(far, p, c), s_r2, r_r2 + mod4(x - lax.rem(far, 4))
        ).start()

    @pl.when(jnp.logical_not(stays))
    def _():
        r_zero.wait_send()

    for k in (0, 1, 3, 2):
        if k == 2:
            pltpu.make_async_copy(fg.at[0:15], fg.at[0:15], send_sem.at[s_r2]).wait()
        await_bytes(fg.at[0:(4 if k else 3)], r_r2 + k)
        for half in range(2):
            part = lax.rem(x - y + k + 4, 4) * 2 + half
            rows = []
            for chip in range(2):
                for core in range(2):
                    tile = fg[2 * part + chip, core].astype(F32)
                    rows += [tile, pltpu.roll(tile, 64, 1)]
            turned = jnp.concatenate(rows, 0).T
            span = pl.ds(pl.multiple_of(part * 128, 128), 128)
            gs_o[:, span] = turned[0:24]
            gn_o[:, span] = turned[24:48]
            gb_o[:, span] = turned[48:49] + turned[49:50]

    assert used[0] <= SENDS and used[1] <= RECVS, used


OUTS = (
    jax.ShapeDtypeStruct((32, 1024), BF16),
    jax.ShapeDtypeStruct((COLS, 1024), F32),
    jax.ShapeDtypeStruct((COLS, 1024), F32),
    jax.ShapeDtypeStruct((1, 1024), F32),
)


def place(hid, gs, gn, gb, hid_o, gs_o, gn_o, gb_o, sem):
    pairs = [(hid, hid_o), (gs, gs_o), (gn, gn_o), (gb, gb_o)]
    moves = [pltpu.make_async_copy(src, dst, sem.at[i]) for i, (src, dst) in enumerate(pairs)]
    for move in moves:
        move.start()
    for move in moves:
        move.wait()


def shards(features, adjacency, offsets, live, w_self, w_neigh, bias, targets):
    vmem = pl.BlockSpec(memory_space=pltpu.VMEM)
    hbm = pl.BlockSpec(memory_space=pltpu.HBM)
    inputs = [features.T, adjacency, offsets, live, w_self, w_neigh, bias.reshape(1, 1024), targets]
    results = pl.pallas_call(
        kernel,
        out_shape=OUTS,
        in_specs=[hbm] * 8,
        out_specs=(vmem,) * 4,
        scratch_shapes=[
            pltpu.VMEM((COLS, 1024), BF16),
            pltpu.VMEM((8, TILE, 256), BF16),
            pltpu.SMEM((8,), jnp.int32),
            pltpu.SMEM((8,), jnp.int32),
            pltpu.VMEM((COLS, 1024), BF16),
            pltpu.VMEM((COLS, 1024), BF16),
            pltpu.VMEM((1, 1024), F32),
            pltpu.VMEM((32, 1024), BF16),
            pltpu.VMEM((COLS, 1024), F32),
            pltpu.VMEM((PAIR, HALF), F32),
            pltpu.VMEM((768, 1280), BF16),
            pltpu.VMEM((768, 1024), BF16),
            pltpu.VMEM((8, TILE, 384), BF16),
            pltpu.VMEM((16, 32, 128), BF16),
            pltpu.VMEM((2, 16, 32, 128), BF16),
            pltpu.VMEM((4, 128, COLUMN), BF16),
            pltpu.VMEM((32, 1024), F32),
            pltpu.VMEM((4, 4, 32, 128), BF16),
            pltpu.VMEM((4, 4, 32, 128), BF16),
            pltpu.VMEM((4, 2, 16, 128), BF16),
            pltpu.VMEM((4, 2, 16, 128), BF16),
            pltpu.VMEM((16, 2, 16, 128), BF16),
            pltpu.SemaphoreType.DMA((8,)),
            pltpu.SemaphoreType.DMA((SENDS,)),
            pltpu.SemaphoreType.DMA((RECVS,)),
        ],
        compiler_params=pltpu.CompilerParams(
            collective_id=0, has_side_effects=True, vmem_limit_bytes=48 * 1024 * 1024
        ),
        cost_estimate=pl.CostEstimate(flops=10**9, bytes_accessed=10**7, transcendentals=32768),
    )(*[pltpu.with_memory_space_constraint(array, pltpu.HBM) for array in inputs])
    hidden, grad_self, grad_neigh, grad_bias = pl.pallas_call(
        place,
        out_shape=OUTS,
        in_specs=[vmem] * 4,
        out_specs=(pl.BlockSpec(memory_space=pl.ANY),) * 4,
        scratch_shapes=[pltpu.SemaphoreType.DMA((4,))],
        compiler_params=pltpu.CompilerParams(vmem_limit_bytes=1024 * 1024),
    )(*[pltpu.with_memory_space_constraint(array, pltpu.VMEM) for array in results])
    return hidden, grad_self, grad_neigh, grad_bias.reshape(1024)


def solution(mesh):
    in_specs = (
        P("grp", "feat"),
        P("grp", None, None),
        P("grp"),
        P("grp"),
        P("feat", None),
        P("feat", None),
        P(),
        P("feat", "grp"),
    )
    out_specs = (P("feat", "grp"), P("feat", None), P("feat", None), P())
    return jax.shard_map(shards, mesh=mesh, in_specs=in_specs, out_specs=out_specs, check_vma=False)
```

```python
import jax
import jax.numpy as jnp
from jax import lax
from jax.experimental import pallas as pl
from jax.experimental.pallas import tpu as pltpu
from jax.sharding import PartitionSpec as P

F32 = jnp.float32
BF16 = jnp.bfloat16
MESH = pl.DeviceIdType.MESH

COLS = 24
PAIR = 48
COLUMN = 4 * PAIR
HALF = 640
PART_A = 384
PART_B = HALF - PART_A
TILE = 128
SENDS = 96
RECVS = 72


def mod4(value):
    return lax.rem(value + 4, 4)


def kernel(
    feat_h, adj_h, off_h, live_h, ws_h, wn_h, bias_h, tgt_h,
    hid, gs_o, gn_o, gb_o,
    feat, adj, off, live, ws, wn, bias, tgt,
    wide, stage, xg, nb, band, wsend, wg, wt, pre_acc, rsend, ra, rbs, rb, fg,
    in_sem, send_sem, recv_sem,
):
    loads = [
        pltpu.make_async_copy(src, dst, in_sem.at[i])
        for i, (src, dst) in enumerate(
            [(feat_h, feat), (ws_h, ws), (wn_h, wn), (adj_h, adj), (off_h, off), (live_h, live),
             (bias_h, bias), (tgt_h, tgt)]
        )
    ]
    for load in loads:
        load.start()

    g = lax.axis_index("grp")
    f = lax.axis_index("feat")
    c = lax.rem(f, 2)
    p = lax.div(f, 2)
    y = lax.div(p, 4)
    zh = lax.rem(p, 4)
    x = lax.rem(g, 4)
    zl = lax.div(g, 4)
    other = 1 - c
    sign = 1 - 2 * c

    def device(group, chip, core):
        return (group, chip * 2 + core)

    partner = device(g, p, other)
    y_fwd = device(g, mod4(y + sign) * 4 + zh, c)
    y_bwd = device(g, mod4(y - sign) * 4 + zh, c)
    y_far = device(g, mod4(y + 2) * 4 + zh, c)
    z_fwd = device(g, y * 4 + mod4(zh + sign), c)
    z_bwd = device(g, y * 4 + mod4(zh - sign), c)
    stays = jnp.logical_and(zh == zl, jnp.logical_and(x == 0, y == 0))

    barrier = pltpu.get_barrier_semaphore()

    def tell(target):
        pl.semaphore_signal(barrier, inc=1, device_id=target, device_id_type=MESH)

    @pl.when(jnp.logical_and(c == 0, g > 0))
    def _():
        tell(device(g - 1, p, 0))
        tell(device(g - 1, p, 1))

    @pl.when(jnp.logical_and(c == 1, g < 15))
    def _():
        tell(device(g + 1, p, 0))
        tell(device(g + 1, p, 1))

    for target in (z_fwd, z_bwd, y_fwd, y_bwd, y_far, partner):
        tell(target)

    w_src_y = mod4(y + x)
    w_dst_y = mod4(y - x)
    r_chip = mod4(x - y) * 4 + zl
    for step in range(1, 4):
        tell(device(g, w_src_y * 4 + mod4(zh + step), c))
        tell(device(g - x + mod4(x + step), p, other))
        tell(device(mod4(zl + step) * 4 + y, r_chip, 0))
        tell(device(mod4(zl + step) * 4 + y, r_chip, 1))

    @pl.when(x != 0)
    def _():
        tell(device(g, w_src_y * 4 + zh, c))

    tell(device(zl * 4 + y, r_chip, other))

    @pl.when(jnp.logical_not(stays))
    def _():
        tell(device(zl * 4 + y, r_chip, c))

    def tell_far(step, carry):
        tell(device(lax.rem(g + step, 16), p, c))
        return carry

    lax.fori_loop(1, 16, tell_far, 0)

    loads[0].wait()
    wide[...] = feat[...].astype(F32)

    @pl.when(c == 0)
    def _():
        stage[0:COLS, TILE:HALF] = wide[:, 0:512]

        @pl.when(g == 0)
        def _():
            stage[:, 0:TILE] = jnp.zeros((PAIR, TILE), F32)

    @pl.when(c == 1)
    def _():
        stage[COLS:PAIR, 0:512] = wide[:, 512:1024]

        @pl.when(g == 15)
        def _():
            stage[:, 512:HALF] = jnp.zeros((PAIR, TILE), F32)

    waits = (
        6 + 3 + 7 + 15 + 3
        + (x != 0).astype(jnp.int32)
        + jnp.logical_not(stays).astype(jnp.int32)
        + (g < 15).astype(jnp.int32)
        + (g > 0).astype(jnp.int32)
    )
    pl.semaphore_wait(barrier, waits)

    used = [0, 0]
    sent = []

    def slot(which, count=1):
        used[which] += count
        return used[which] - count

    def remote(src, dst, target, send, recv):
        return pltpu.make_async_remote_copy(
            src_ref=src, dst_ref=dst, send_sem=send_sem.at[send], recv_sem=recv_sem.at[recv],
            device_id=target, device_id_type=MESH,
        )

    def copy(src, dst, target, recv):
        made = remote(src, dst, target, slot(0), recv)
        made.start()
        sent.append(made)

    def start_unless(skip, made):
        @pl.when(jnp.logical_not(skip))
        def _():
            made.start()

    def drain(first, last):
        for made in sent[first:last]:
            made.wait_send()

    def await_bytes(ref, recv):
        pltpu.make_async_copy(ref, ref, recv_sem.at[recv]).wait()

    own_rows = pl.ds(pl.multiple_of(c * COLS, 8), COLS)
    other_rows = pl.ds(pl.multiple_of(other * COLS, 8), COLS)
    r_left, r_right, r_swap = slot(1, 2), slot(1, 2), slot(1)
    halo_up = remote(
        wide.at[:, 896:1024], stage.at[own_rows, 0:TILE], device(g + 1, p, 0), slot(0), r_left + c
    )
    halo_down = remote(
        wide.at[:, 0:TILE], stage.at[own_rows, 512:HALF], device(g - 1, p, 1), slot(0), r_right + c
    )

    @pl.when(g < 15)
    def _():
        halo_up.start()

    @pl.when(g > 0)
    def _():
        halo_down.start()

    copy(
        wide.at[:, pl.ds(pl.multiple_of(other * 512, 128), 512)],
        stage.at[own_rows, pl.ds(pl.multiple_of(c * TILE, 128), 512)],
        partner, r_swap,
    )

    loads[1].wait()
    loads[2].wait()
    lane = lax.broadcasted_iota(jnp.int32, (COLS, 128), 1)
    pad = jnp.zeros((32 - COLS, 128), F32)
    for pair in range(8):
        s_tile = ws[:, pair * 128:(pair + 1) * 128].astype(F32)
        n_tile = wn[:, pair * 128:(pair + 1) * 128].astype(F32)
        low = jnp.where(lane < 64, s_tile, pltpu.roll(n_tile, 64, 1))
        high = jnp.where(lane < 64, pltpu.roll(s_tile, 64, 1), n_tile)
        wsend[2 * pair] = jnp.concatenate([low, pad], 0).astype(BF16)
        wsend[2 * pair + 1] = jnp.concatenate([high, pad], 0).astype(BF16)

    r_w1 = slot(1, 4)
    for step in range(1, 4):
        chip = w_dst_y * 4 + mod4(zh + step)
        copy(wsend.at[chip], wg.at[c, p], device(g, chip, c), r_w1 + step)
    chip0 = w_dst_y * 4 + zh
    w_zero = remote(wsend.at[chip0], wg.at[c, p], device(g, chip0, c), slot(0), r_w1)

    @pl.when(x != 0)
    def _():
        w_zero.start()

    @pl.when(x == 0)
    def _():
        wg[c, p] = wsend[chip0]

    def block(by, bz, part):
        rows = pl.ds(pl.multiple_of((mod4(bz) * 4 + mod4(by)) * PAIR, 16), PAIR)
        start = {"all": 0, "a": other * PART_B, "b": c * PART_A}[part]
        width = {"all": HALF, "a": PART_A, "b": PART_B}[part]
        return xg.at[rows, pl.ds(pl.multiple_of(c * HALF + start, 128), width)]

    r_pair = slot(1, 4)

    def forward(by, bz, part, target, recv):
        view = block(by, bz, part)
        copy(view, view, target, recv)

    def share(by, bz, part):
        forward(by, bz, part, partner, r_pair + mod4(bz))

    r_z1 = slot(1, 4)
    r_z2 = slot(1, 2)
    r_y1 = slot(1, 12)
    r_y2 = slot(1, 6)
    r_y3 = slot(1, 6)

    def column(number):
        return zh + sign * (0, -1, 1)[number]

    def send_y1(number, part):
        first = r_y1 + 4 * number + (0 if part == "a" else 2)
        forward(y, column(number), part, y_fwd, first)
        forward(y, column(number), part, y_bwd, first + 1)

    def take_y1(number):
        bz = column(number)
        first = r_y1 + 4 * number
        await_bytes(block(y - sign, bz, "a"), first)
        forward(y - sign, bz, "a", y_fwd, r_y2 + 2 * number)
        await_bytes(block(y + sign, bz, "b"), first + 3)
        forward(y + sign, bz, "b", y_bwd, r_y2 + 2 * number + 1)
        await_bytes(block(y - sign, bz, "b"), first + 2)
        share(y - sign, bz, "all")
        await_bytes(block(y + sign, bz, "a"), first + 1)
        share(y + sign, bz, "all")

    def take_y2(number):
        bz = column(number)
        await_bytes(block(y + 2, bz, "a"), r_y2 + 2 * number)
        share(y + 2, bz, "a")
        await_bytes(block(y + 2, bz, "b"), r_y2 + 2 * number + 1)
        share(y + 2, bz, "b")

    def send_y3(part):
        first = r_y3 + (0 if part == "a" else 3)
        forward(y, zh + 2, part, y_fwd, first)
        forward(y, zh + 2, part, y_bwd, first + 1)
        forward(y, zh + 2, part, y_far, first + 2)
        share(y, zh + 2, part)

    def take_y3(part):
        first = r_y3 + (0 if part == "a" else 3)
        for offset, by in enumerate((y - sign, y + sign, y + 2)):
            await_bytes(block(by, zh + 2, part), first + offset)
            share(by, zh + 2, part)

    await_bytes(stage.at[other_rows, pl.ds(pl.multiple_of(other * TILE, 128), 512)], r_swap)
    block(y, zh, "a")[...] = stage[:, pl.ds(pl.multiple_of(other * PART_B, 128), PART_A)].astype(BF16)
    forward(y, zh, "a", z_fwd, r_z1)
    forward(y, zh, "a", z_bwd, r_z1 + 3)
    send_y1(0, "a")

    @pl.when(jnp.logical_and(c == 0, g > 0))
    def _():
        await_bytes(stage.at[0:COLS, 0:TILE], r_left)
        await_bytes(stage.at[COLS:PAIR, 0:TILE], r_left + 1)

    @pl.when(jnp.logical_and(c == 1, g < 15))
    def _():
        await_bytes(stage.at[0:COLS, 512:HALF], r_right)
        await_bytes(stage.at[COLS:PAIR, 512:HALF], r_right + 1)

    block(y, zh, "b")[...] = stage[:, pl.ds(pl.multiple_of(c * PART_A, 128), PART_B)].astype(BF16)
    forward(y, zh, "b", z_bwd, r_z1 + 1)
    forward(y, zh, "b", z_fwd, r_z1 + 2)

    send_y1(0, "b")
    share(y, zh, "all")

    for load in loads[3:6]:
        load.wait()
    for tile in range(8):
        dense = adj[tile].astype(F32)
        padded = jnp.concatenate([dense, jnp.zeros((TILE, TILE), F32)], 1)
        moved = pltpu.roll(padded, off[tile] - tile * TILE, 1)
        band[tile] = (moved * live[tile].astype(F32)).astype(BF16)

    def neighbours(bz):
        col = mod4(bz)
        rows = pl.ds(pl.multiple_of(col * COLUMN, 16), COLUMN)
        await_bytes(xg.at[rows, pl.ds(pl.multiple_of(other * HALF, 128), HALF)], r_pair + col)
        for tile in range(8):
            nb[rows, tile * TILE:(tile + 1) * TILE] = lax.dot_general(
                xg[rows, tile * TILE:tile * TILE + 3 * TILE], band[tile],
                (((1,), (1,)), ((), ())), preferred_element_type=F32,
            ).astype(BF16)

    def products(bz):
        col = mod4(bz)
        rows = pl.ds(pl.multiple_of(col * COLUMN, 16), COLUMN)
        ws_t = wt[col, pl.ds(pl.multiple_of(c * 32, 16), 32), :]
        wn_t = wt[col, pl.ds(pl.multiple_of(64 + c * 32, 16), 32), :]
        pre_acc[...] += (
            jnp.dot(ws_t, xg[rows, TILE:TILE + 1024], preferred_element_type=F32)
            + jnp.dot(wn_t, nb[rows, :], preferred_element_type=F32)
        )

    take_y1(0)

    await_bytes(block(y, zh - sign, "a"), r_z1)
    forward(y, zh - sign, "a", z_fwd, r_z2)
    send_y1(1, "a")
    await_bytes(block(y, zh + sign, "a"), r_z1 + 3)
    send_y1(2, "a")

    for step in range(1, 4):
        await_bytes(wg.at[c, w_src_y * 4 + mod4(zh + step)], r_w1 + 4 - step)

    @pl.when(x != 0)
    def _():
        await_bytes(wg.at[c, w_src_y * 4 + zh], r_w1)

    r_w2 = slot(1, 2)
    part_w = wg.at[c, pl.ds(w_src_y * 4, 4)]
    copy(part_w, part_w, partner, r_w2 + c)
    for step in range(1, 4):
        for core in range(2):
            copy(part_w, part_w, device(g - x + mod4(x + step), p, core), r_w2 + c)

    take_y2(0)
    await_bytes(block(y, zh + sign, "b"), r_z1 + 1)
    forward(y, zh + sign, "b", z_bwd, r_z2 + 1)
    send_y1(2, "b")
    await_bytes(block(y, zh - sign, "b"), r_z1 + 2)
    send_y1(1, "b")
    share(y, zh - sign, "all")
    share(y, zh + sign, "all")
    neighbours(zh)
    take_y1(1)
    take_y1(2)
    await_bytes(block(y, zh + 2, "a"), r_z2)
    send_y3("a")
    await_bytes(block(y, zh + 2, "b"), r_z2 + 1)
    send_y3("b")
    take_y2(2)
    take_y2(1)

    neighbours(zh - 1)
    take_y3("a")
    neighbours(zh + 1)
    take_y3("b")

    await_bytes(wg.at[other], r_w2 + other)
    await_bytes(wg.at[c, 0:12], r_w2 + c)
    for col in range(4):
        rows = []
        for row in range(4):
            for core in range(2):
                rows.append(wg[core, row * 4 + col].astype(F32)[0:COLS])
        wt[col] = jnp.concatenate(rows, 0).T.astype(BF16)
    loads[6].wait()
    spot = lax.broadcasted_iota(jnp.int32, (32, 1024), 1)
    row = lax.broadcasted_iota(jnp.int32, (32, 1024), 0)
    bias_own = jnp.sum(
        jnp.where(spot == row + f * 32, jnp.broadcast_to(bias[...], (32, 1024)), 0.0),
        axis=1, keepdims=True,
    )
    pre_acc[...] = jnp.broadcast_to(bias_own, (32, 1024))
    products(zh)
    products(zh - 1)
    products(zh + 1)
    neighbours(zh + 2)
    products(zh + 2)

    loads[7].wait()
    pre = pre_acc[...]
    gate = jax.nn.sigmoid(pre)
    act = pre * gate
    hid[...] = act.astype(BF16)
    delta = (act - tgt[...].astype(F32)) * (gate * (1.0 + pre * (1.0 - gate))) * (1.0 / 128.0)

    head = delta.astype(BF16)
    rest = (delta - head.astype(F32)).astype(BF16)
    both = jnp.concatenate([head] * 4 + [rest] * 4, 0)
    turn = (((1,), (1,)), ((), ()))
    bias_term = jnp.sum(delta, axis=1, keepdims=True)
    quarter = lax.div(lax.broadcasted_iota(jnp.int32, (PAIR, 128), 1), 32)
    blank = jnp.zeros((16, 128), F32)

    def with_bias(tile, low_total, high_total):
        lane_of = lax.broadcasted_iota(jnp.int32, tile.shape, 1)
        bias_sum = jnp.where(lane_of < 64, low_total, high_total)
        first = bias_sum.astype(BF16).astype(F32)
        tile = jnp.where(lax.rem(lane_of, 64) == 48, first, tile)
        return jnp.where(lax.rem(lane_of, 64) == 49, bias_sum - first, tile)

    r_ra = slot(1, 4)
    for turn_of in range(1, 5):
        row = mod4(x + turn_of)
        spans = [
            pl.ds(pl.multiple_of((col * 4 + row) * PAIR, 16), PAIR) for col in range(4)
        ]
        left = jnp.concatenate(
            [xg[span, TILE:TILE + 1024] for span in spans] + [nb[span, :] for span in spans], 0
        )
        grad = lax.dot_general(left, both, turn, preferred_element_type=F32)
        grad = grad[:, 0:128] + grad[:, 128:256]

        def packed(first):
            parts = [grad[first + col * PAIR:first + (col + 1) * PAIR] for col in range(4)]
            low = jnp.where(quarter == 0, parts[0], parts[1])
            high = jnp.where(quarter == 2, parts[2], parts[3])
            return jnp.where(quarter < 2, low, high)

        own_term, nb_term = packed(0), packed(COLUMN)
        turned = jnp.concatenate(
            [own_term[0:COLS], nb_term[0:COLS], blank, own_term[COLS:PAIR], nb_term[COLS:PAIR], blank], 0
        ).T
        for col in range(4):
            tile = with_bias(turned[col * 32:(col + 1) * 32], bias_term, bias_term)
            rsend[row, col] = tile.astype(BF16)
        if turn_of < 4:
            copy(rsend.at[row], ra.at[turn_of], device(g - x + row, p, c), r_ra + turn_of)

    before_x = len(sent) - 3
    drain(0, before_x)

    @pl.when(g < 15)
    def _():
        halo_up.wait_send()

    @pl.when(g > 0)
    def _():
        halo_down.wait_send()

    @pl.when(x != 0)
    def _():
        w_zero.wait_send()

    for turn_of in range(1, 4):
        await_bytes(ra.at[turn_of], r_ra + turn_of)

    r_rb = slot(1)
    to_group = zh * 4 + mod4(y + x)
    halves = lax.broadcasted_iota(jnp.int32, (16, 128), 1) < 64
    for step in (2, 1, 3, 0):
        col = mod4(zh + step)
        summed = (rsend[x, col].astype(F32) + ra[1, col].astype(F32)) + (
            ra[2, col].astype(F32) + ra[3, col].astype(F32)
        )
        bias_sum = summed[:, 48:49] + summed[:, 49:50]
        summed = with_bias(summed, bias_sum, bias_sum)
        top, bottom = summed[0:16], summed[16:32]
        rbs[col, 0] = jnp.where(halves, top, pltpu.roll(bottom, 64, 1)).astype(BF16)
        rbs[col, 1] = jnp.where(halves, pltpu.roll(top, 64, 1), bottom).astype(BF16)
        if step:
            for core in range(2):
                copy(rbs.at[col, core], rb.at[zl, c], device(to_group, x * 4 + col, core), r_rb)

    copy(rbs.at[zh, other], rb.at[zl, c], device(to_group, x * 4 + zh, other), r_rb)
    r_zero = remote(rbs.at[zh, c], rb.at[zl, c], device(to_group, x * 4 + zh, c), slot(0), r_rb)
    start_unless(stays, r_zero)

    @pl.when(stays)
    def _():
        pltpu.make_async_copy(rbs.at[zh, c], rb.at[zl, c], recv_sem.at[r_rb]).start()

    drain(before_x, None)
    await_bytes(rb, r_rb)
    for core in range(2):
        total = (rb[0, core].astype(F32) + rb[1, core].astype(F32)) + (
            rb[2, core].astype(F32) + rb[3, core].astype(F32)
        )
        fg[r_chip, core] = with_bias(
            total, total[:, 48:49] + total[:, 49:50], total[:, 112:113] + total[:, 113:114]
        ).astype(BF16)

    r_r2, s_r2 = slot(1, 4), slot(0)
    for step in range(1, 16):
        far = lax.rem(g + step, 16)
        remote(
            fg.at[r_chip], fg.at[r_chip], device(far, p, c), s_r2, r_r2 + mod4(x - lax.rem(far, 4))
        ).start()

    @pl.when(jnp.logical_not(stays))
    def _():
        r_zero.wait_send()

    for k in (0, 1, 3, 2):
        if k == 2:
            pltpu.make_async_copy(fg.at[0:15], fg.at[0:15], send_sem.at[s_r2]).wait()
        await_bytes(fg.at[0:(4 if k else 3)], r_r2 + k)
        for half in range(2):
            part = lax.rem(x - y + k + 4, 4) * 2 + half
            rows = []
            for chip in range(2):
                for core in range(2):
                    tile = fg[2 * part + chip, core].astype(F32)
                    rows += [tile, pltpu.roll(tile, 64, 1)]
            turned = jnp.concatenate(rows, 0).T
            span = pl.ds(pl.multiple_of(part * 128, 128), 128)
            gs_o[:, span] = turned[0:24]
            gn_o[:, span] = turned[24:48]
            gb_o[:, span] = turned[48:49] + turned[49:50]

    assert used[0] <= SENDS and used[1] <= RECVS, used


OUTS = (
    jax.ShapeDtypeStruct((32, 1024), BF16),
    jax.ShapeDtypeStruct((COLS, 1024), F32),
    jax.ShapeDtypeStruct((COLS, 1024), F32),
    jax.ShapeDtypeStruct((1, 1024), F32),
)


def place(hid, gs, gn, gb, hid_o, gs_o, gn_o, gb_o, sem):
    pairs = [(hid, hid_o), (gs, gs_o), (gn, gn_o), (gb, gb_o)]
    moves = [pltpu.make_async_copy(src, dst, sem.at[i]) for i, (src, dst) in enumerate(pairs)]
    for move in moves:
        move.start()
    for move in moves:
        move.wait()


def shards(features, adjacency, offsets, live, w_self, w_neigh, bias, targets):
    vmem = pl.BlockSpec(memory_space=pltpu.VMEM)
    hbm = pl.BlockSpec(memory_space=pltpu.HBM)
    inputs = [features.T, adjacency, offsets, live, w_self, w_neigh, bias.reshape(1, 1024), targets]
    results = pl.pallas_call(
        kernel,
        out_shape=OUTS,
        in_specs=[hbm] * 8,
        out_specs=(vmem,) * 4,
        scratch_shapes=[
            pltpu.VMEM((COLS, 1024), BF16),
            pltpu.VMEM((8, TILE, 256), BF16),
            pltpu.SMEM((8,), jnp.int32),
            pltpu.SMEM((8,), jnp.int32),
            pltpu.VMEM((COLS, 1024), BF16),
            pltpu.VMEM((COLS, 1024), BF16),
            pltpu.VMEM((1, 1024), F32),
            pltpu.VMEM((32, 1024), BF16),
            pltpu.VMEM((COLS, 1024), F32),
            pltpu.VMEM((PAIR, HALF), F32),
            pltpu.VMEM((768, 1280), BF16),
            pltpu.VMEM((768, 1024), BF16),
            pltpu.VMEM((8, TILE, 384), BF16),
            pltpu.VMEM((16, 32, 128), BF16),
            pltpu.VMEM((2, 16, 32, 128), BF16),
            pltpu.VMEM((4, 128, COLUMN), BF16),
            pltpu.VMEM((32, 1024), F32),
            pltpu.VMEM((4, 4, 32, 128), BF16),
            pltpu.VMEM((4, 4, 32, 128), BF16),
            pltpu.VMEM((4, 2, 16, 128), BF16),
            pltpu.VMEM((4, 2, 16, 128), BF16),
            pltpu.VMEM((16, 2, 16, 128), BF16),
            pltpu.SemaphoreType.DMA((8,)),
            pltpu.SemaphoreType.DMA((SENDS,)),
            pltpu.SemaphoreType.DMA((RECVS,)),
        ],
        compiler_params=pltpu.CompilerParams(
            collective_id=0, has_side_effects=True, vmem_limit_bytes=48 * 1024 * 1024
        ),
        cost_estimate=pl.CostEstimate(flops=10**9, bytes_accessed=10**7, transcendentals=32768),
    )(*[pltpu.with_memory_space_constraint(array, pltpu.HBM) for array in inputs])
    hidden, grad_self, grad_neigh, grad_bias = pl.pallas_call(
        place,
        out_shape=OUTS,
        in_specs=[vmem] * 4,
        out_specs=(pl.BlockSpec(memory_space=pl.ANY),) * 4,
        scratch_shapes=[pltpu.SemaphoreType.DMA((4,))],
        compiler_params=pltpu.CompilerParams(vmem_limit_bytes=1024 * 1024),
    )(*[pltpu.with_memory_space_constraint(array, pltpu.VMEM) for array in results])
    return hidden, grad_self, grad_neigh, grad_bias.reshape(1024)


def solution(mesh):
    in_specs = (
        P("grp", "feat"),
        P("grp", None, None),
        P("grp"),
        P("grp"),
        P("feat", None),
        P("feat", None),
        P(),
        P("feat", "grp"),
    )
    out_specs = (P("feat", "grp"), P("feat", None), P("feat", None), P())
    return jax.shard_map(shards, mesh=mesh, in_specs=in_specs, out_specs=out_specs, check_vma=False)
```
